32 devices in a mesh: dev: 32 (over z, y, x, core).
Axes of the slice: x: 2, y: 2, z: 4, core: 2. Of those that a mesh axis runs over, the one named last changes fastest.
Arguments:
- tokens: bfloat16 [6144, 1792], P('dev'), may hold values from -6 to 6
- segments: int32 [6144], replicated, may hold values from 0 to 192, as said below
- cotangent: bfloat16 [6144, 1792], P('dev'), may hold values from -6 to 6
- mixer_gain: bfloat16 [1792], P('dev'), may hold values from 0.5 to 1.5
- qkv_weight: bfloat16 [1792, 5376], P('dev'), may hold values from -0.125 to 0.125
- conv_taps: bfloat16 [3, 5376], P(None, 'dev'), may hold values from -4 to 4
- out_weight: bfloat16 [1792, 1792], P('dev'), may hold values from -0.5 to 0.5
- dense_gain: bfloat16 [1792], P('dev'), may hold values from 0.5 to 1.5
- gateup_weight: bfloat16 [1792, 9728], P('dev'), may hold values from -0.125 to 0.125
- down_weight: bfloat16 [4864, 1792], P('dev'), may hold values from -0.078125 to 0.078125
Outputs:
- layer_out: bfloat16 [6144, 1792], P('dev')
- input_grad: float32 [6144, 1792], P('dev')
- mixer_gain_grad: float32 [1792], P('dev')
- qkv_grad: float32 [1792, 5376], P('dev')
- taps_grad: float32 [3, 5376], P(None, 'dev')
- out_grad: float32 [1792, 1792], P('dev')
- dense_gain_grad: float32 [1792], P('dev')
- gateup_grad: float32 [1792, 9728], P('dev')
- down_grad: float32 [4864, 1792], P('dev')
The draws below stay inside these ranges and needn't reach their ends.
Inputs may be any that keep to these rules, and one draw needn't show every extreme that they name: `segments`: document numbers start at 0 on the first token, never fall, and rise by at most one from a token to the next; the number never changes between the last token of one block of 192 tokens and the first token of the next; each such block holds exactly 6 rises.
All inputs are finite; a program needn't handle non-finite values.
Results may differ from the reference program's by a relative error of at most 0.015.
Values may be sent and summed in bfloat16 or wider, within the bound.
No kernel may reach another device: no remote copies, remote signals or barrier semaphores. Data moves between devices by JAX's collectives and lax.ppermute only.
A program may use at most 512 MiB of HBM per device.

```python
import jax
import jax.numpy as jnp
from jax import lax

D = 1792
FF = 4864
HDIM = 64
WINDOW = 64
TOKENS_PER_PART = 192
TOKENS = 6144


def draw_segments(key, part):
    key = jax.random.fold_in(key, 7)
    rate_key, roll_key = jax.random.split(key)
    block_count = TOKENS // TOKENS_PER_PART
    rises = TOKENS_PER_PART // 32
    occupied_flag = jax.random.randint(rate_key, (TOKENS // 16,), 0, 4)
    rotations = jax.random.randint(roll_key, (TOKENS,), 0, 4096)
    extra_score = jnp.repeat(jnp.where(occupied_flag == 0, 4096, 0), 16)
    places = jnp.arange(TOKENS, dtype=jnp.int32)
    inside_window = places % TOKENS_PER_PART
    logit_scores = (rotations + extra_score) * TOKENS_PER_PART + inside_window
    logit_scores = jnp.where(inside_window == 0, -1, logit_scores).reshape(block_count, TOKENS_PER_PART)
    unused, chosen = jax.lax.top_k(logit_scores, rises)
    columns = jnp.arange(TOKENS_PER_PART, dtype=jnp.int32)
    starts = jnp.sum((columns[None, :, None] == chosen[:, None, :]).astype(jnp.int32), axis=2)
    return jnp.cumsum(starts.reshape(TOKENS)).astype(jnp.int32)


def steps_of(rng, dims, shards, least, high):
    gain = 1.0
    for dim, blocks in shards:
        heights = jax.random.uniform(jax.random.fold_in(jax.random.fold_in(rng, 6), dim), (blocks,), jnp.float32, least / len(shards), high / len(shards))
        gain = gain * jnp.repeat(jnp.exp(heights), dims[dim] // blocks).reshape((-1,) + (1,) * (len(dims) - 1 - dim))
    return gain


def gaussian(key, extent, spread, reach, shards=(), held_as=jnp.bfloat16):
    gain = steps_of(key, extent, shards, -0.22, 0.18) if shards else 1.0
    entries = jax.random.normal(key, extent, jnp.float32) * spread * gain
    return jnp.minimum(jnp.maximum(entries, -reach), reach).astype(held_as)


def setup_inputs(seed: int = 0) -> dict:
    arg_keys = jax.random.split(jax.random.key(seed), 11)
    return {
        "tokens": gaussian(arg_keys[0], (TOKENS, D), 1.0, 6.0, ((0, 32),)),
        "segments": draw_segments(jax.random.fold_in(arg_keys[10], 71), 0),
        "cotangent": gaussian(arg_keys[2], (TOKENS, D), 1.0, 6.0, ((0, 32),)),
        "mixer_gain": jnp.clip(1.0 + 0.1 * jax.random.normal(arg_keys[3], (D,), jnp.float32), 0.5, 1.5).astype(jnp.bfloat16),
        "qkv_weight": gaussian(arg_keys[4], (D, 3 * D), D ** -0.5, 0.125, ((0, 32),)),
        "conv_taps": gaussian(arg_keys[5], (3, 3 * D), 1.2, 4.0, ((1, 32),)),
        "out_weight": gaussian(arg_keys[6], (D, D), (D // 16) ** -0.5, 0.5, ((0, 32),)),
        "dense_gain": jnp.clip(1.0 + 0.1 * jax.random.normal(arg_keys[7], (D,), jnp.float32), 0.5, 1.5).astype(jnp.bfloat16),
        "gateup_weight": gaussian(arg_keys[8], (D, 2 * FF), D ** -0.5, 0.125, ((0, 32),)),
        "down_weight": gaussian(arg_keys[9], (FF, D), FF ** -0.5, 0.078125, ((0, 32),)),
    }


eps_norm = 1e-05
masked_score = -1e+30
block_rows = 512

@jax.custom_vjp
def low(v):
    return lax.optimization_barrier(v.astype(jnp.bfloat16)).astype(jnp.float32)

@jax.custom_vjp
def low_back(v):
    return v

def low_keep(v):
    return (low(v), None)

def low_pass(kept, grad):
    return (grad,)

def back_keep(v):
    return (v, None)

def back_low(kept, grad):
    return (low(grad),)
low.defvjp(low_keep, low_pass)
low_back.defvjp(back_keep, back_low)

def exact_dot(left_side, right_side):
    return jnp.dot(left_side, right_side, precision=lax.Precision.HIGHEST, preferred_element_type=jnp.float32)

def rms_scale(values, gains):
    inverse = lax.rsqrt(lax.optimization_barrier(jnp.mean(values * values, axis=-1, keepdims=True)) + eps_norm)
    return values * inverse * gains

def conv_gate(projected, kernel, same_one, same_two):
    newest = projected[2:]
    summed = kernel[0] * newest + kernel[1] * (same_one * projected[1:-1]) + kernel[2] * (same_two * projected[:-2])
    return summed * jax.nn.sigmoid(newest)

def swiglu(joined):
    split_at = joined.shape[-1] // 2
    return jax.nn.silu(joined[:, :split_at]) * joined[:, split_at:]

def reference(tokens, segments, cotangent, mixer_gain, qkv_weight, conv_taps, out_weight, dense_gain, gateup_weight, down_weight):
    token_count = tokens.shape[0]
    hidden_width = tokens.shape[1]
    head_count = hidden_width // HDIM
    score_scale = 1.0 / HDIM ** 0.5
    padded_two = jnp.concatenate([jnp.full((2,), -1, jnp.int32), segments.astype(jnp.int32)])
    same_one = (padded_two[2:] == padded_two[1:-1]).astype(jnp.float32)[:, None]
    same_two = (padded_two[2:] == padded_two[:-2]).astype(jnp.float32)[:, None]
    padded_keys = jnp.concatenate([jnp.full((WINDOW - 1,), -1, jnp.int32), segments.astype(jnp.int32)])
    key_span = block_rows + WINDOW - 1
    offsets = jnp.arange(block_rows, dtype=jnp.int32)[:, None] + (WINDOW - 1) - jnp.arange(key_span, dtype=jnp.int32)[None, :]
    near = (offsets >= 0) & (offsets < WINDOW)

    def attention(queries, keyset, valueset):
        keys_padded = jnp.pad(keyset, ((WINDOW - 1, 0), (0, 0)))
        values_padded = jnp.pad(valueset, ((WINDOW - 1, 0), (0, 0)))

        def one_block(index):
            first = (index * block_rows).astype(jnp.int32)
            query_rows = lax.dynamic_slice_in_dim(queries, first, block_rows).reshape(block_rows, head_count, HDIM)
            key_rows = lax.dynamic_slice_in_dim(keys_padded, first, key_span).reshape(key_span, head_count, HDIM)
            value_rows = lax.dynamic_slice_in_dim(values_padded, first, key_span).reshape(key_span, head_count, HDIM)
            query_segments = lax.dynamic_slice_in_dim(segments.astype(jnp.int32), first, block_rows)
            key_segments = lax.dynamic_slice_in_dim(padded_keys, first, key_span)
            allowed = near & (query_segments[:, None] == key_segments[None, :])
            logit_scores = low_back(jnp.einsum('rhe,khe->hrk', query_rows, key_rows, precision=lax.Precision.HIGHEST) * score_scale)
            logit_scores = jnp.where(allowed[None], logit_scores, masked_score)
            largest = lax.optimization_barrier(jnp.max(logit_scores, axis=-1, keepdims=True))
            exponent = jnp.exp(logit_scores - largest)
            weights = low(exponent / lax.optimization_barrier(jnp.sum(exponent, axis=-1, keepdims=True)))
            attended = jnp.einsum('hrk,khe->rhe', weights, value_rows, precision=lax.Precision.HIGHEST)
            return attended.reshape(block_rows, hidden_width)
        blocks = lax.map(jax.checkpoint(one_block), jnp.arange(token_count // block_rows, dtype=jnp.int32))
        return blocks.reshape(token_count, hidden_width)

    def forward(inputs_f, gain_one, qkv_f, taps_f, out_f, gain_two, gateup_f, down_f):
        normed = low(rms_scale(inputs_f, gain_one))
        projected = low_back(exact_dot(normed, qkv_f))
        mixed = conv_gate(jnp.pad(projected, ((2, 0), (0, 0))), taps_f, same_one, same_two)
        queries = low(mixed[:, :hidden_width])
        keyset = low(mixed[:, hidden_width:2 * hidden_width])
        valueset = low(mixed[:, 2 * hidden_width:])
        attended = low(low_back(attention(queries, keyset, valueset)))
        residual = inputs_f + low_back(exact_dot(attended, out_f))
        normed_dense = low(rms_scale(residual, gain_two))
        joined = low_back(exact_dot(normed_dense, gateup_f))
        hidden = low(swiglu(joined))
        return residual + exact_dot(hidden, down_f)
    layer_out, backward = jax.vjp(forward, tokens.astype(jnp.float32), mixer_gain.astype(jnp.float32), qkv_weight.astype(jnp.float32), conv_taps.astype(jnp.float32), out_weight.astype(jnp.float32), dense_gain.astype(jnp.float32), gateup_weight.astype(jnp.float32), down_weight.astype(jnp.float32))
    grads = backward(cotangent.astype(jnp.float32))
    return (layer_out.astype(jnp.bfloat16), grads[0], grads[1], grads[2], grads[3], grads[4], grads[5], grads[6], grads[7])
```

```python
import math

import jax
import jax.numpy as jnp
from jax import lax
from jax.sharding import PartitionSpec as P

HDIM = 64
WINDOW = 64
EDGE = WINDOW + 1
PLANE = 8

eps_norm = 1e-05
masked_score = -1e30
bf16 = jnp.bfloat16
f32 = jnp.float32


def coords(device):
    return (device // 8, (device // 4) % 2, (device // 2) % 2, device % 2)


def flat(z, y, x, c):
    return ((z * 2 + y) * 2 + x) * 2 + c


def move(array, count, target):
    pairs = [(d, flat(*target(*coords(d)))) for d in range(count)]
    return lax.ppermute(array, "dev", pairs)


def rms_scale(values, gains):
    inverse = lax.rsqrt(jnp.mean(values * values, axis=-1, keepdims=True) + eps_norm)
    return values * inverse * gains


def conv_gate(projected, kernel, same_one, same_two):
    newest = projected[2:]
    summed = (
        kernel[0] * newest
        + kernel[1] * (same_one * projected[1:-1])
        + kernel[2] * (same_two * projected[:-2])
    )
    return summed * jax.nn.sigmoid(newest)


def swiglu(joined):
    split_at = joined.shape[-1] // 2
    return jax.nn.silu(joined[:, :split_at]) * joined[:, split_at:]


def contract_last(left_side, right_side):
    return lax.dot_general(
        left_side, right_side, (((1,), (1,)), ((), ())), preferred_element_type=f32
    )


def contract_first(left_side, right_side):
    return lax.dot_general(
        left_side, right_side, (((0,), (0,)), ((), ())), preferred_element_type=f32
    )


def xor_order(parts, hi, lo):
    stacked = jnp.stack(parts)
    mask = 2 * hi + lo
    return [lax.dynamic_index_in_dim(stacked, j ^ mask, 0, keepdims=False) for j in range(4)]


def heads_of(values):
    return values.reshape(values.shape[0], values.shape[1] // HDIM, HDIM)


def attend(queries, keyset, valueset, allowed, score_scale):
    scores = (
        jnp.einsum("rhe,khe->hrk", heads_of(queries), heads_of(keyset), preferred_element_type=f32)
        * score_scale
    )
    scores = jnp.where(allowed[None], scores, masked_score)
    largest = jnp.max(scores, axis=-1, keepdims=True)
    exponent = jnp.exp(scores - largest)
    probs = exponent / jnp.sum(exponent, axis=-1, keepdims=True)
    attended = jnp.einsum(
        "hrk,khe->rhe", probs.astype(bf16), heads_of(valueset), preferred_element_type=f32
    )
    return attended.reshape(queries.shape).astype(bf16), probs


def attend_back(queries, keyset, valueset, probs, grad_out, score_scale):
    grad_heads = heads_of(grad_out)
    grad_probs = jnp.einsum(
        "rhe,khe->hrk", grad_heads, heads_of(valueset), preferred_element_type=f32
    )
    inner = jnp.sum(probs * grad_probs, axis=-1, keepdims=True)
    grad_scores = (probs * (grad_probs - inner)).astype(bf16)
    grad_queries = (
        jnp.einsum("hrk,khe->rhe", grad_scores, heads_of(keyset), preferred_element_type=f32)
        * score_scale
    )
    grad_keys = (
        jnp.einsum("hrk,rhe->khe", grad_scores, heads_of(queries), preferred_element_type=f32)
        * score_scale
    )
    grad_values = jnp.einsum(
        "hrk,rhe->khe", probs.astype(bf16), grad_heads, preferred_element_type=f32
    )
    return (
        grad_queries.reshape(queries.shape),
        grad_keys.reshape(keyset.shape),
        grad_values.reshape(keyset.shape),
    )


def layer(
    count,
    tokens,
    segments,
    cotangent,
    mixer_gain,
    qkv_weight,
    conv_taps,
    out_weight,
    dense_gain,
    gateup_weight,
    down_weight,
):
    planes = count // PLANE
    rows, width = tokens.shape
    group_rows = 4 * rows
    quarter = width // 4
    hidden_width = down_weight.shape[0] * count
    hidden_part = hidden_width // 4
    shard_rows = qkv_weight.shape[0]
    down_rows = down_weight.shape[0]
    me = lax.axis_index("dev")
    z, y, x, c = coords(me)
    score_scale = 1.0 / math.sqrt(HDIM)

    def spread(parts):
        return [
            move(parts[2 * a + b], count, lambda z, y, x, c: (z, c ^ b, x ^ a, y))
            for a in range(2)
            for b in range(2)
        ]

    def collect(parts):
        return [
            move(parts[2 * a + b], count, lambda z, y, x, c: (z, c, x ^ a, y ^ b))
            for a in range(2)
            for b in range(2)
        ]

    def to_sibling(array):
        return move(array, count, lambda z, y, x, c: (z, y, x, c ^ 1))

    def ring_gather(piece):
        pieces = [piece]
        for unused in range(planes - 1):
            pieces.append(move(pieces[-1], count, lambda z, y, x, c: ((z - 1) % planes, y, x, c)))
        return pieces

    def absolute(pieces):
        stacked = jnp.stack(pieces + pieces)
        return lax.dynamic_slice_in_dim(stacked, planes - z, planes, 0)

    def both_cores(own, other):
        return jnp.where(c == 0, jnp.stack([own, other], 1), jnp.stack([other, own], 1))

    def ring_scatter(parts):
        carried = lax.dynamic_index_in_dim(parts, (z - 1) % planes, 0, keepdims=False)
        for step in range(1, planes):
            arrived = move(carried.astype(bf16), count, lambda z, y, x, c: ((z + 1) % planes, y, x, c))
            mine = lax.dynamic_index_in_dim(parts, (z - 1 - step) % planes, 0, keepdims=False)
            carried = arrived.astype(f32) + mine.astype(f32)
        return carried

    def to_columns(slices):
        by_xy = [slices[2 * (j % 2) + j // 2] for j in range(4)]
        return jnp.concatenate(xor_order(spread(xor_order(by_xy, x, c)), x, y), 0)

    def from_columns(array):
        pieces = jnp.split(array, 4, 0)
        arrived = xor_order(collect(xor_order(pieces, x, y)), x, c)
        return jnp.stack([arrived[2 * (j % 2) + j // 2] for j in range(4)])

    spot = me * shard_rows
    gains = lax.dynamic_update_slice(
        jnp.zeros((2, width), bf16), jnp.stack([mixer_gain, dense_gain]), (0, spot)
    )
    taps = lax.dynamic_update_slice(
        jnp.zeros((3, 3 * width), bf16), conv_taps, (0, me * conv_taps.shape[1])
    )

    def butterfly(array):
        bit = 1
        while bit < count:
            pairs = [(d, d ^ bit) for d in range(count)]
            array = array + lax.ppermute(array, "dev", pairs)
            bit *= 2
        return array

    small = butterfly(jnp.concatenate([gains.reshape(-1), taps.reshape(-1)]))
    gain_one = small[:width].astype(f32)
    gain_two = small[width : 2 * width].astype(f32)
    taps_full = small[2 * width :].reshape(3, 3, 4, quarter).astype(f32)
    part = 2 * y + x
    taps_mine = lax.dynamic_index_in_dim(taps_full, part, 2, keepdims=False).reshape(3, 3 * quarter)

    qkv_slices = qkv_weight.reshape(shard_rows, 3, 4, quarter).transpose(2, 0, 1, 3)
    qkv_piece = to_columns(qkv_slices.reshape(4, shard_rows, 3 * quarter))
    gateup_slices = gateup_weight.reshape(shard_rows, 2, planes, 4, hidden_part // planes)
    gateup_slices = gateup_slices.transpose(3, 0, 1, 2, 4).reshape(4, shard_rows, 2 * hidden_part)
    gateup_piece = to_columns(gateup_slices)

    def whole(piece):
        pieces = ring_gather(piece)
        others = [to_sibling(p) for p in pieces]
        both = both_cores(absolute(pieces), absolute(others))
        return both.reshape(-1, piece.shape[1])

    qkv_full = whole(qkv_piece)
    out_planes = absolute(ring_gather(out_weight)).reshape(4, -1, width)
    out_by_xy = [out_planes[2 * (j % 2) + j // 2] for j in range(4)]
    out_own = xor_order(spread(xor_order(out_by_xy, x, c)), x, y)
    out_own = jnp.stack(out_own).reshape(4, planes // 4, shard_rows, width).transpose(1, 0, 2, 3)
    out_own = out_own.reshape(planes // 4, 4 * shard_rows, width)
    out_full = both_cores(out_own, to_sibling(out_own)).reshape(quarter, width)
    gateup_full = whole(gateup_piece)
    down_full = whole(down_weight)

    padded_segments = jnp.concatenate([jnp.full((EDGE,), -1, jnp.int32), segments])
    window_segments = lax.dynamic_slice_in_dim(
        padded_segments, (2 * z + c) * group_rows, EDGE + group_rows
    )
    same_one = (window_segments[2:] == window_segments[1:-1]).astype(f32)[:, None]
    same_two = (window_segments[2:] == window_segments[:-2]).astype(f32)[:, None]
    key_count = rows + WINDOW - 1
    offsets = jnp.arange(rows)[:, None] + (WINDOW - 1) - jnp.arange(key_count)[None, :]
    near = (offsets >= 0) & (offsets < WINDOW)

    def allowed_in(block):
        first = block * rows
        own = window_segments[EDGE + first : EDGE + first + rows]
        seen = window_segments[2 + first : 2 + first + key_count]
        return near & (own[:, None] == seen[None, :])

    own_tokens = tokens.astype(f32)
    normed = rms_scale(own_tokens, gain_one).astype(bf16)
    edge_rows = sum(
        lax.ppermute(
            normed[rows - EDGE :],
            "dev",
            [(4 * g - 1, 8 * (g // 2) + 2 * p + g % 2) for g in range(1, count // 4)],
        )
        for p in range(4)
    )
    normed_group = jnp.concatenate([edge_rows] + xor_order(spread([normed] * 4), x, y))
    projected = jnp.dot(normed_group, qkv_full, preferred_element_type=f32)
    mixed = conv_gate(projected, taps_mine, same_one, same_two).astype(bf16)
    queries = mixed[WINDOW - 1 :, :quarter]
    keyset = mixed[:, quarter : 2 * quarter]
    valueset = mixed[:, 2 * quarter :]
    attended = []
    probs = []
    for block in range(4):
        first = block * rows
        attended_block, probs_block = attend(
            queries[first : first + rows],
            keyset[first : first + key_count],
            valueset[first : first + key_count],
            allowed_in(block),
            score_scale,
        )
        attended.append(attended_block)
        probs.append(probs_block)
    attended = jnp.concatenate(attended)

    def scatter_rows(array):
        pieces = jnp.split(array.astype(bf16), 4, 0)
        arrived = collect(pieces)
        return sum(a.astype(f32) for a in arrived)

    def gather_rows(array):
        return jnp.concatenate(spread([array] * 4))

    def natural(array):
        return jnp.concatenate(xor_order(jnp.split(array, 4, 0), x, y))

    cotangent_group = gather_rows(cotangent)
    mixer_out = jnp.dot(attended, out_full, preferred_element_type=f32).astype(bf16)
    residual = own_tokens + scatter_rows(natural(mixer_out))
    normed_dense = rms_scale(residual, gain_two).astype(bf16)
    dense_group = gather_rows(normed_dense)
    joined = jnp.dot(dense_group, gateup_full, preferred_element_type=f32)
    hidden = swiglu(joined).astype(bf16)
    dense_out = jnp.dot(hidden, down_full, preferred_element_type=f32)
    layer_out = (residual + scatter_rows(dense_out)).astype(bf16)

    down_grad = contract_first(hidden, cotangent_group).astype(bf16)
    grad_hidden = contract_last(cotangent_group, down_full)
    unused, swiglu_back = jax.vjp(swiglu, joined)
    grad_joined = swiglu_back(grad_hidden)[0].astype(bf16)
    gateup_grad = contract_first(dense_group, grad_joined).astype(bf16)
    grad_dense = scatter_rows(contract_last(grad_joined, gateup_full))
    unused, dense_back = jax.vjp(rms_scale, residual, gain_two)
    grad_residual, dense_gain_sum = dense_back(grad_dense)
    grad_residual = grad_residual + cotangent.astype(f32)
    grad_branch = natural(gather_rows(grad_residual.astype(bf16)))
    out_grad = contract_first(attended, grad_branch).astype(bf16)
    grad_attended = contract_last(grad_branch, out_full).astype(bf16)
    grad_queries = []
    grad_kv = jnp.zeros((group_rows + WINDOW - 1, 2 * quarter), f32)
    for block in range(4):
        first = block * rows
        gq, gk, gv = attend_back(
            queries[first : first + rows],
            keyset[first : first + key_count],
            valueset[first : first + key_count],
            probs[block],
            grad_attended[first : first + rows],
            score_scale,
        )
        grad_queries.append(gq)
        grad_kv = grad_kv + jnp.pad(
            jnp.concatenate([gk, gv], 1), ((first, group_rows - rows - first), (0, 0))
        )
    grad_queries = jnp.pad(jnp.concatenate(grad_queries), ((WINDOW - 1, 0), (0, 0)))
    grad_mixed = jnp.concatenate([grad_queries, grad_kv], axis=1)

    def gated(projected, kernel):
        return conv_gate(projected, kernel, same_one, same_two)

    unused, conv_back = jax.vjp(gated, projected, taps_mine)
    grad_widened, grad_taps = conv_back(grad_mixed)
    arriving = lax.ppermute(
        grad_widened[:EDGE].astype(bf16),
        "dev",
        [
            (d, flat(*((coords(d)[0],) + coords(d)[1:3] + (0,))))
            if d % 2
            else (d, flat(coords(d)[0] - 1, coords(d)[1], coords(d)[2], 1))
            for d in range(count)
            if d % 2 or d >= 8
        ],
    )
    grad_projected = grad_widened[EDGE:] + jnp.pad(
        arriving.astype(f32), ((group_rows - EDGE, 0), (0, 0))
    )
    grad_projected = grad_projected.astype(bf16)
    qkv_grad = contract_first(normed_group[EDGE:], grad_projected).astype(bf16)
    grad_normed = contract_last(grad_projected, qkv_full).astype(bf16)
    grad_normed = scatter_rows(natural(grad_normed))
    unused, mixer_back = jax.vjp(rms_scale, own_tokens, gain_one)
    grad_rows, mixer_gain_sum = mixer_back(grad_normed)
    input_grad = grad_residual + grad_rows

    def core_sum(array):
        own = lax.dynamic_index_in_dim(array, c, 1, keepdims=False)
        other = lax.dynamic_index_in_dim(array, 1 - c, 1, keepdims=False)
        return (own.astype(f32) + to_sibling(other).astype(f32)).astype(bf16)

    down_mine = ring_scatter(core_sum(down_grad.reshape(planes, 2, down_rows, width)))
    gateup_part = ring_scatter(
        core_sum(gateup_grad.reshape(planes, 2, 4 * shard_rows, 2 * hidden_part))
    ).astype(bf16)
    gateup_mine = from_columns(gateup_part).reshape(4, shard_rows, 2, planes, hidden_part // planes)
    gateup_mine = gateup_mine.transpose(1, 2, 3, 0, 4).reshape(shard_rows, 2 * hidden_width)
    out_part = core_sum(out_grad.reshape(planes // 4, 2, 4 * shard_rows, width))
    out_part = out_part.reshape(planes // 4, 4, shard_rows, width).transpose(1, 0, 2, 3)
    out_part = from_columns(out_part.reshape(-1, width))
    out_mine = ring_scatter(out_part.reshape(planes, shard_rows, width))
    qkv_part = ring_scatter(
        core_sum(qkv_grad.reshape(planes, 2, 4 * shard_rows, 3 * quarter))
    ).astype(bf16)
    qkv_mine = from_columns(qkv_part).reshape(4, shard_rows, 3, quarter)
    qkv_mine = qkv_mine.transpose(1, 2, 0, 3).reshape(shard_rows, 3 * width)

    grad_taps = lax.dynamic_update_slice(
        jnp.zeros((3, 3, 4, quarter), f32), grad_taps.reshape(3, 3, 1, quarter), (0, 0, part, 0)
    )
    sums = butterfly(jnp.concatenate([mixer_gain_sum, dense_gain_sum, grad_taps.reshape(-1)]))
    mixer_mine = lax.dynamic_slice_in_dim(sums, spot, shard_rows)
    dense_mine = lax.dynamic_slice_in_dim(sums, width + spot, shard_rows)
    taps_mine = lax.dynamic_slice_in_dim(
        sums[2 * width :].reshape(3, 3 * width), me * conv_taps.shape[1], conv_taps.shape[1], 1
    )
    return (
        layer_out,
        input_grad,
        mixer_mine,
        qkv_mine.astype(f32),
        taps_mine,
        out_mine,
        dense_mine,
        gateup_mine.astype(f32),
        down_mine,
    )


def solution(mesh):
    count = mesh.devices.size

    def local(*arguments):
        return layer(count, *arguments)

    placed = (
        P("dev", None),
        P(),
        P("dev", None),
        P("dev"),
        P("dev", None),
        P(None, "dev"),
        P("dev", None),
        P("dev"),
        P("dev", None),
        P("dev", None),
    )
    return jax.shard_map(
        local,
        mesh=mesh,
        in_specs=placed,
        out_specs=(
            P("dev", None),
            P("dev", None),
            P("dev"),
            P("dev", None),
            P(None, "dev"),
            P("dev", None),
            P("dev"),
            P("dev", None),
            P("dev", None),
        ),
        check_vma=False,
    )
```

```python
import functools
import math

import jax
import jax.numpy as jnp
from jax import lax
from jax.experimental import pallas as pl
from jax.experimental.pallas import tpu as pltpu
from jax.sharding import Mesh, PartitionSpec as P

HDIM = 64
WINDOW = 64
HALO = 80
LANES = 128
PLANE = 8

eps_norm = 1e-05
masked_score = -1e30
bf16 = jnp.bfloat16
f32 = jnp.float32
ALL = ("z", "y", "x", "core")
SQUARE = ("y", "x")
OCTET = ("y", "x", "core")


def rms_scale(values, gains):
    inverse = lax.rsqrt(jnp.mean(values * values, axis=-1, keepdims=True) + eps_norm)
    return values * inverse * gains


def swiglu(joined):
    gate, up = joined
    return jax.nn.silu(gate) * up


def contract_last(left_side, right_side):
    return lax.dot_general(
        left_side, right_side, (((1,), (1,)), ((), ())), preferred_element_type=f32
    )


def contract_first(left_side, right_side):
    return lax.dot_general(
        left_side, right_side, (((0,), (0,)), ((), ())), preferred_element_type=f32
    )


def plain(left_side, right_side):
    return jnp.dot(left_side, right_side, preferred_element_type=f32)


def shifted_down(values, by):
    return pltpu.roll(values, by, 0)


def shifted_up(values, by):
    return pltpu.roll(values, values.shape[0] - by, 0)


def gate_of(values, taps, same_one, same_two):
    conv = (
        taps[0:1] * values
        + taps[1:2] * (same_one * shifted_down(values, 1))
        + taps[2:3] * (same_two * shifted_down(values, 2))
    )
    return conv, jax.nn.sigmoid(values)


def by_head(values):
    lane = lax.broadcasted_iota(jnp.int32, values.shape, 1)
    zero = jnp.zeros_like(values)
    return jnp.concatenate(
        [jnp.where(lane < HDIM, values, zero), jnp.where(lane < HDIM, zero, values)], 0
    )


def join_heads(values):
    half = values.shape[0] // 2
    lane = lax.broadcasted_iota(jnp.int32, (half, values.shape[1]), 1)
    return jnp.where(lane < HDIM, values[:half], values[half:])


def block_masks(seg_ref, keys_ref, subs):
    span = 2 * WINDOW
    row = lax.broadcasted_iota(jnp.int32, (WINDOW, span), 0)
    col = lax.broadcasted_iota(jnp.int32, (WINDOW, span), 1)
    near = (col > row) & (col <= row + WINDOW)
    masks = []
    for sub in range(subs):
        first = HALO + sub * WINDOW
        same = seg_ref[0, first : first + WINDOW] == keys_ref[0, sub : sub + 1]
        mask = near & same
        masks.append(jnp.concatenate([mask, mask], 0))
    return masks


def same_rows(seg_ref):
    seg = seg_ref[0]
    same_one = (seg == shifted_down(seg, 1)).astype(f32)
    same_two = (seg == shifted_down(seg, 2)).astype(f32)
    return same_one, same_two


def sub_probs(queries, keyset, mask, score_scale):
    scores = contract_last(queries, keyset) * score_scale
    scores = jnp.where(mask, scores, masked_score)
    exponent = jnp.exp(scores - jnp.max(scores, axis=-1, keepdims=True))
    return exponent / jnp.sum(exponent, axis=-1, keepdims=True)


def attend_kernel(proj_ref, taps_ref, seg_ref, keys_ref, out_ref, *, pairs, subs, score_scale):
    same_one, same_two = same_rows(seg_ref)
    masks = block_masks(seg_ref, keys_ref, subs)
    first_key = HALO - WINDOW
    for pair in range(pairs):
        mixed = []
        for kind in range(3):
            at = (kind * pairs + pair) * LANES
            conv, sig = gate_of(
                proj_ref[0, :, at : at + LANES], taps_ref[:, at : at + LANES], same_one, same_two
            )
            mixed.append((conv * sig).astype(bf16))
        for sub in range(subs):
            first = HALO + sub * WINDOW
            seen = first_key + sub * WINDOW
            queries = by_head(mixed[0][first : first + WINDOW])
            probs = sub_probs(
                queries, mixed[1][seen : seen + 2 * WINDOW], masks[sub], score_scale
            )
            attended = plain(probs.astype(bf16), mixed[2][seen : seen + 2 * WINDOW])
            out_ref[0, sub * WINDOW : (sub + 1) * WINDOW, pair * LANES : (pair + 1) * LANES] = (
                join_heads(attended).astype(bf16)
            )


def attend_back_kernel(
    proj_ref, grad_ref, taps_ref, seg_ref, keys_ref, out_ref, tap_ref, *, pairs, subs, score_scale
):
    @pl.when(pl.program_id(0) == 0)
    def clear():
        tap_ref[...] = jnp.zeros_like(tap_ref)

    same_one, same_two = same_rows(seg_ref)
    masks = block_masks(seg_ref, keys_ref, subs)
    first_key = HALO - WINDOW
    for pair in range(pairs):
        values, convs, sigs, mixed = [], [], [], []
        for kind in range(3):
            at = (kind * pairs + pair) * LANES
            value = proj_ref[0, :, at : at + LANES]
            conv, sig = gate_of(value, taps_ref[:, at : at + LANES], same_one, same_two)
            values.append(value)
            convs.append(conv)
            sigs.append(sig)
            mixed.append((conv * sig).astype(bf16))
        grad_queries, grad_keys, grad_values = [], [], []
        for sub in range(subs):
            first = HALO + sub * WINDOW
            seen = first_key + sub * WINDOW
            queries = by_head(mixed[0][first : first + WINDOW])
            keyset = mixed[1][seen : seen + 2 * WINDOW]
            probs = sub_probs(queries, keyset, masks[sub], score_scale)
            grads = by_head(
                grad_ref[0, sub * WINDOW : (sub + 1) * WINDOW, pair * LANES : (pair + 1) * LANES]
            )
            grad_probs = contract_last(grads, mixed[2][seen : seen + 2 * WINDOW])
            inner = jnp.sum(probs * grad_probs, axis=-1, keepdims=True)
            grad_scores = (probs * (grad_probs - inner)).astype(bf16)
            grad_queries.append(join_heads(plain(grad_scores, keyset)) * score_scale)
            grad_keys.append(contract_first(grad_scores, queries) * score_scale)
            grad_values.append(contract_first(probs.astype(bf16), grads))

        def overlapped(parts):
            rows = [jnp.zeros((first_key, LANES), f32), parts[0][:WINDOW]]
            for sub in range(1, subs):
                rows.append(parts[sub - 1][WINDOW:] + parts[sub][:WINDOW])
            rows.append(parts[subs - 1][WINDOW:])
            return jnp.concatenate(rows, 0)

        grads = (
            jnp.concatenate([jnp.zeros((HALO, LANES), f32)] + grad_queries, 0),
            overlapped(grad_keys),
            overlapped(grad_values),
        )
        for kind in range(3):
            at = (kind * pairs + pair) * LANES
            taps = taps_ref[:, at : at + LANES]
            through = grads[kind] * sigs[kind]
            one = same_one * through
            two = same_two * through
            summed = (
                through * convs[kind] * (1.0 - sigs[kind])
                + taps[0:1] * through
                + taps[1:2] * shifted_up(one, 1)
                + taps[2:3] * shifted_up(two, 2)
            )
            out_ref[0, :, at : at + LANES] = summed.astype(bf16)
            value = values[kind]
            tap_ref[0:1, at : at + LANES] += jnp.sum(through * value, 0, keepdims=True)
            tap_ref[1:2, at : at + LANES] += jnp.sum(
                one * shifted_down(value, 1), 0, keepdims=True
            )
            tap_ref[2:3, at : at + LANES] += jnp.sum(
                two * shifted_down(value, 2), 0, keepdims=True
            )


def attention_specs(blocks, rows, columns, subs):
    return [
        pl.BlockSpec((3, columns), lambda b: (0, 0)),
        pl.BlockSpec((1, rows, LANES), lambda b: (b, 0, 0)),
        pl.BlockSpec((1, subs, 2 * WINDOW), lambda b: (b, 0, 0)),
    ]


def attend(projected, taps, seg_rows, seg_keys, score_scale):
    blocks, rows, columns = projected.shape
    subs = seg_keys.shape[1]
    heads_wide = columns // 3
    return pl.pallas_call(
        functools.partial(
            attend_kernel, pairs=heads_wide // LANES, subs=subs, score_scale=score_scale
        ),
        grid=(blocks,),
        out_shape=jax.ShapeDtypeStruct((blocks, rows - HALO, heads_wide), bf16),
        in_specs=[pl.BlockSpec((1, rows, columns), lambda b: (b, 0, 0))]
        + attention_specs(blocks, rows, columns, subs),
        out_specs=pl.BlockSpec((1, rows - HALO, heads_wide), lambda b: (b, 0, 0)),
        compiler_params=pltpu.CompilerParams(vmem_limit_bytes=40 * 1024 * 1024),
        name="attend",
    )(projected, taps, seg_rows, seg_keys)


def attend_back(projected, grad_attended, taps, seg_rows, seg_keys, score_scale):
    blocks, rows, columns = projected.shape
    subs = seg_keys.shape[1]
    heads_wide = columns // 3
    return pl.pallas_call(
        functools.partial(
            attend_back_kernel, pairs=heads_wide // LANES, subs=subs, score_scale=score_scale
        ),
        grid=(blocks,),
        out_shape=(
            jax.ShapeDtypeStruct((blocks, rows, columns), bf16),
            jax.ShapeDtypeStruct((8, columns), f32),
        ),
        in_specs=[
            pl.BlockSpec((1, rows, columns), lambda b: (b, 0, 0)),
            pl.BlockSpec((1, rows - HALO, heads_wide), lambda b: (b, 0, 0)),
        ]
        + attention_specs(blocks, rows, columns, subs),
        out_specs=(
            pl.BlockSpec((1, rows, columns), lambda b: (b, 0, 0)),
            pl.BlockSpec((8, columns), lambda b: (0, 0)),
        ),
        compiler_params=pltpu.CompilerParams(vmem_limit_bytes=40 * 1024 * 1024),
        name="attend_back",
    )(projected, grad_attended, taps, seg_rows, seg_keys)


def layer(
    planes,
    tokens,
    segments,
    cotangent,
    mixer_gain,
    qkv_weight,
    conv_taps,
    out_weight,
    dense_gain,
    gateup_weight,
    down_weight,
):
    count = planes * PLANE
    rows, width = tokens.shape
    ext = HALO + rows
    subs = rows // WINDOW
    quarter = width // 4
    padded = -(-quarter // LANES) * LANES
    half_wide = 3 * padded // 2
    half_width = width // 2
    hidden_width = down_weight.shape[0] * count
    hidden_part = hidden_width // 4
    shard_rows = qkv_weight.shape[0]
    down_rows = down_weight.shape[0]
    tap_columns = conv_taps.shape[1]
    out_planes = planes // 4
    z = lax.axis_index("z")
    y = lax.axis_index("y")
    x = lax.axis_index("x")
    c = lax.axis_index("core")
    part = 2 * y + x
    score_scale = 1.0 / math.sqrt(HDIM)

    def swap(array, axes):
        return lax.all_to_all(array, axes, 0, 0)

    def to_sibling(array):
        return lax.ppermute(array, "core", [(0, 1), (1, 0)])

    def ring_gather(piece):
        pieces = [piece]
        for unused in range(planes - 1):
            pieces.append(
                lax.ppermute(pieces[-1], "z", [(i, (i - 1) % planes) for i in range(planes)])
            )
        return pieces

    def absolute(pieces):
        stacked = jnp.concatenate([p[None] for p in pieces + pieces], 0)
        return lax.dynamic_slice_in_dim(stacked, planes - z, planes, 0)

    def whole(piece):
        pieces = ring_gather(piece)
        others = [to_sibling(p) for p in pieces]
        return (
            absolute(pieces).reshape(-1, piece.shape[1]),
            absolute(others).reshape(-1, piece.shape[1]),
        )

    def in_order(own, other):
        return jnp.where(c == 0, own, other), jnp.where(c == 0, other, own)

    owned = jnp.concatenate([mixer_gain, dense_gain, conv_taps.reshape(-1)])
    small = swap(jnp.broadcast_to(owned, (PLANE, owned.shape[0])), OCTET)
    small = swap(jnp.broadcast_to(small, (planes,) + small.shape), "z").astype(f32)
    gain_one = small[:, :, :shard_rows].reshape(width)
    gain_two = small[:, :, shard_rows : 2 * shard_rows].reshape(width)
    taps = small[:, :, 2 * shard_rows :].reshape(count, 3, tap_columns).transpose(1, 0, 2)
    taps = lax.dynamic_index_in_dim(taps.reshape(3, 3, 4, quarter), part, 2, keepdims=False)
    taps = jnp.pad(taps, ((0, 0), (0, 0), (0, padded - quarter))).reshape(3, 3 * padded)

    qkv_slices = qkv_weight.reshape(shard_rows, 3, 4, quarter)
    qkv_slices = jnp.pad(qkv_slices, ((0, 0), (0, 0), (0, 0), (0, padded - quarter)))
    qkv_slices = qkv_slices.transpose(2, 0, 1, 3).reshape(4, shard_rows, 2, half_wide)
    qkv_slices = qkv_slices.transpose(0, 2, 1, 3).reshape(PLANE, shard_rows, half_wide)
    qkv_piece = swap(qkv_slices, OCTET).reshape(PLANE * shard_rows, half_wide)
    gateup_slices = gateup_weight.reshape(shard_rows, 2, planes, 4, hidden_part // planes)
    gateup_slices = gateup_slices.transpose(3, 1, 0, 2, 4).reshape(PLANE, shard_rows, hidden_part)
    gateup_piece = swap(gateup_slices, OCTET).reshape(PLANE * shard_rows, hidden_part)

    qkv_full = jnp.concatenate(in_order(*whole(qkv_piece)), 1)
    out_slices = absolute(ring_gather(out_weight))
    out_slices = out_slices.reshape(4, out_planes, shard_rows, 2, half_width)
    out_slices = out_slices.transpose(0, 3, 1, 2, 4)
    out_piece = swap(out_slices.reshape(PLANE, out_planes, shard_rows, half_width), OCTET)
    out_piece = out_piece.transpose(1, 0, 2, 3).reshape(quarter, half_width)
    out_full = jnp.concatenate(in_order(out_piece, to_sibling(out_piece)), 1)
    out_full = jnp.pad(out_full, ((0, padded - quarter), (0, 0)))
    gateup_own, gateup_other = whole(gateup_piece)
    down_left, down_right = down_weight[:, :half_width], down_weight[:, half_width:]
    down_kept, down_sent = in_order(down_left, down_right)
    down_come = to_sibling(down_sent)
    down_piece = jnp.concatenate(in_order(down_kept, down_come), 0)
    down_full = jnp.concatenate(in_order(*whole(down_piece)), 1)

    padded_segments = jnp.concatenate([jnp.full((HALO,), -1, jnp.int32), segments])
    blocks = [
        lax.dynamic_slice_in_dim(padded_segments, (PLANE * z + 2 * b + c) * rows, ext)
        for b in range(4)
    ]
    seg_rows = jnp.stack(blocks)
    seg_keys = jnp.stack(
        [
            seg_rows[:, HALO - WINDOW + s * WINDOW : HALO + WINDOW + s * WINDOW]
            for s in range(subs)
        ],
        1,
    )
    seg_rows = jnp.broadcast_to(seg_rows[:, :, None], (4, ext, LANES))

    def gather_rows(array):
        return swap(jnp.broadcast_to(array, (4,) + array.shape), SQUARE)

    def scatter_rows(array):
        return jnp.sum(swap(array.astype(bf16), SQUARE).astype(f32), 0)

    own_tokens = tokens.astype(f32)
    normed = rms_scale(own_tokens, gain_one).astype(bf16)
    halo = lax.ppermute(normed[rows - HALO :], ALL, [(d, d + 1) for d in range(count - 1)])
    normed_group = gather_rows(jnp.concatenate([halo, normed])).reshape(4 * ext, width)
    projected = plain(normed_group, qkv_full).reshape(4, ext, 3 * padded)
    attended = attend(projected, taps, seg_rows, seg_keys, score_scale).reshape(4 * rows, padded)
    cotangent_group = gather_rows(cotangent).reshape(4 * rows, width)
    mixer_out = plain(attended, out_full).astype(bf16)
    residual = own_tokens + scatter_rows(mixer_out.reshape(4, rows, width))
    normed_dense = rms_scale(residual, gain_two).astype(bf16)
    dense_group = gather_rows(normed_dense).reshape(4 * rows, width)
    joined = in_order(plain(dense_group, gateup_own), plain(dense_group, gateup_other))
    hidden = swiglu(joined).astype(bf16)
    dense_out = plain(hidden, down_full).reshape(4, rows, width)
    layer_out = (residual + scatter_rows(dense_out)).astype(bf16)

    def core_sum(own, other):
        return (own + to_sibling(other.astype(bf16)).astype(f32)).astype(bf16)

    def scatter_planes(array):
        return lax.psum_scatter(array, "z", scatter_dimension=0)

    down_grad = core_sum(
        *in_order(
            contract_first(hidden, cotangent_group[:, :half_width]),
            contract_first(hidden, cotangent_group[:, half_width:]),
        )
    )
    down_mine = scatter_planes(down_grad.reshape(planes, 2 * down_rows, half_width))
    down_kept, down_sent = in_order(down_mine[:down_rows], down_mine[down_rows:])
    down_mine = jnp.concatenate(in_order(down_kept, to_sibling(down_sent)), 1)

    grad_hidden = contract_last(cotangent_group, down_full)
    unused, swiglu_back = jax.vjp(swiglu, joined)
    grad_gate, grad_up = swiglu_back(grad_hidden)[0]
    grad_own, grad_other = in_order(grad_gate.astype(bf16), grad_up.astype(bf16))
    grad_dense = contract_last(grad_own, gateup_own) + contract_last(grad_other, gateup_other)
    grad_dense = scatter_rows(grad_dense.reshape(4, rows, width))
    gateup_grad = core_sum(
        contract_first(dense_group, grad_own), contract_first(dense_group, grad_other)
    )
    gateup_mine = scatter_planes(gateup_grad.reshape(planes, PLANE * shard_rows, hidden_part))
    gateup_mine = swap(gateup_mine.reshape(PLANE, shard_rows, hidden_part), OCTET)
    gateup_mine = gateup_mine.reshape(4, 2, shard_rows, planes, hidden_part // planes)
    gateup_mine = gateup_mine.transpose(2, 1, 3, 0, 4).reshape(shard_rows, 2 * hidden_width)

    unused, dense_back = jax.vjp(rms_scale, residual, gain_two)
    grad_residual, dense_gain_sum = dense_back(grad_dense)
    grad_residual = grad_residual + cotangent.astype(f32)
    grad_branch = gather_rows(grad_residual.astype(bf16)).reshape(4 * rows, width)
    grad_attended = contract_last(grad_branch, out_full).astype(bf16)
    out_grad = core_sum(
        *in_order(
            contract_first(attended, grad_branch[:, :half_width])[:quarter],
            contract_first(attended, grad_branch[:, half_width:])[:quarter],
        )
    )
    out_mine = out_grad.reshape(out_planes, PLANE, shard_rows, half_width).transpose(1, 0, 2, 3)
    out_mine = swap(out_mine, OCTET).reshape(4, 2, out_planes, shard_rows, half_width)
    out_mine = out_mine.transpose(0, 2, 3, 1, 4).reshape(planes, shard_rows, width)
    out_mine = scatter_planes(out_mine)

    grad_projected, grad_taps = attend_back(
        projected, grad_attended.reshape(4, rows, padded), taps, seg_rows, seg_keys, score_scale
    )
    grad_projected = grad_projected.reshape(4 * ext, 3 * padded)
    qkv_grad = core_sum(
        *in_order(
            contract_first(normed_group, grad_projected[:, :half_wide]),
            contract_first(normed_group, grad_projected[:, half_wide:]),
        )
    )
    qkv_mine = scatter_planes(qkv_grad.reshape(planes, PLANE * shard_rows, half_wide))
    qkv_mine = swap(qkv_mine.reshape(PLANE, shard_rows, half_wide), OCTET)
    qkv_mine = qkv_mine.reshape(4, 2, shard_rows, half_wide).transpose(2, 0, 1, 3)
    qkv_mine = qkv_mine.reshape(shard_rows, 4, 3, padded)[..., :quarter].transpose(0, 2, 1, 3)
    qkv_mine = qkv_mine.reshape(shard_rows, 3 * width)

    grad_normed = scatter_rows(contract_last(grad_projected, qkv_full).reshape(4, ext, width))
    late = lax.ppermute(
        grad_normed[:HALO].astype(bf16), ALL, [(d, d - 1) for d in range(1, count)]
    ).astype(f32)
    grad_normed = grad_normed[HALO:] + jnp.pad(late, ((rows - HALO, 0), (0, 0)))
    unused, mixer_back = jax.vjp(rms_scale, own_tokens, gain_one)
    grad_rows, mixer_gain_sum = mixer_back(grad_normed)
    input_grad = grad_residual + grad_rows

    grad_taps = grad_taps[:3].reshape(3, 3, 1, padded)[..., :quarter]
    grad_taps = lax.dynamic_update_slice(
        jnp.zeros((3, 3, 4, quarter), f32), grad_taps, (0, 0, part, 0)
    )
    grad_taps = grad_taps.reshape(3, count, tap_columns).transpose(1, 0, 2)
    sums = jnp.concatenate(
        [
            mixer_gain_sum.reshape(count, shard_rows),
            dense_gain_sum.reshape(count, shard_rows),
            grad_taps.reshape(count, 3 * tap_columns),
        ],
        1,
    )
    sums = sums.reshape(planes, PLANE, -1).transpose(1, 0, 2)
    sums = jnp.sum(swap(sums, OCTET), 0)
    sums = jnp.sum(swap(sums, "z"), 0)
    return (
        layer_out,
        input_grad,
        sums[:shard_rows],
        qkv_mine.astype(f32),
        sums[2 * shard_rows :].reshape(3, tap_columns),
        out_mine.astype(f32),
        sums[shard_rows : 2 * shard_rows],
        gateup_mine.astype(f32),
        down_mine.astype(f32),
    )


def solution(mesh):
    planes = mesh.devices.size // PLANE
    split = Mesh(mesh.devices.reshape(planes, 2, 2, 2), ALL)
    over_rows = P(ALL, None)
    over_columns = P(None, ALL)
    return jax.shard_map(
        functools.partial(layer, planes),
        mesh=split,
        in_specs=(
            over_rows,
            P(),
            over_rows,
            P(ALL),
            over_rows,
            over_columns,
            over_rows,
            P(ALL),
            over_rows,
            over_rows,
        ),
        out_specs=(
            over_rows,
            over_rows,
            P(ALL),
            over_rows,
            over_columns,
            over_rows,
            P(ALL),
            over_rows,
            over_rows,
        ),
        check_vma=False,
    )
```

```python
import functools
import math

import jax
import jax.numpy as jnp
from jax import lax
from jax.experimental import pallas as pl
from jax.experimental.pallas import tpu as pltpu
from jax.sharding import Mesh, PartitionSpec as P

HDIM = 64
WINDOW = 64
HALO = 80
LANES = 128
PLANE = 8

eps_norm = 1e-05
masked_score = -1e30
bf16 = jnp.bfloat16
f32 = jnp.float32
MIB = 1024 * 1024
ALL = ("z", "y", "x", "core")
SQUARE = ("y", "x")
OCTET = ("y", "x", "core")
LINE = ("z", "core")


def rms_scale(values, gains):
    inverse = lax.rsqrt(jnp.mean(values * values, axis=-1, keepdims=True) + eps_norm)
    return values * inverse * gains


def contract_last(left_side, right_side):
    return lax.dot_general(
        left_side, right_side, (((1,), (1,)), ((), ())), preferred_element_type=f32
    )


def contract_first(left_side, right_side):
    return lax.dot_general(
        left_side, right_side, (((0,), (0,)), ((), ())), preferred_element_type=f32
    )


def plain(left_side, right_side):
    return jnp.dot(left_side, right_side, preferred_element_type=f32)


def shifted_down(values, by):
    return pltpu.roll(values, by, 0)


def shifted_up(values, by):
    return pltpu.roll(values, values.shape[0] - by, 0)


def gate_of(values, taps, same_one, same_two):
    conv = (
        taps[0:1] * values
        + taps[1:2] * (same_one * shifted_down(values, 1))
        + taps[2:3] * (same_two * shifted_down(values, 2))
    )
    return conv, jax.nn.sigmoid(values)


def by_head(values):
    lane = lax.broadcasted_iota(jnp.int32, values.shape, 1)
    zero = jnp.zeros_like(values)
    return jnp.concatenate(
        [jnp.where(lane < HDIM, values, zero), jnp.where(lane < HDIM, zero, values)], 0
    )


def join_heads(values):
    half = values.shape[0] // 2
    lane = lax.broadcasted_iota(jnp.int32, (half, values.shape[1]), 1)
    return jnp.where(lane < HDIM, values[:half], values[half:])


def block_masks(seg_ref, keys_ref, subs):
    span = 2 * WINDOW
    row = lax.broadcasted_iota(jnp.int32, (WINDOW, span), 0)
    col = lax.broadcasted_iota(jnp.int32, (WINDOW, span), 1)
    near = (col > row) & (col <= row + WINDOW)
    masks = []
    for sub in range(subs):
        first = HALO + sub * WINDOW
        same = seg_ref[0, first : first + WINDOW] == keys_ref[0, sub : sub + 1]
        masks.append(near & same)
    return jnp.concatenate([mask for mask in masks for unused in range(2)], 0)


def same_rows(seg_ref):
    seg = seg_ref[0]
    same_one = (seg == shifted_down(seg, 1)).astype(f32)
    same_two = (seg == shifted_down(seg, 2)).astype(f32)
    return same_one, same_two


def pair_probs(queries, keysets, mask, score_scale):
    scores = jnp.concatenate([contract_last(q, k) for q, k in zip(queries, keysets)], 0)
    scores = jnp.where(mask, scores * score_scale, masked_score)
    exponent = jnp.exp(scores - jnp.max(scores, axis=-1, keepdims=True))
    return exponent * (1.0 / jnp.sum(exponent, axis=-1, keepdims=True))


def cut(values, subs, first, size):
    return [values[first + s * WINDOW : first + s * WINDOW + size] for s in range(subs)]


def parts_of(values, subs):
    return jnp.split(values, subs, 0)


def place_pieces(refs, chunk, where_ref, row, target, sems):
    copies = []
    for ref in refs:
        for first in range(0, ref.shape[0] // chunk * chunk, chunk):
            spot = pl.multiple_of(where_ref[row + len(copies), 1], 16)
            copy = pltpu.make_async_copy(
                ref.at[first : first + chunk],
                target.at[where_ref[row + len(copies), 0], pl.ds(spot, chunk)],
                sems.at[row + len(copies)],
            )
            copy.start()
            copies.append(copy)
    return copies


def attend_kernel(
    where_ref,
    tokens_ref,
    halo_ref,
    gain_ref,
    taps_ref,
    seg_ref,
    keys_ref,
    *rest,
    n,
    chunk,
    subs,
    score_scale,
):
    piece_refs, (out_ref, proj_ref, weight_ref, normed_ref, sems) = rest[:n], rest[n:]

    @pl.when(pl.program_id(0) == 0)
    def fetch():
        for copy in place_pieces(piece_refs, chunk, where_ref, 0, weight_ref, sems):
            copy.wait()

    normed_ref[0, :HALO] = rms_scale(halo_ref[0].astype(f32), gain_ref[...]).astype(bf16)
    normed_ref[0, HALO:] = rms_scale(tokens_ref[0].astype(f32), gain_ref[...]).astype(bf16)
    half_wide = weight_ref.shape[2]
    for half in range(2):
        proj_ref[0, :, half * half_wide : (half + 1) * half_wide] = plain(
            normed_ref[0], weight_ref[half]
        )
    pairs = 2 * half_wide // (3 * LANES)
    same_one, same_two = same_rows(seg_ref)
    mask = block_masks(seg_ref, keys_ref, subs)
    first_key = HALO - WINDOW
    for pair in range(pairs):
        mixed = []
        for kind in range(3):
            at = (kind * pairs + pair) * LANES
            conv, sig = gate_of(
                proj_ref[0, :, at : at + LANES], taps_ref[:, at : at + LANES], same_one, same_two
            )
            mixed.append((conv * sig).astype(bf16))
        queries = [by_head(q) for q in cut(mixed[0], subs, HALO, WINDOW)]
        keysets = cut(mixed[1], subs, first_key, 2 * WINDOW)
        valuesets = cut(mixed[2], subs, first_key, 2 * WINDOW)
        weights = parts_of(pair_probs(queries, keysets, mask, score_scale).astype(bf16), subs)
        for sub in range(subs):
            out_ref[0, sub * WINDOW : (sub + 1) * WINDOW, pair * LANES : (pair + 1) * LANES] = (
                join_heads(plain(weights[sub], valuesets[sub])).astype(bf16)
            )


def attend_back_kernel(
    branch_ref, out_weight_ref, proj_ref, taps_ref, seg_ref, keys_ref, out_ref, tap_ref, *, subs, score_scale
):
    @pl.when(pl.program_id(0) == 0)
    def clear():
        tap_ref[...] = jnp.zeros_like(tap_ref)

    grad_attended = contract_last(branch_ref[0], out_weight_ref[...]).astype(bf16)
    pairs = proj_ref.shape[2] // (3 * LANES)
    same_one, same_two = same_rows(seg_ref)
    mask = block_masks(seg_ref, keys_ref, subs)
    first_key = HALO - WINDOW
    for pair in range(pairs):
        values, convs, sigs, mixed = [], [], [], []
        for kind in range(3):
            at = (kind * pairs + pair) * LANES
            value = proj_ref[0, :, at : at + LANES]
            conv, sig = gate_of(value, taps_ref[:, at : at + LANES], same_one, same_two)
            values.append(value)
            convs.append(conv)
            sigs.append(sig)
            mixed.append((conv * sig).astype(bf16))
        queries = [by_head(q) for q in cut(mixed[0], subs, HALO, WINDOW)]
        keysets = cut(mixed[1], subs, first_key, 2 * WINDOW)
        valuesets = cut(mixed[2], subs, first_key, 2 * WINDOW)
        grads = [
            by_head(g)
            for g in cut(grad_attended[:, pair * LANES : (pair + 1) * LANES], subs, 0, WINDOW)
        ]
        probs = pair_probs(queries, keysets, mask, score_scale)
        grad_probs = jnp.concatenate([contract_last(g, v) for g, v in zip(grads, valuesets)], 0)
        inner = jnp.sum(probs * grad_probs, axis=-1, keepdims=True)
        grad_scores = parts_of((probs * (grad_probs - inner)).astype(bf16), subs)
        weights = parts_of(probs.astype(bf16), subs)
        grad_queries = [
            join_heads(plain(g, k)) * score_scale for g, k in zip(grad_scores, keysets)
        ]
        grad_keys = [contract_first(g, q) * score_scale for g, q in zip(grad_scores, queries)]
        grad_values = [contract_first(w, g) for w, g in zip(weights, grads)]

        def overlapped(parts):
            rows = [jnp.zeros((first_key, LANES), f32), parts[0][:WINDOW]]
            for sub in range(1, subs):
                rows.append(parts[sub - 1][WINDOW:] + parts[sub][:WINDOW])
            rows.append(parts[subs - 1][WINDOW:])
            return jnp.concatenate(rows, 0)

        grads_mixed = (
            jnp.concatenate([jnp.zeros((HALO, LANES), f32)] + grad_queries, 0),
            overlapped(grad_keys),
            overlapped(grad_values),
        )
        for kind in range(3):
            at = (kind * pairs + pair) * LANES
            taps = taps_ref[:, at : at + LANES]
            through = grads_mixed[kind] * sigs[kind]
            one = same_one * through
            two = same_two * through
            summed = (
                through * convs[kind] * (1.0 - sigs[kind])
                + taps[0:1] * through
                + taps[1:2] * shifted_up(one, 1)
                + taps[2:3] * shifted_up(two, 2)
            )
            out_ref[0, :, at : at + LANES] = summed.astype(bf16)
            value = values[kind]
            tap_ref[0:1, at : at + LANES] += jnp.sum(through * value, 0, keepdims=True)
            tap_ref[1:2, at : at + LANES] += jnp.sum(
                one * shifted_down(value, 1), 0, keepdims=True
            )
            tap_ref[2:3, at : at + LANES] += jnp.sum(
                two * shifted_down(value, 2), 0, keepdims=True
            )


def attention_specs(rows, columns, subs):
    return [
        pl.BlockSpec((3, columns), lambda b: (0, 0)),
        pl.BlockSpec((1, rows, LANES), lambda b: (b, 0, 0)),
        pl.BlockSpec((1, subs, 2 * WINDOW), lambda b: (b, 0, 0)),
    ]


def attend(where, tokens, halo, gain, taps, seg_rows, seg_keys, pieces, chunk, score_scale):
    blocks, rows, width = tokens.shape
    rows += HALO
    columns = taps.shape[1]
    subs = seg_keys.shape[1]
    copies = sum(p.shape[0] // chunk for p in pieces)
    return pl.pallas_call(
        functools.partial(
            attend_kernel, n=len(pieces), chunk=chunk, subs=subs, score_scale=score_scale
        ),
        grid=(blocks,),
        out_shape=(
            jax.ShapeDtypeStruct((blocks, rows - HALO, columns // 3), bf16),
            jax.ShapeDtypeStruct((blocks, rows, columns), f32),
            jax.ShapeDtypeStruct((2, width, columns // 2), bf16),
            jax.ShapeDtypeStruct((blocks, rows, width), bf16),
        ),
        in_specs=[
            pl.BlockSpec(memory_space=pltpu.SMEM),
            pl.BlockSpec((1, rows - HALO, width), lambda b: (b, 0, 0)),
            pl.BlockSpec((1, HALO, width), lambda b: (b, 0, 0)),
            pl.BlockSpec((1, width), lambda b: (0, 0)),
        ]
        + attention_specs(rows, columns, subs)
        + [pl.BlockSpec(memory_space=pl.ANY)] * len(pieces),
        out_specs=(
            pl.BlockSpec((1, rows - HALO, columns // 3), lambda b: (b, 0, 0)),
            pl.BlockSpec((1, rows, columns), lambda b: (b, 0, 0)),
            pl.BlockSpec((2, width, columns // 2), lambda b: (0, 0, 0)),
            pl.BlockSpec((1, rows, width), lambda b: (b, 0, 0)),
        ),
        scratch_shapes=[pltpu.SemaphoreType.DMA((copies,))],
        compiler_params=pltpu.CompilerParams(vmem_limit_bytes=48 * MIB),
        cost_estimate=pl.CostEstimate(
            flops=20 * 10**9, bytes_accessed=20 * 10**6, transcendentals=0
        ),
        name="attend",
    )(where, tokens, halo, gain, taps, seg_rows, seg_keys, *pieces)


def attend_back(branch, out_weight, projected, taps, seg_rows, seg_keys, score_scale):
    blocks, rows, columns = projected.shape
    width = branch.shape[2]
    subs = seg_keys.shape[1]
    return pl.pallas_call(
        functools.partial(attend_back_kernel, subs=subs, score_scale=score_scale),
        grid=(blocks,),
        out_shape=(
            jax.ShapeDtypeStruct((blocks, rows, columns), bf16),
            jax.ShapeDtypeStruct((8, columns), f32),
        ),
        in_specs=[
            pl.BlockSpec((1, rows - HALO, width), lambda b: (b, 0, 0)),
            pl.BlockSpec((columns // 3, width), lambda b: (0, 0)),
            pl.BlockSpec((1, rows, columns), lambda b: (b, 0, 0)),
        ]
        + attention_specs(rows, columns, subs),
        out_specs=(
            pl.BlockSpec((1, rows, columns), lambda b: (b, 0, 0)),
            pl.BlockSpec((8, columns), lambda b: (0, 0)),
        ),
        compiler_params=pltpu.CompilerParams(vmem_limit_bytes=48 * MIB),
        cost_estimate=pl.CostEstimate(
            flops=20 * 10**9, bytes_accessed=20 * 10**6, transcendentals=0
        ),
        name="attend_back",
    )(branch, out_weight, projected, taps, seg_rows, seg_keys)


def dense_kernel(where_ref, dense_ref, cotangent_ref, *rest, n_gate, n_down, gate_chunk, down_chunk):
    gate_refs, down_refs = rest[:n_gate], rest[n_gate : n_gate + n_down]
    grad_ref, hidden_ref, inner_ref, down_ref, gate_ref, sems = rest[n_gate + n_down :]
    gate_copies = place_pieces(gate_refs, gate_chunk, where_ref, 0, gate_ref, sems)
    down_copies = place_pieces(
        down_refs, down_chunk, where_ref, len(gate_copies), down_ref, sems
    )
    real = down_refs[0].shape[0] // 2
    if real < down_ref.shape[1]:
        down_ref[:, real:] = jnp.zeros((2, down_ref.shape[1] - real, down_ref.shape[2]), bf16)
    for copy in gate_copies + down_copies:
        copy.wait()
    rows, width = dense_ref.shape
    hidden_part = hidden_ref.shape[1]
    half_width = down_ref.shape[2]
    tile = 256

    @pl.loop(0, rows // tile)
    def block(index):
        own = pl.ds(pl.multiple_of(index * tile, tile), tile)
        dense = dense_ref[own, :]
        left = cotangent_ref[own, :half_width]
        right = cotangent_ref[own, half_width:]
        for first in range(0, hidden_part, tile):
            unit = slice(first, min(first + tile, hidden_part))
            gate = plain(dense, gate_ref[0, :, unit])
            up = plain(dense, gate_ref[1, :, unit])
            grad = contract_last(left, down_ref[0, unit]) + contract_last(right, down_ref[1, unit])
            sig = jax.nn.sigmoid(gate)
            silu = gate * sig
            hidden_ref[own, unit] = (silu * up).astype(bf16)
            inner_ref[0, own, unit] = (grad * up * (sig * (1.0 + gate * (1.0 - sig)))).astype(bf16)
            inner_ref[1, own, unit] = (grad * silu).astype(bf16)
        gates = inner_ref[0, own, :]
        ups = inner_ref[1, own, :]
        for first in range(0, width, tile):
            unit = slice(first, first + tile)
            grad_ref[own, unit] = (
                contract_last(gates, gate_ref[0, unit]) + contract_last(ups, gate_ref[1, unit])
            ).astype(bf16)


def dense(where, dense_group, cotangent_group, gate_pieces, gate_chunk, down_pieces, down_chunk):
    rows, width = dense_group.shape
    hidden_part = gate_pieces[0].shape[1]
    copies = sum(p.shape[0] // gate_chunk for p in gate_pieces)
    copies += sum(p.shape[0] // down_chunk for p in down_pieces)
    whole = pl.BlockSpec(memory_space=pltpu.VMEM)
    return pl.pallas_call(
        functools.partial(
            dense_kernel,
            n_gate=len(gate_pieces),
            n_down=len(down_pieces),
            gate_chunk=gate_chunk,
            down_chunk=down_chunk,
        ),
        out_shape=(
            jax.ShapeDtypeStruct((rows, width), bf16),
            jax.ShapeDtypeStruct((rows, hidden_part), bf16),
            jax.ShapeDtypeStruct((2, rows, hidden_part), bf16),
            jax.ShapeDtypeStruct((2, hidden_part, width // 2), bf16),
        ),
        in_specs=[pl.BlockSpec(memory_space=pltpu.SMEM), whole, whole]
        + [pl.BlockSpec(memory_space=pl.ANY)] * (len(gate_pieces) + len(down_pieces)),
        out_specs=(whole, whole, whole, whole),
        scratch_shapes=[
            pltpu.VMEM((2, width, hidden_part), bf16),
            pltpu.SemaphoreType.DMA((copies,)),
        ],
        compiler_params=pltpu.CompilerParams(vmem_limit_bytes=56 * MIB),
        cost_estimate=pl.CostEstimate(
            flops=30 * 10**9, bytes_accessed=30 * 10**6, transcendentals=0
        ),
        name="dense",
    )(where, dense_group, cotangent_group, *gate_pieces, *down_pieces)


def weight_grad_kernel(left_ref, right_ref, out_ref):
    right = right_ref[...].reshape(right_ref.shape[-2:])
    product = contract_first(left_ref[...], right).astype(bf16)
    planes, unused, rows, columns = out_ref.shape
    out_ref[:, 0] = product[: planes * rows].reshape(planes, rows, columns)


def weight_grad(left, right, planes, rows, name):
    tokens, depth = left.shape
    columns = right.shape[-1] if right.ndim == 3 else right.shape[-1] // 2
    steps = 2 if planes * rows == depth else 1
    if right.ndim == 3:
        right_spec = pl.BlockSpec((1, tokens, columns), lambda h, k: (h, 0, 0))
    else:
        right_spec = pl.BlockSpec((tokens, columns), lambda h, k: (0, h))
    return pl.pallas_call(
        weight_grad_kernel,
        grid=(2, steps),
        out_shape=jax.ShapeDtypeStruct((planes, 2, rows, columns), bf16),
        in_specs=[pl.BlockSpec((tokens, depth // steps), lambda h, k: (0, k)), right_spec],
        out_specs=pl.BlockSpec((planes // steps, 1, rows, columns), lambda h, k: (k, h, 0, 0)),
        compiler_params=pltpu.CompilerParams(vmem_limit_bytes=48 * MIB),
        cost_estimate=pl.CostEstimate(flops=10**6, bytes_accessed=10**4, transcendentals=0),
        name=name,
    )(left, right)


def fence(*values):
    return lax.optimization_barrier(values)


def layer(
    planes,
    tokens,
    segments,
    cotangent,
    mixer_gain,
    qkv_weight,
    conv_taps,
    out_weight,
    dense_gain,
    gateup_weight,
    down_weight,
):
    count = planes * PLANE
    rows, width = tokens.shape
    ext = HALO + rows
    subs = rows // WINDOW
    quarter = width // 4
    padded = -(-quarter // LANES) * LANES
    half_wide = 3 * padded // 2
    half_width = width // 2
    shard_rows = qkv_weight.shape[0]
    down_rows = down_weight.shape[0]
    square_rows = 4 * shard_rows
    octet_rows = PLANE * shard_rows
    hidden_width = down_rows * count
    hidden_part = hidden_width // 4
    hidden_wide = -(-hidden_part // 256) * 256
    tap_columns = conv_taps.shape[1]
    out_planes = planes // 4
    z = lax.axis_index("z")
    y = lax.axis_index("y")
    x = lax.axis_index("x")
    c = lax.axis_index("core")
    part = 2 * y + x
    score_scale = 1.0 / math.sqrt(HDIM)

    def swap(array, axes):
        return lax.all_to_all(array, axes, 0, 0)

    def flip(array, axis):
        return lax.ppermute(array, axis, [(0, 1), (1, 0)])

    def in_order(own, other, bit):
        return jnp.where(bit == 0, own, other), jnp.where(bit == 0, other, own)

    def absolute(pieces, size, mine):
        stacked = jnp.concatenate([p[None] for p in pieces + pieces], 0)
        return lax.dynamic_slice_in_dim(stacked, size - mine, size, 0)

    def gather_rows(array, axes):
        return swap(jnp.broadcast_to(array, (4,) + array.shape), axes)

    def rows_at(bits, size):
        return jnp.stack([jnp.asarray(b, jnp.int32) for b in bits]).reshape(-1, size)

    qkv_slices = qkv_weight.reshape(shard_rows, 3, 4, quarter)
    qkv_slices = jnp.pad(qkv_slices, ((0, 0), (0, 0), (0, 0), (0, padded - quarter)))
    qkv_slices = qkv_slices.transpose(2, 0, 1, 3).reshape(4, shard_rows, 2, half_wide)
    qkv_slices = qkv_slices.transpose(0, 2, 1, 3).reshape(PLANE, shard_rows, half_wide)
    owned = jnp.concatenate([mixer_gain, dense_gain, conv_taps.reshape(-1)])
    owned_size = owned.shape[0]
    owned = jnp.pad(owned.reshape(1, -1), ((0, 1), (0, half_wide - owned_size)))
    owned = jnp.broadcast_to(owned, (PLANE, 2, half_wide))
    (qkv_slices,) = fence(jnp.concatenate([qkv_slices, owned], 1))

    qkv_piece = swap(qkv_slices, OCTET)
    gateup_slices = gateup_weight.reshape(shard_rows, 2, planes, 4, hidden_part // planes)
    gateup_slices = gateup_slices.transpose(3, 1, 0, 2, 4)
    gateup_slices = gateup_slices.reshape(PLANE, shard_rows, hidden_part)
    gateup_slices = jnp.pad(gateup_slices, ((0, 0), (0, 0), (0, hidden_wide - hidden_part)))
    down_kept, down_sent = in_order(down_weight[:, :half_width], down_weight[:, half_width:], c)
    down_piece = jnp.concatenate(in_order(down_kept, flip(down_sent, "core"), c), 0)
    qkv_piece, gateup_slices, down_piece, tokens_now = fence(
        qkv_piece, gateup_slices, down_piece, tokens
    )
    qkv_piece = jnp.concatenate(
        [
            qkv_piece[:, :shard_rows].reshape(octet_rows, half_wide),
            qkv_piece[:, shard_rows:].reshape(2 * PLANE, half_wide),
        ]
    )
    (qkv_piece,) = fence(qkv_piece)

    qkv_pieces, qkv_others, out_rows = [qkv_piece], [], [out_weight]
    onward = [(i, (i - 1) % planes) for i in range(planes)]
    for step in range(1, planes):
        qkv_next = lax.ppermute(qkv_pieces[-1], "z", onward)
        out_next = lax.ppermute(out_rows[-1], "z", onward)
        if step == 1:
            gateup_piece = swap(gateup_slices, OCTET).reshape(octet_rows, hidden_wide)
            qkv_next, out_next, gateup_piece, tokens_now = fence(
                qkv_next, out_next, gateup_piece, tokens_now
            )
            token_group = gather_rows(tokens_now, SQUARE)
        elif step < planes - 1:
            qkv_next, out_next = fence(qkv_next, out_next)
        else:
            qkv_next, out_next, token_group = fence(qkv_next, out_next, token_group)
        qkv_others.append(flip(qkv_pieces[-1][:octet_rows], "core"))
        qkv_pieces.append(qkv_next)
        out_rows.append(out_next)
    qkv_pieces, gateup_piece, down_piece, cotangent_now = fence(
        qkv_pieces, gateup_piece, down_piece, cotangent
    )
    gateup_all = lax.all_gather(gateup_piece, LINE)
    down_all = lax.all_gather(down_piece, LINE)
    out_slices = absolute(out_rows, planes, z)
    out_slices = out_slices.reshape(4, out_planes, shard_rows, 2, half_width)
    out_slices = out_slices.transpose(0, 3, 1, 2, 4)
    out_slices = out_slices.reshape(PLANE, out_planes, shard_rows, half_width)

    tails = token_group[:, rows - HALO :]
    near_halo = flip(tails, "core")
    far_halo = lax.ppermute(
        tails[3],
        LINE,
        [(2 * i + 1, 2 * i + 2) for i in range(planes - 1)],
    )
    halo = jnp.where(c == 0, jnp.concatenate([far_halo[None], near_halo[:3]]), near_halo)
    qkv_others.append(flip(qkv_pieces[-1][:octet_rows], "core"))
    small = absolute([p[octet_rows : octet_rows + 2 * PLANE] for p in qkv_pieces], planes, z)
    small = small.reshape(planes, PLANE, 2, half_wide)[:, :, 0, :owned_size].astype(f32)
    gain_one = small[:, :, :shard_rows].reshape(1, width)
    gain_two = small[:, :, shard_rows : 2 * shard_rows].reshape(width)
    taps = small[:, :, 2 * shard_rows :].reshape(count, 3, tap_columns).transpose(1, 0, 2)
    taps = lax.dynamic_index_in_dim(taps.reshape(3, 3, 4, quarter), part, 2, keepdims=False)
    taps = jnp.pad(taps, ((0, 0), (0, 0), (0, padded - quarter))).reshape(3, 3 * padded)
    qkv_others, halo, out_slices, gain_one, taps = fence(
        qkv_others, halo, out_slices, gain_one, taps
    )
    out_piece = swap(out_slices, OCTET)
    out_piece = out_piece.transpose(1, 0, 2, 3).reshape(quarter, half_width)

    padded_segments = jnp.concatenate([jnp.full((HALO,), -1, jnp.int32), segments])
    seg_rows = jnp.stack(
        [
            lax.dynamic_slice_in_dim(padded_segments, (PLANE * z + 2 * b + c) * rows, ext)
            for b in range(4)
        ]
    )
    seg_keys = jnp.stack(
        [
            seg_rows[:, HALO - WINDOW + s * WINDOW : HALO + WINDOW + s * WINDOW]
            for s in range(subs)
        ],
        1,
    )
    seg_rows = jnp.broadcast_to(seg_rows[:, :, None], (4, ext, LANES))

    where_qkv = []
    for own in range(2):
        for step in range(planes):
            where_qkv += [c ^ own, (z + step) % planes * octet_rows]
    attended, projected, qkv_full, normed_group = attend(
        rows_at(where_qkv, 2),
        token_group,
        halo,
        gain_one,
        taps,
        seg_rows,
        seg_keys,
        qkv_pieces + qkv_others,
        octet_rows,
        score_scale,
    )
    attended = attended.reshape(4 * rows, padded)
    attended, normed_group, out_piece = fence(attended, normed_group, out_piece)
    out_other = flip(out_piece, "core")
    out_full = jnp.concatenate(in_order(out_piece, out_other, c), 1)
    out_full = jnp.pad(out_full, ((0, padded - quarter), (0, 0)))
    mixer_out = plain(attended, out_full).astype(bf16).reshape(4, rows, width)

    mixer_sum = swap(mixer_out, SQUARE)
    own_tokens = tokens.astype(f32)
    residual = own_tokens + jnp.sum(mixer_sum.astype(f32), 0)
    normed_dense = rms_scale(residual, gain_two).astype(bf16)
    dense_group = gather_rows(normed_dense, SQUARE).reshape(4 * rows, width)
    dense_group, cotangent_now = fence(dense_group, cotangent_now)
    cotangent_group = gather_rows(cotangent_now, SQUARE).reshape(4 * rows, width)

    gateup_chunk, down_chunk = octet_rows, 2 * down_rows
    where_gateup = [k for i in range(planes) for h in range(2) for k in (h, i * gateup_chunk)]
    where_down = [k for i in range(planes) for h in range(2) for k in (h, i * down_chunk)]
    if down_chunk % 16:
        down_chunk, where_down = hidden_part, [0, 0, 1, 0]
        down_all = down_all.reshape(planes, 2, -1, half_width).transpose(1, 0, 2, 3)
    gateup_all = gateup_all.reshape(-1, hidden_wide)
    down_all = down_all.reshape(-1, half_width)
    grad_dense, hidden, grad_inner, down_full = fence(
        *dense(
            rows_at(where_gateup + where_down, 2),
            dense_group,
            cotangent_group,
            [gateup_all],
            gateup_chunk,
            [down_all],
            down_chunk,
        )
    )

    def by_core(halves):
        return (jnp.where(c == 0, halves[0], halves[1]), jnp.where(c == 0, halves[1], halves[0]))

    def core_pair(left_side, halves):
        own, other = by_core(halves)
        other = contract_first(left_side, other).astype(bf16)
        return contract_first(left_side, own), other

    def scatter_line(array):
        return lax.psum_scatter(
            array.reshape((2 * planes,) + array.shape[2:]), LINE, scatter_dimension=0
        )

    grad_dense = swap(grad_dense.reshape(4, rows, width), SQUARE)
    if 2 * down_rows % 16:
        down_grad = contract_first(hidden, cotangent_group)[:hidden_part].astype(bf16)
        down_grad = down_grad.reshape(planes, 2 * down_rows, 2, half_width).transpose(0, 2, 1, 3)
    else:
        down_grad = weight_grad(hidden, cotangent_group, planes, 2 * down_rows, "down_grad")
    gateup_grad = weight_grad(dense_group, grad_inner, planes, octet_rows, "gateup_grad")
    down_mine = scatter_line(down_grad)
    gateup_mine = scatter_line(gateup_grad)
    grad_dense, hidden, down_full = fence(grad_dense, hidden, down_full)

    unused, dense_back = jax.vjp(rms_scale, residual, gain_two)
    grad_residual, dense_gain_sum = dense_back(jnp.sum(grad_dense.astype(f32), 0))
    grad_residual = grad_residual + cotangent.astype(f32)
    grad_branch = gather_rows(grad_residual.astype(bf16), SQUARE)
    dense_out = jnp.concatenate([plain(hidden, down_full[0]), plain(hidden, down_full[1])], 1)
    dense_out = dense_out.astype(bf16).reshape(4, rows, width)
    grad_branch, out_full, dense_out = fence(grad_branch, out_full, dense_out)
    dense_sum = swap(dense_out, SQUARE)

    grad_projected, grad_taps = attend_back(
        grad_branch, out_full, projected, taps, seg_rows, seg_keys, score_scale
    )
    grad_projected, grad_taps = fence(grad_projected, grad_taps)

    grad_projected = grad_projected.reshape(4 * ext, 3 * padded)
    normed_rows = normed_group.reshape(4 * ext, width)
    qkv_grad = weight_grad(normed_rows, grad_projected, planes, octet_rows, "qkv_grad")
    qkv_grad, grad_projected, grad_branch, attended = fence(
        qkv_grad, grad_projected, grad_branch, attended
    )
    qkv_part = scatter_line(qkv_grad)

    grad_branch = grad_branch.reshape(4 * rows, width)
    out_own, out_other = core_pair(
        attended, (grad_branch[:, :half_width], grad_branch[:, half_width:])
    )
    out_grad = (out_own + flip(out_other, "core").astype(f32)).astype(bf16)
    grad_normed = contract_last(grad_projected[:, :half_wide], qkv_full[0])
    grad_normed = grad_normed + contract_last(grad_projected[:, half_wide:], qkv_full[1])
    grad_normed = grad_normed.astype(bf16).reshape(4, ext, width)
    grad_halo = grad_normed[:, :HALO]
    near_grad = flip(grad_halo, "core")
    far_grad = lax.ppermute(
        grad_halo[0],
        LINE,
        [(2 * i, 2 * i - 1) for i in range(1, planes)],
    )
    halo_grad = jnp.where(
        c == 0, near_grad, jnp.concatenate([near_grad[1:], far_grad[None]])
    )
    grad_normed = grad_normed[:, HALO:].astype(f32) + jnp.pad(
        halo_grad.astype(f32), ((0, 0), (rows - HALO, 0), (0, 0))
    )
    grad_normed = grad_normed.astype(bf16)
    dense_sum, grad_normed = fence(dense_sum, grad_normed)
    normed_sum = swap(grad_normed, SQUARE)
    normed_sum, out_grad, gateup_mine = fence(normed_sum, out_grad, gateup_mine)
    out_mine = out_grad[:quarter].reshape(out_planes, PLANE, shard_rows, half_width)
    out_mine = swap(out_mine.transpose(1, 0, 2, 3), OCTET)

    qkv_mine = swap(qkv_part.reshape(PLANE, shard_rows, half_wide), OCTET)
    out_mine = out_mine.reshape(4, 2, out_planes, shard_rows, half_width)
    out_mine = out_mine.transpose(0, 2, 3, 1, 4).reshape(planes, shard_rows, width)
    out_mine = jnp.sum(swap(out_mine, "z").astype(f32), 0)
    down_kept, down_sent = in_order(down_mine[:down_rows], down_mine[down_rows:], c)
    down_mine = jnp.concatenate(in_order(down_kept, flip(down_sent, "core"), c), 1)

    qkv_mine = qkv_mine.reshape(4, 2, shard_rows, half_wide).transpose(2, 0, 1, 3)
    qkv_mine = qkv_mine.reshape(shard_rows, 4, 3, padded)[..., :quarter].transpose(0, 2, 1, 3)
    qkv_mine = qkv_mine.reshape(shard_rows, 3 * width)
    gateup_mine = swap(gateup_mine.reshape(PLANE, shard_rows, hidden_wide), OCTET)
    gateup_mine = gateup_mine[:, :, :hidden_part]
    gateup_mine = gateup_mine.reshape(4, 2, shard_rows, planes, hidden_part // planes)
    gateup_mine = gateup_mine.transpose(2, 1, 3, 0, 4).reshape(shard_rows, 2 * hidden_width)
    layer_out = (residual + jnp.sum(dense_sum.astype(f32), 0)).astype(bf16)

    grad_normed = jnp.sum(normed_sum.astype(f32), 0)
    unused, mixer_back = jax.vjp(rms_scale, own_tokens, gain_one.reshape(width))
    grad_rows, mixer_gain_sum = mixer_back(grad_normed)
    input_grad = grad_residual + grad_rows

    grad_taps = grad_taps[:3].reshape(3, 3, 1, padded)[..., :quarter]
    grad_taps = lax.dynamic_update_slice(
        jnp.zeros((3, 3, 4, quarter), f32), grad_taps, (0, 0, part, 0)
    )
    grad_taps = grad_taps.reshape(3, count, tap_columns).transpose(1, 0, 2)
    sums = jnp.concatenate(
        [
            mixer_gain_sum.reshape(count, shard_rows),
            dense_gain_sum.reshape(count, shard_rows),
            grad_taps.reshape(count, 3 * tap_columns),
        ],
        1,
    )
    sums = sums.reshape(planes, PLANE, -1).transpose(1, 0, 2)
    sums = jnp.sum(swap(sums, OCTET), 0)
    sums = jnp.sum(swap(sums, "z"), 0)
    return (
        layer_out,
        input_grad,
        sums[:shard_rows],
        qkv_mine.astype(f32),
        sums[2 * shard_rows :].reshape(3, tap_columns),
        out_mine,
        sums[shard_rows : 2 * shard_rows],
        gateup_mine.astype(f32),
        down_mine.astype(f32),
    )


def solution(mesh):
    planes = mesh.devices.size // PLANE
    split = Mesh(mesh.devices.reshape(planes, 2, 2, 2), ALL)
    over_rows = P(ALL, None)
    over_columns = P(None, ALL)
    return jax.shard_map(
        functools.partial(layer, planes),
        mesh=split,
        in_specs=(
            over_rows,
            P(),
            over_rows,
            P(ALL),
            over_rows,
            over_columns,
            over_rows,
            P(ALL),
            over_rows,
            over_rows,
        ),
        out_specs=(
            over_rows,
            over_rows,
            P(ALL),
            over_rows,
            over_columns,
            over_rows,
            P(ALL),
            over_rows,
            over_rows,
        ),
        check_vma=False,
    )
```

```python
import functools
import math

import jax
import jax.numpy as jnp
from jax import lax
from jax.experimental import pallas as pl
from jax.experimental.pallas import tpu as pltpu
from jax.sharding import Mesh, PartitionSpec as P

HDIM = 64
WINDOW = 64
HALO = 80
LANES = 128
PLANE = 8

eps_norm = 1e-05
masked_score = -1e30
bf16 = jnp.bfloat16
f32 = jnp.float32
MIB = 1024 * 1024
TILE = 256
ALL = ("z", "y", "x", "core")
SQUARE = ("y", "x")
OCTET = ("y", "x", "core")
LINE = ("z", "core")


def rms_scale(values, gains):
    inverse = lax.rsqrt(jnp.mean(values * values, axis=-1, keepdims=True) + eps_norm)
    return values * inverse * gains


def contract_last(left_side, right_side):
    return lax.dot_general(
        left_side, right_side, (((1,), (1,)), ((), ())), preferred_element_type=f32
    )


def contract_first(left_side, right_side):
    return lax.dot_general(
        left_side, right_side, (((0,), (0,)), ((), ())), preferred_element_type=f32
    )


def plain(left_side, right_side):
    return jnp.dot(left_side, right_side, preferred_element_type=f32)


def shifted_down(values, by):
    return pltpu.roll(values, by, 0)


def shifted_up(values, by):
    return pltpu.roll(values, values.shape[0] - by, 0)


def gate_of(values, taps, same_one, same_two):
    conv = (
        taps[0:1] * values
        + taps[1:2] * (same_one * shifted_down(values, 1))
        + taps[2:3] * (same_two * shifted_down(values, 2))
    )
    return conv, jax.nn.sigmoid(values)


def by_head(values):
    lane = lax.broadcasted_iota(jnp.int32, values.shape, 1)
    zero = jnp.zeros_like(values)
    return jnp.concatenate(
        [jnp.where(lane < HDIM, values, zero), jnp.where(lane < HDIM, zero, values)], 0
    )


def join_heads(values):
    half = values.shape[0] // 2
    lane = lax.broadcasted_iota(jnp.int32, (half, values.shape[1]), 1)
    return jnp.where(lane < HDIM, values[:half], values[half:])


def block_masks(seg_ref, keys_ref, subs):
    span = 2 * WINDOW
    row = lax.broadcasted_iota(jnp.int32, (WINDOW, span), 0)
    col = lax.broadcasted_iota(jnp.int32, (WINDOW, span), 1)
    near = (col > row) & (col <= row + WINDOW)
    masks = []
    for sub in range(subs):
        first = HALO + sub * WINDOW
        same = seg_ref[0, first : first + WINDOW] == keys_ref[0, sub : sub + 1]
        masks.append(near & same)
    return jnp.concatenate([mask for mask in masks for unused in range(2)], 0)


def same_rows(seg_ref):
    seg = seg_ref[0]
    same_one = (seg == shifted_down(seg, 1)).astype(f32)
    same_two = (seg == shifted_down(seg, 2)).astype(f32)
    return same_one, same_two


def pair_probs(queries, keysets, mask, score_scale):
    scores = jnp.concatenate([contract_last(q, k) for q, k in zip(queries, keysets)], 0)
    scores = jnp.where(mask, scores * score_scale, masked_score)
    exponent = jnp.exp(scores - jnp.max(scores, axis=-1, keepdims=True))
    return exponent * (1.0 / jnp.sum(exponent, axis=-1, keepdims=True))


def cut(values, subs, first, size):
    return [values[first + s * WINDOW : first + s * WINDOW + size] for s in range(subs)]


def parts_of(values, subs):
    return jnp.split(values, subs, 0)


def place_pieces(refs, chunk, where_ref, row, target, sems):
    copies = []
    for ref in refs:
        for first in range(0, ref.shape[0] // chunk * chunk, chunk):
            spot = pl.multiple_of(where_ref[row + len(copies), 1], 16)
            copy = pltpu.make_async_copy(
                ref.at[first : first + chunk],
                target.at[where_ref[row + len(copies), 0], pl.ds(spot, chunk)],
                sems.at[row + len(copies)],
            )
            copy.start()
            copies.append(copy)
    return copies


def attend_kernel(
    where_ref,
    tokens_ref,
    gain_ref,
    taps_ref,
    seg_ref,
    keys_ref,
    *rest,
    n,
    chunk,
    subs,
    score_scale,
):
    piece_refs, (out_ref, proj_ref, weight_ref, normed_ref, sems) = rest[:n], rest[n:]

    @pl.when(pl.program_id(0) == 0)
    def fetch():
        for copy in place_pieces(piece_refs, chunk, where_ref, 0, weight_ref, sems):
            copy.wait()

    normed_ref[0] = rms_scale(tokens_ref[0].astype(f32), gain_ref[...]).astype(bf16)
    half_wide = weight_ref.shape[2]
    for half in range(2):
        proj_ref[0, :, half * half_wide : (half + 1) * half_wide] = plain(
            normed_ref[0], weight_ref[half]
        )
    pairs = 2 * half_wide // (3 * LANES)
    same_one, same_two = same_rows(seg_ref)
    mask = block_masks(seg_ref, keys_ref, subs)
    first_key = HALO - WINDOW
    for pair in range(pairs):
        mixed = []
        for kind in range(3):
            at = (kind * pairs + pair) * LANES
            conv, sig = gate_of(
                proj_ref[0, :, at : at + LANES], taps_ref[:, at : at + LANES], same_one, same_two
            )
            mixed.append((conv * sig).astype(bf16))
        queries = [by_head(q) for q in cut(mixed[0], subs, HALO, WINDOW)]
        keysets = cut(mixed[1], subs, first_key, 2 * WINDOW)
        valuesets = cut(mixed[2], subs, first_key, 2 * WINDOW)
        weights = parts_of(pair_probs(queries, keysets, mask, score_scale).astype(bf16), subs)
        for sub in range(subs):
            out_ref[0, sub * WINDOW : (sub + 1) * WINDOW, pair * LANES : (pair + 1) * LANES] = (
                join_heads(plain(weights[sub], valuesets[sub])).astype(bf16)
            )


def attend_back_kernel(
    branch_ref, out_weight_ref, proj_ref, taps_ref, seg_ref, keys_ref, out_ref, tap_ref, *, subs, score_scale
):
    @pl.when(pl.program_id(0) == 0)
    def clear():
        tap_ref[...] = jnp.zeros_like(tap_ref)

    grad_attended = contract_last(branch_ref[0], out_weight_ref[...]).astype(bf16)
    pairs = proj_ref.shape[2] // (3 * LANES)
    same_one, same_two = same_rows(seg_ref)
    mask = block_masks(seg_ref, keys_ref, subs)
    first_key = HALO - WINDOW
    for pair in range(pairs):
        values, convs, sigs, mixed = [], [], [], []
        for kind in range(3):
            at = (kind * pairs + pair) * LANES
            value = proj_ref[0, :, at : at + LANES]
            conv, sig = gate_of(value, taps_ref[:, at : at + LANES], same_one, same_two)
            values.append(value)
            convs.append(conv)
            sigs.append(sig)
            mixed.append((conv * sig).astype(bf16))
        queries = [by_head(q) for q in cut(mixed[0], subs, HALO, WINDOW)]
        keysets = cut(mixed[1], subs, first_key, 2 * WINDOW)
        valuesets = cut(mixed[2], subs, first_key, 2 * WINDOW)
        grads = [
            by_head(g)
            for g in cut(grad_attended[:, pair * LANES : (pair + 1) * LANES], subs, 0, WINDOW)
        ]
        probs = pair_probs(queries, keysets, mask, score_scale)
        grad_probs = jnp.concatenate([contract_last(g, v) for g, v in zip(grads, valuesets)], 0)
        inner = jnp.sum(probs * grad_probs, axis=-1, keepdims=True)
        grad_scores = parts_of((probs * (grad_probs - inner)).astype(bf16), subs)
        weights = parts_of(probs.astype(bf16), subs)
        grad_queries = [
            join_heads(plain(g, k)) * score_scale for g, k in zip(grad_scores, keysets)
        ]
        grad_keys = [contract_first(g, q) * score_scale for g, q in zip(grad_scores, queries)]
        grad_values = [contract_first(w, g) for w, g in zip(weights, grads)]

        def overlapped(parts):
            rows = [jnp.zeros((first_key, LANES), f32), parts[0][:WINDOW]]
            for sub in range(1, subs):
                rows.append(parts[sub - 1][WINDOW:] + parts[sub][:WINDOW])
            rows.append(parts[subs - 1][WINDOW:])
            return jnp.concatenate(rows, 0)

        grads_mixed = (
            jnp.concatenate([jnp.zeros((HALO, LANES), f32)] + grad_queries, 0),
            overlapped(grad_keys),
            overlapped(grad_values),
        )
        for kind in range(3):
            at = (kind * pairs + pair) * LANES
            taps = taps_ref[:, at : at + LANES]
            through = grads_mixed[kind] * sigs[kind]
            one = same_one * through
            two = same_two * through
            summed = (
                through * convs[kind] * (1.0 - sigs[kind])
                + taps[0:1] * through
                + taps[1:2] * shifted_up(one, 1)
                + taps[2:3] * shifted_up(two, 2)
            )
            out_ref[0, :, at : at + LANES] = summed.astype(bf16)
            value = values[kind]
            tap_ref[0:1, at : at + LANES] += jnp.sum(through * value, 0, keepdims=True)
            tap_ref[1:2, at : at + LANES] += jnp.sum(
                one * shifted_down(value, 1), 0, keepdims=True
            )
            tap_ref[2:3, at : at + LANES] += jnp.sum(
                two * shifted_down(value, 2), 0, keepdims=True
            )


def attention_specs(rows, columns, subs):
    return [
        pl.BlockSpec((3, columns), lambda b: (0, 0)),
        pl.BlockSpec((1, rows, LANES), lambda b: (b, 0, 0)),
        pl.BlockSpec((1, subs, 2 * WINDOW), lambda b: (b, 0, 0)),
    ]


def attend(where, tokens, gain, taps, seg_rows, seg_keys, pieces, chunk, score_scale):
    blocks, rows, width = tokens.shape
    columns = taps.shape[1]
    subs = seg_keys.shape[1]
    copies = sum(p.shape[0] // chunk for p in pieces)
    return pl.pallas_call(
        functools.partial(
            attend_kernel, n=len(pieces), chunk=chunk, subs=subs, score_scale=score_scale
        ),
        grid=(blocks,),
        out_shape=(
            jax.ShapeDtypeStruct((blocks, rows - HALO, columns // 3), bf16),
            jax.ShapeDtypeStruct((blocks, rows, columns), f32),
            jax.ShapeDtypeStruct((2, width, columns // 2), bf16),
            jax.ShapeDtypeStruct((blocks, rows, width), bf16),
        ),
        in_specs=[
            pl.BlockSpec(memory_space=pltpu.SMEM),
            pl.BlockSpec((1, rows, width), lambda b: (b, 0, 0)),
            pl.BlockSpec((1, width), lambda b: (0, 0)),
        ]
        + attention_specs(rows, columns, subs)
        + [pl.BlockSpec(memory_space=pl.ANY)] * len(pieces),
        out_specs=(
            pl.BlockSpec((1, rows - HALO, columns // 3), lambda b: (b, 0, 0)),
            pl.BlockSpec((1, rows, columns), lambda b: (b, 0, 0)),
            pl.BlockSpec((2, width, columns // 2), lambda b: (0, 0, 0)),
            pl.BlockSpec((1, rows, width), lambda b: (b, 0, 0)),
        ),
        scratch_shapes=[pltpu.SemaphoreType.DMA((copies,))],
        compiler_params=pltpu.CompilerParams(vmem_limit_bytes=60 * MIB),
        cost_estimate=pl.CostEstimate(
            flops=20 * 10**9, bytes_accessed=20 * 10**6, transcendentals=0
        ),
        name="attend",
    )(where, tokens, gain, taps, seg_rows, seg_keys, *pieces)


def attend_back(branch, out_weight, projected, taps, seg_rows, seg_keys, score_scale):
    blocks, rows, columns = projected.shape
    width = branch.shape[2]
    subs = seg_keys.shape[1]
    return pl.pallas_call(
        functools.partial(attend_back_kernel, subs=subs, score_scale=score_scale),
        grid=(blocks,),
        out_shape=(
            jax.ShapeDtypeStruct((blocks, rows, columns), bf16),
            jax.ShapeDtypeStruct((8, columns), f32),
        ),
        in_specs=[
            pl.BlockSpec((1, rows - HALO, width), lambda b: (b, 0, 0)),
            pl.BlockSpec((columns // 3, width), lambda b: (0, 0)),
            pl.BlockSpec((1, rows, columns), lambda b: (b, 0, 0)),
        ]
        + attention_specs(rows, columns, subs),
        out_specs=(
            pl.BlockSpec((1, rows, columns), lambda b: (b, 0, 0)),
            pl.BlockSpec((8, columns), lambda b: (0, 0)),
        ),
        compiler_params=pltpu.CompilerParams(vmem_limit_bytes=60 * MIB),
        cost_estimate=pl.CostEstimate(
            flops=20 * 10**9, bytes_accessed=20 * 10**6, transcendentals=0
        ),
        name="attend_back",
    )(branch, out_weight, projected, taps, seg_rows, seg_keys)


def dense_kernel(where_ref, dense_ref, gate_hbm, hidden_ref, inner_ref, gate_ref, sems, *, chunk):
    for copy in place_pieces([gate_hbm], chunk, where_ref, 0, gate_ref, sems):
        copy.wait()
    rows, hidden_wide = hidden_ref.shape

    @pl.loop(0, rows // TILE)
    def block(index):
        own = pl.ds(pl.multiple_of(index * TILE, TILE), TILE)
        normed = dense_ref[own, :]
        for first in range(0, hidden_wide, TILE):
            unit = slice(first, first + TILE)
            gate = plain(normed, gate_ref[0, :, unit])
            up = plain(normed, gate_ref[1, :, unit])
            sig = jax.nn.sigmoid(gate)
            silu = gate * sig
            hidden_ref[own, unit] = (silu * up).astype(bf16)
            inner_ref[0, own, unit] = up * (sig * (1.0 + gate * (1.0 - sig)))
            inner_ref[1, own, unit] = silu


def dense_back_kernel(
    where_ref,
    cotangent_ref,
    inner_hbm,
    gate_hbm,
    down_hbm,
    grad_ref,
    joined_ref,
    down_ref,
    inner_ref,
    gate_ref,
    sems,
    *,
    gate_chunk,
    down_chunk,
):
    rows, width = cotangent_ref.shape
    hidden_wide = joined_ref.shape[2]
    half_width = width // 2
    count = down_hbm.shape[0] // down_chunk
    down_copies = place_pieces([down_hbm], down_chunk, where_ref, 0, down_ref, sems)
    inner_copies = []
    for index in range(rows // TILE):
        own = slice(index * TILE, (index + 1) * TILE)
        copy = pltpu.make_async_copy(
            inner_hbm.at[:, own], inner_ref.at[:, own], sems.at[count + index]
        )
        copy.start()
        inner_copies.append(copy)
    gate_copies = place_pieces(
        [gate_hbm], gate_chunk, where_ref, count + rows // TILE, gate_ref, sems
    )
    real = down_hbm.shape[0] // 2
    if real < hidden_wide:
        down_ref[:, real:] = jnp.zeros((2, hidden_wide - real, half_width), bf16)
    for copy in down_copies:
        copy.wait()
    for index in range(rows // TILE):
        inner_copies[index].wait()
        own = slice(index * TILE, (index + 1) * TILE)
        left = cotangent_ref[own, :half_width]
        right = cotangent_ref[own, half_width:]
        for first in range(0, hidden_wide, TILE):
            unit = slice(first, first + TILE)
            grad = contract_last(left, down_ref[0, unit]) + contract_last(right, down_ref[1, unit])
            joined_ref[0, own, unit] = (grad * inner_ref[0, own, unit]).astype(bf16)
            joined_ref[1, own, unit] = (grad * inner_ref[1, own, unit]).astype(bf16)
    for copy in gate_copies:
        copy.wait()

    @pl.loop(0, rows // TILE)
    def block(index):
        own = pl.ds(pl.multiple_of(index * TILE, TILE), TILE)
        gates = joined_ref[0, own, :]
        ups = joined_ref[1, own, :]
        for first in range(0, width, TILE):
            unit = slice(first, first + TILE)
            grad_ref[own, unit] = (
                contract_last(gates, gate_ref[0, unit]) + contract_last(ups, gate_ref[1, unit])
            ).astype(bf16)


def dense_out_kernel(where_ref, hidden_ref, down_hbm, out_ref, down_ref, sems, *, chunk):
    copies = place_pieces([down_hbm], chunk, where_ref, 0, down_ref, sems)
    real = down_hbm.shape[0] // 2
    if real < down_ref.shape[1]:
        down_ref[:, real:] = jnp.zeros((2, down_ref.shape[1] - real, down_ref.shape[2]), bf16)
    for copy in copies:
        copy.wait()
    half_width = down_ref.shape[2]

    @pl.loop(0, hidden_ref.shape[0] // TILE)
    def block(index):
        own = pl.ds(pl.multiple_of(index * TILE, TILE), TILE)
        for half in range(2):
            out_ref[own, half * half_width : (half + 1) * half_width] = plain(
                hidden_ref[own, :], down_ref[half]
            ).astype(bf16)


WHOLE = pl.BlockSpec(memory_space=pltpu.VMEM)
OUTSIDE = pl.BlockSpec(memory_space=pl.ANY)
SCALARS = pl.BlockSpec(memory_space=pltpu.SMEM)


def kernel_params(giga_flops):
    return dict(
        compiler_params=pltpu.CompilerParams(vmem_limit_bytes=60 * MIB),
        cost_estimate=pl.CostEstimate(
            flops=giga_flops * 10**9, bytes_accessed=20 * 10**6, transcendentals=0
        ),
    )


def dense(where, normed, gate, chunk):
    rows, width = normed.shape
    hidden_wide = gate.shape[1]
    return pl.pallas_call(
        functools.partial(dense_kernel, chunk=chunk),
        out_shape=(
            jax.ShapeDtypeStruct((rows, hidden_wide), bf16),
            jax.ShapeDtypeStruct((2, rows, hidden_wide), f32),
        ),
        in_specs=[SCALARS, WHOLE, OUTSIDE],
        out_specs=(WHOLE, WHOLE),
        scratch_shapes=[
            pltpu.VMEM((2, width, hidden_wide), bf16),
            pltpu.SemaphoreType.DMA((gate.shape[0] // chunk,)),
        ],
        name="dense",
        **kernel_params(15),
    )(where, normed, gate)


def dense_back(where, cotangent, inner, gate, gate_chunk, down, down_chunk):
    rows, width = cotangent.shape
    hidden_wide = gate.shape[1]
    copies = down.shape[0] // down_chunk + rows // TILE + gate.shape[0] // gate_chunk
    return pl.pallas_call(
        functools.partial(dense_back_kernel, gate_chunk=gate_chunk, down_chunk=down_chunk),
        out_shape=(
            jax.ShapeDtypeStruct((rows, width), bf16),
            jax.ShapeDtypeStruct((2, rows, hidden_wide), bf16),
        ),
        in_specs=[SCALARS, WHOLE, OUTSIDE, OUTSIDE, OUTSIDE],
        out_specs=(WHOLE, WHOLE),
        scratch_shapes=[
            pltpu.VMEM((2, hidden_wide, width // 2), bf16),
            pltpu.VMEM((2, rows, hidden_wide), f32),
            pltpu.VMEM((2, width, hidden_wide), bf16),
            pltpu.SemaphoreType.DMA((copies,)),
        ],
        name="dense_back",
        **kernel_params(20),
    )(where, cotangent, inner, gate, down)


def dense_out(where, hidden, down, chunk):
    rows, hidden_wide = hidden.shape
    half_width = down.shape[1]
    return pl.pallas_call(
        functools.partial(dense_out_kernel, chunk=chunk),
        out_shape=jax.ShapeDtypeStruct((rows, 2 * half_width), bf16),
        in_specs=[SCALARS, WHOLE, OUTSIDE],
        out_specs=WHOLE,
        scratch_shapes=[
            pltpu.VMEM((2, hidden_wide, half_width), bf16),
            pltpu.SemaphoreType.DMA((down.shape[0] // chunk,)),
        ],
        name="dense_out",
        **kernel_params(8),
    )(where, hidden, down)


def normed_grad_kernel(grad_ref, weight_ref, out_ref, halo_ref):
    half_wide = weight_ref.shape[2]
    grads = grad_ref[0]
    product = (
        contract_last(grads[:, :half_wide], weight_ref[0])
        + contract_last(grads[:, half_wide:], weight_ref[1])
    ).astype(bf16)
    halo_ref[0] = product[:HALO]
    out_ref[0] = product[HALO:]


def normed_grad(grad_projected, weight):
    blocks, rows, columns = grad_projected.shape
    width = weight.shape[1]
    return pl.pallas_call(
        normed_grad_kernel,
        grid=(blocks,),
        out_shape=(
            jax.ShapeDtypeStruct((blocks, rows - HALO, width), bf16),
            jax.ShapeDtypeStruct((blocks, HALO, width), bf16),
        ),
        in_specs=[
            pl.BlockSpec((1, rows, columns), lambda b: (b, 0, 0)),
            pl.BlockSpec((2, width, columns // 2), lambda b: (0, 0, 0)),
        ],
        out_specs=(
            pl.BlockSpec((1, rows - HALO, width), lambda b: (b, 0, 0)),
            pl.BlockSpec((1, HALO, width), lambda b: (b, 0, 0)),
        ),
        name="normed_grad",
        **kernel_params(15),
    )(grad_projected, weight)


def weight_grad_kernel(left_ref, right_ref, out_ref):
    right = right_ref[...].reshape(right_ref.shape[-2:])
    product = contract_first(left_ref[...], right).astype(bf16)
    planes, unused, rows, columns = out_ref.shape
    out_ref[:, 0] = product[: planes * rows].reshape(planes, rows, columns)


def weight_grad(left, right, planes, rows, name):
    tokens, depth = left.shape
    columns = right.shape[-1] if right.ndim == 3 else right.shape[-1] // 2
    steps = 2 if planes * rows == depth else 1
    if right.ndim == 3:
        right_spec = pl.BlockSpec((1, tokens, columns), lambda h, k: (h, 0, 0))
    else:
        right_spec = pl.BlockSpec((tokens, columns), lambda h, k: (0, h))
    return pl.pallas_call(
        weight_grad_kernel,
        grid=(2, steps),
        out_shape=jax.ShapeDtypeStruct((planes, 2, rows, columns), bf16),
        in_specs=[pl.BlockSpec((tokens, depth // steps), lambda h, k: (0, k)), right_spec],
        out_specs=pl.BlockSpec((planes // steps, 1, rows, columns), lambda h, k: (k, h, 0, 0)),
        compiler_params=pltpu.CompilerParams(vmem_limit_bytes=60 * MIB),
        cost_estimate=pl.CostEstimate(
            flops=20 * 10**9, bytes_accessed=20 * 10**6, transcendentals=0
        ),
        name=name,
    )(left, right)


def fence(*values):
    return lax.optimization_barrier(values)


def layer(
    planes,
    tokens,
    segments,
    cotangent,
    mixer_gain,
    qkv_weight,
    conv_taps,
    out_weight,
    dense_gain,
    gateup_weight,
    down_weight,
):
    count = planes * PLANE
    rows, width = tokens.shape
    ext = HALO + rows
    subs = rows // WINDOW
    quarter = width // 4
    padded = -(-quarter // LANES) * LANES
    half_wide = 3 * padded // 2
    half_width = width // 2
    shard_rows = qkv_weight.shape[0]
    down_rows = down_weight.shape[0]
    square_rows = 4 * shard_rows
    octet_rows = PLANE * shard_rows
    hidden_width = down_rows * count
    hidden_part = hidden_width // 4
    hidden_wide = -(-hidden_part // 256) * 256
    tap_columns = conv_taps.shape[1]
    out_planes = planes // 4
    z = lax.axis_index("z")
    y = lax.axis_index("y")
    x = lax.axis_index("x")
    c = lax.axis_index("core")
    part = 2 * y + x
    score_scale = 1.0 / math.sqrt(HDIM)

    def swap(array, axes):
        return lax.all_to_all(array, axes, 0, 0)

    def flip(array, axis):
        return lax.ppermute(array, axis, [(0, 1), (1, 0)])

    def in_order(own, other, bit):
        return jnp.where(bit == 0, own, other), jnp.where(bit == 0, other, own)

    def absolute(pieces):
        whole = jnp.zeros((planes,) + pieces[0].shape, pieces[0].dtype)
        for step, piece in enumerate(pieces):
            first = ((z + step) % planes,) + (0,) * piece.ndim
            whole = lax.dynamic_update_slice(whole, piece[None], first)
        return whole

    def gather_rows(array, axes):
        return swap(jnp.broadcast_to(array, (4,) + array.shape), axes)

    def rows_at(bits, size):
        return jnp.stack([jnp.asarray(b, jnp.int32) for b in bits]).reshape(-1, size)

    qkv_slices = qkv_weight.reshape(shard_rows, 3, 4, quarter)
    qkv_slices = jnp.pad(qkv_slices, ((0, 0), (0, 0), (0, 0), (0, padded - quarter)))
    qkv_slices = qkv_slices.transpose(2, 0, 1, 3).reshape(4, shard_rows, 2, half_wide)
    qkv_slices = qkv_slices.transpose(0, 2, 1, 3).reshape(PLANE, shard_rows, half_wide)
    owned = jnp.concatenate([mixer_gain, dense_gain, conv_taps.reshape(-1)])
    owned_size = owned.shape[0]
    owned = jnp.pad(owned.reshape(1, -1), ((0, 1), (0, half_wide - owned_size)))
    owned = jnp.broadcast_to(owned, (PLANE, 2, half_wide))
    qkv_slices, gateup_weight, down_weight, out_weight = fence(
        jnp.concatenate([qkv_slices, owned], 1), gateup_weight, down_weight, out_weight
    )

    before = lax.ppermute(tokens[rows - HALO :], ALL, [(d, d + 1) for d in range(count - 1)])

    qkv_piece = swap(qkv_slices, OCTET)
    gateup_slices = gateup_weight.reshape(shard_rows, 2, planes, 4, hidden_part // planes)
    gateup_slices = gateup_slices.transpose(3, 1, 0, 2, 4)
    gateup_slices = gateup_slices.reshape(PLANE, shard_rows, hidden_part)
    gateup_slices = jnp.pad(gateup_slices, ((0, 0), (0, 0), (0, hidden_wide - hidden_part)))
    down_kept, down_sent = in_order(down_weight[:, :half_width], down_weight[:, half_width:], c)
    down_piece = jnp.concatenate(in_order(down_kept, flip(down_sent, "core"), c), 0)
    out_halves = out_weight.reshape(shard_rows, 2, half_width).transpose(1, 0, 2)
    qkv_piece, gateup_slices, down_piece, out_halves, tokens_now, before = fence(
        qkv_piece, gateup_slices, down_piece, out_halves, tokens, before
    )
    small = [qkv_piece[:, shard_rows, :owned_size]]
    qkv_piece, small[0] = fence(qkv_piece[:, :shard_rows].reshape(octet_rows, half_wide), small[0])

    qkv_pieces, qkv_others, out_rows = [qkv_piece], [], [out_halves]
    onward = [(i, (i - 1) % planes) for i in range(planes)]
    for step in range(1, planes):
        qkv_next = lax.ppermute(qkv_pieces[-1], "z", onward)
        if step == 1:
            gateup_piece = swap(gateup_slices, OCTET).reshape(octet_rows, hidden_wide)
            for by in range(1, planes):
                shift = [(i, (i - by) % planes) for i in range(planes)]
                small.append(lax.ppermute(small[0], "z", shift))
            qkv_next, gateup_piece, tokens_now, small = fence(
                qkv_next, gateup_piece, tokens_now, small
            )
            token_group = gather_rows(jnp.concatenate([before, tokens_now]), SQUARE)
        elif step < planes - 1:
            for unused in range(2 if step == 2 else 1):
                out_rows.append(lax.ppermute(out_rows[-1], "z", onward))
            qkv_next, out_rows = fence(qkv_next, out_rows)
        else:
            out_rows.append(lax.ppermute(out_rows[-1], "z", onward))
            out_slices = absolute(out_rows)
            out_slices = out_slices.reshape(4, out_planes, 2, shard_rows, half_width)
            out_slices = out_slices.transpose(0, 2, 1, 3, 4)
            out_slices = out_slices.reshape(PLANE, out_planes, shard_rows, half_width)
            small = absolute(small).astype(f32)
            gain_one = small[:, :, :shard_rows].reshape(1, width)
            gain_two = small[:, :, shard_rows : 2 * shard_rows].reshape(width)
            taps = small[:, :, 2 * shard_rows :].reshape(count, 3, tap_columns).transpose(1, 0, 2)
            taps = taps.reshape(3, 3, 4, quarter)
            taps = lax.dynamic_index_in_dim(taps, part, 2, keepdims=False)
            taps = jnp.pad(taps, ((0, 0), (0, 0), (0, padded - quarter)))
            taps = taps.reshape(3, 3 * padded)
            out = fence(qkv_next, out_slices, token_group, gateup_piece, gain_one, gain_two, taps)
            qkv_next, out_slices, token_group, gateup_piece, gain_one, gain_two, taps = out
        qkv_others.append(flip(qkv_pieces[-1], "core"))
        qkv_pieces.append(qkv_next)
    qkv_pieces, qkv_others, down_piece, cotangent_now = fence(
        qkv_pieces, qkv_others, down_piece, cotangent
    )
    gateup_all = lax.all_gather(gateup_piece, LINE)
    down_all = lax.all_gather(down_piece, LINE)
    qkv_others.append(flip(qkv_pieces[-1], "core"))
    out_piece = swap(out_slices, OCTET)
    out_piece = out_piece.transpose(1, 0, 2, 3).reshape(quarter, half_width)
    cotangent_now = jnp.broadcast_to(cotangent_now, (4,) + cotangent.shape)
    qkv_others, out_piece, cotangent_now = fence(qkv_others, out_piece, cotangent_now)

    padded_segments = jnp.concatenate([jnp.full((HALO,), -1, jnp.int32), segments])
    seg_rows = jnp.stack(
        [
            lax.dynamic_slice_in_dim(padded_segments, (PLANE * z + 2 * b + c) * rows, ext)
            for b in range(4)
        ]
    )
    seg_keys = jnp.stack(
        [
            seg_rows[:, HALO - WINDOW + s * WINDOW : HALO + WINDOW + s * WINDOW]
            for s in range(subs)
        ],
        1,
    )
    seg_rows = jnp.broadcast_to(seg_rows[:, :, None], (4, ext, LANES))

    cotangent_group = swap(cotangent_now, SQUARE).reshape(4 * rows, width)
    out_other = flip(out_piece, "core")
    where_qkv = []
    for own in range(2):
        for step in range(planes):
            where_qkv += [c ^ own, (z + step) % planes * octet_rows]
    attended, projected, qkv_full, normed_group = attend(
        rows_at(where_qkv, 2),
        token_group,
        gain_one,
        taps,
        seg_rows,
        seg_keys,
        qkv_pieces + qkv_others,
        octet_rows,
        score_scale,
    )
    attended = attended.reshape(4 * rows, padded)
    attended, normed_group, cotangent_group, out_other = fence(
        attended, normed_group, cotangent_group, out_other
    )
    out_full = jnp.concatenate(in_order(out_piece, out_other, c), 1)
    out_full = jnp.pad(out_full, ((0, padded - quarter), (0, 0)))
    mixer_out = plain(attended, out_full).astype(bf16).reshape(4, rows, width)

    mixer_sum = swap(mixer_out, SQUARE)
    own_tokens = tokens.astype(f32)
    residual = own_tokens + jnp.sum(mixer_sum.astype(f32), 0)
    normed_dense = rms_scale(residual, gain_two).astype(bf16)
    dense_group = gather_rows(normed_dense, SQUARE).reshape(4 * rows, width)

    gateup_chunk, down_chunk = octet_rows, 2 * down_rows
    where_gateup = [k for i in range(planes) for h in range(2) for k in (h, i * gateup_chunk)]
    where_down = [k for i in range(planes) for h in range(2) for k in (h, i * down_chunk)]
    if down_chunk % 16:
        down_chunk, where_down = hidden_part, [0, 0, 1, 0]
        down_all = down_all.reshape(planes, 2, -1, half_width).transpose(1, 0, 2, 3)
    where_back = where_down + [0, 0] * (4 * rows // TILE) + where_gateup
    gateup_all = gateup_all.reshape(-1, hidden_wide)
    down_all = down_all.reshape(-1, half_width)
    where_gateup = rows_at(where_gateup, 2)
    where_down = rows_at(where_down, 2)
    hidden, inner = dense(where_gateup, dense_group, gateup_all, gateup_chunk)
    hidden, inner, cotangent_group = fence(hidden, inner, cotangent_group)
    if down_chunk % 16 or 2 * down_rows % 16:
        down_grad = contract_first(hidden, cotangent_group)[:hidden_part].astype(bf16)
        down_grad = down_grad.reshape(planes, 2 * down_rows, 2, half_width).transpose(0, 2, 1, 3)
    else:
        down_grad = weight_grad(hidden, cotangent_group, planes, 2 * down_rows, "down_grad")
    inner, cotangent_group, down_grad, hidden = fence(inner, cotangent_group, down_grad, hidden)
    grad_dense, grad_inner = fence(
        *dense_back(
            rows_at(where_back, 2),
            cotangent_group,
            inner,
            gateup_all,
            gateup_chunk,
            down_all,
            down_chunk,
        )
    )

    def by_core(halves):
        return (jnp.where(c == 0, halves[0], halves[1]), jnp.where(c == 0, halves[1], halves[0]))

    def core_pair(left_side, halves):
        own, other = by_core(halves)
        other = contract_first(left_side, other).astype(bf16)
        return contract_first(left_side, own), other

    def scatter_line(array):
        return lax.psum_scatter(
            array.reshape((2 * planes,) + array.shape[2:]), LINE, scatter_dimension=0
        )

    down_mine = scatter_line(down_grad)
    grad_dense = swap(grad_dense.reshape(4, rows, width), SQUARE)
    gateup_grad = weight_grad(dense_group, grad_inner, planes, octet_rows, "gateup_grad")
    grad_dense, gateup_grad, hidden, down_all = fence(grad_dense, gateup_grad, hidden, down_all)
    gateup_mine = scatter_line(gateup_grad)

    unused, rms_back = jax.vjp(rms_scale, residual, gain_two)
    grad_residual, dense_gain_sum = rms_back(jnp.sum(grad_dense.astype(f32), 0))
    grad_residual = grad_residual + cotangent.astype(f32)
    grad_branch = gather_rows(grad_residual.astype(bf16), SQUARE)
    dense_rows = dense_out(where_down, hidden, down_all, down_chunk).reshape(4, rows, width)
    grad_branch, out_full, dense_rows, down_mine = fence(
        grad_branch, out_full, dense_rows, down_mine
    )
    dense_sum = swap(dense_rows, SQUARE)

    grad_projected, grad_taps = attend_back(
        grad_branch, out_full, projected, taps, seg_rows, seg_keys, score_scale
    )
    grad_projected = grad_projected.reshape(4 * ext, 3 * padded)
    normed_rows = normed_group.reshape(4 * ext, width)
    qkv_grad = weight_grad(normed_rows, grad_projected, planes, octet_rows, "qkv_grad")
    qkv_grad, dense_sum, grad_projected, grad_branch, attended = fence(
        qkv_grad, dense_sum, grad_projected, grad_branch, attended
    )
    qkv_part = scatter_line(qkv_grad)

    grad_normed, grad_halo = normed_grad(grad_projected.reshape(4, ext, 3 * padded), qkv_full)
    halo_sum = swap(grad_halo, SQUARE)
    grad_branch = grad_branch.reshape(4 * rows, width)
    out_own, out_other = core_pair(
        attended, (grad_branch[:, :half_width], grad_branch[:, half_width:])
    )
    out_grad = (out_own + flip(out_other, "core").astype(f32)).astype(bf16)
    out_mine = out_grad[:quarter].reshape(out_planes, PLANE, shard_rows, half_width)
    out_mine = out_mine.transpose(1, 0, 2, 3).reshape(PLANE, -1, half_width)
    grad_normed, halo_sum, out_mine = fence(grad_normed, halo_sum, out_mine)

    normed_sum = swap(grad_normed, SQUARE)
    late = jnp.sum(halo_sum.astype(f32), 0).astype(bf16)
    late = lax.ppermute(late, ALL, [(d, d - 1) for d in range(1, count)])
    layer_out = (residual + jnp.sum(dense_sum.astype(f32), 0)).astype(bf16)
    normed_sum, late, gateup_mine, layer_out = fence(normed_sum, late, gateup_mine, layer_out)

    gateup_mine = swap(gateup_mine.reshape(PLANE, shard_rows, hidden_wide), OCTET)
    grad_normed = jnp.sum(normed_sum.astype(f32), 0)
    grad_normed = grad_normed + jnp.pad(late.astype(f32), ((rows - HALO, 0), (0, 0)))
    unused, mixer_back = jax.vjp(rms_scale, own_tokens, gain_one.reshape(width))
    grad_rows, mixer_gain_sum = mixer_back(grad_normed)
    input_grad = grad_residual + grad_rows

    grad_taps = grad_taps[:3].reshape(3, 3, 1, padded)[..., :quarter]
    grad_taps = lax.dynamic_update_slice(
        jnp.zeros((3, 3, 4, quarter), f32), grad_taps, (0, 0, part, 0)
    )
    grad_taps = grad_taps.reshape(3, count, tap_columns).transpose(1, 0, 2)
    sums = jnp.concatenate(
        [
            mixer_gain_sum.reshape(count, shard_rows),
            dense_gain_sum.reshape(count, shard_rows),
            grad_taps.reshape(count, 3 * tap_columns),
        ],
        1,
    )
    sums = sums.reshape(planes, PLANE, owned_size).transpose(1, 0, 2).reshape(PLANE, -1)
    sum_rows = -(-planes * owned_size // half_width)
    sums = jnp.pad(sums, ((0, 0), (0, sum_rows * half_width - planes * owned_size)))
    sums = sums.reshape(PLANE, sum_rows, half_width).astype(bf16)
    out_mine = jnp.concatenate([out_mine, sums], 1)
    gateup_mine, out_mine, qkv_part, input_grad = fence(
        gateup_mine, out_mine, qkv_part, input_grad
    )

    qkv_mine = swap(qkv_part.reshape(PLANE, shard_rows, half_wide), OCTET)
    gateup_mine = gateup_mine[:, :, :hidden_part]
    gateup_mine = gateup_mine.reshape(4, 2, shard_rows, planes, hidden_part // planes)
    gateup_mine = gateup_mine.transpose(2, 1, 3, 0, 4).reshape(shard_rows, 2 * hidden_width)
    gateup_mine = gateup_mine.astype(f32)
    down_kept, down_sent = in_order(down_mine[:down_rows], down_mine[down_rows:], c)
    down_mine = jnp.concatenate(in_order(down_kept, flip(down_sent, "core"), c), 1).astype(f32)
    qkv_mine, out_mine, gateup_mine, down_mine = fence(qkv_mine, out_mine, gateup_mine, down_mine)
    out_mine = swap(out_mine, OCTET)
    sums = out_mine[:, out_planes * shard_rows :].astype(f32).reshape(PLANE, -1)
    sums = jnp.sum(sums, 0)[: planes * owned_size].reshape(planes, 1, owned_size)
    sums = jnp.pad(sums, ((0, 0), (0, 0), (0, width - owned_size))).astype(bf16)
    out_mine = out_mine[:, : out_planes * shard_rows]
    out_mine = out_mine.reshape(4, 2, out_planes, shard_rows, half_width)
    out_mine = out_mine.transpose(0, 2, 3, 1, 4).reshape(planes, shard_rows, width)
    out_mine = swap(jnp.concatenate([out_mine, sums], 1), "z")
    out_mine = jnp.sum(out_mine.astype(f32), 0)
    sums = out_mine[shard_rows, :owned_size]
    qkv_mine = qkv_mine.reshape(4, 2, shard_rows, half_wide).transpose(2, 0, 1, 3)
    qkv_mine = qkv_mine.reshape(shard_rows, 4, 3, padded)[..., :quarter].transpose(0, 2, 1, 3)
    qkv_mine = qkv_mine.reshape(shard_rows, 3 * width).astype(f32)
    return (
        layer_out,
        input_grad,
        sums[:shard_rows],
        qkv_mine,
        sums[2 * shard_rows :].reshape(3, tap_columns),
        out_mine[:shard_rows],
        sums[shard_rows : 2 * shard_rows],
        gateup_mine,
        down_mine,
    )


def solution(mesh):
    planes = mesh.devices.size // PLANE
    split = Mesh(mesh.devices.reshape(planes, 2, 2, 2), ALL)
    over_rows = P(ALL, None)
    over_columns = P(None, ALL)
    return jax.shard_map(
        functools.partial(layer, planes),
        mesh=split,
        in_specs=(
            over_rows,
            P(),
            over_rows,
            P(ALL),
            over_rows,
            over_columns,
            over_rows,
            P(ALL),
            over_rows,
            over_rows,
        ),
        out_specs=(
            over_rows,
            over_rows,
            P(ALL),
            over_rows,
            over_columns,
            over_rows,
            P(ALL),
            over_rows,
            over_rows,
        ),
        check_vma=False,
    )
```

```python
import functools
import math

import jax
import jax.numpy as jnp
from jax import lax
from jax.experimental import pallas as pl
from jax.experimental.pallas import tpu as pltpu
from jax.sharding import Mesh, PartitionSpec as P

HDIM = 64
WINDOW = 64
HALO = 80
LANES = 128
PLANE = 8

eps_norm = 1e-05
masked_score = -1e30
bf16 = jnp.bfloat16
f32 = jnp.float32
MIB = 1024 * 1024
TILE = 256
ALL = ("z", "y", "x", "core")
SQUARE = ("y", "x")
OCTET = ("y", "x", "core")
LINE = ("z", "core")


def rms_scale(values, gains):
    inverse = lax.rsqrt(jnp.mean(values * values, axis=-1, keepdims=True) + eps_norm)
    return values * inverse * gains


def contract_last(left_side, right_side):
    return lax.dot_general(
        left_side, right_side, (((1,), (1,)), ((), ())), preferred_element_type=f32
    )


def contract_first(left_side, right_side):
    return lax.dot_general(
        left_side, right_side, (((0,), (0,)), ((), ())), preferred_element_type=f32
    )


def plain(left_side, right_side):
    return jnp.dot(left_side, right_side, preferred_element_type=f32)


def shifted_down(values, by):
    return pltpu.roll(values, by, 0)


def shifted_up(values, by):
    return pltpu.roll(values, values.shape[0] - by, 0)


def gate_of(values, taps, same_one, same_two):
    conv = (
        taps[0:1] * values
        + taps[1:2] * (same_one * shifted_down(values, 1))
        + taps[2:3] * (same_two * shifted_down(values, 2))
    )
    return conv, jax.nn.sigmoid(values)


def by_head(values):
    lane = lax.broadcasted_iota(jnp.int32, values.shape, 1)
    zero = jnp.zeros_like(values)
    return jnp.concatenate(
        [jnp.where(lane < HDIM, values, zero), jnp.where(lane < HDIM, zero, values)], 0
    )


def join_heads(values):
    half = values.shape[0] // 2
    lane = lax.broadcasted_iota(jnp.int32, (half, values.shape[1]), 1)
    return jnp.where(lane < HDIM, values[:half], values[half:])


def block_masks(seg_ref, keys_ref, subs):
    span = 2 * WINDOW
    row = lax.broadcasted_iota(jnp.int32, (WINDOW, span), 0)
    col = lax.broadcasted_iota(jnp.int32, (WINDOW, span), 1)
    near = (col > row) & (col <= row + WINDOW)
    masks = []
    for sub in range(subs):
        first = HALO + sub * WINDOW
        same = seg_ref[0, first : first + WINDOW] == keys_ref[0, sub : sub + 1]
        masks.append(near & same)
    return jnp.concatenate([mask for mask in masks for unused in range(2)], 0)


def same_rows(seg_ref):
    seg = seg_ref[0]
    same_one = (seg == shifted_down(seg, 1)).astype(f32)
    same_two = (seg == shifted_down(seg, 2)).astype(f32)
    return same_one, same_two


def pair_probs(queries, keysets, mask, score_scale):
    scores = jnp.concatenate([contract_last(q, k) for q, k in zip(queries, keysets)], 0)
    scores = jnp.where(mask, scores * score_scale, masked_score)
    exponent = jnp.exp(scores - jnp.max(scores, axis=-1, keepdims=True))
    return exponent * (1.0 / jnp.sum(exponent, axis=-1, keepdims=True))


def cut(values, subs, first, size):
    return [values[first + s * WINDOW : first + s * WINDOW + size] for s in range(subs)]


def parts_of(values, subs):
    return jnp.split(values, subs, 0)


def place_pieces(refs, chunk, where_ref, row, target, sems):
    copies = []
    for ref in refs:
        for first in range(0, ref.shape[0] // chunk * chunk, chunk):
            spot = pl.multiple_of(where_ref[row + len(copies), 1], 16)
            copy = pltpu.make_async_copy(
                ref.at[first : first + chunk],
                target.at[where_ref[row + len(copies), 0], pl.ds(spot, chunk)],
                sems.at[row + len(copies)],
            )
            copy.start()
            copies.append(copy)
    return copies


def attend_kernel(
    where_ref,
    tokens_ref,
    gain_ref,
    taps_ref,
    seg_ref,
    keys_ref,
    *rest,
    n,
    chunk,
    subs,
    score_scale,
):
    piece_refs, (out_ref, proj_ref, weight_ref, normed_ref, sems) = rest[:n], rest[n:]

    @pl.when(pl.program_id(0) == 0)
    def fetch():
        for copy in place_pieces(piece_refs, chunk, where_ref, 0, weight_ref, sems):
            copy.wait()

    normed_ref[0] = rms_scale(tokens_ref[0].astype(f32), gain_ref[...]).astype(bf16)
    half_wide = weight_ref.shape[2]
    for half in range(2):
        proj_ref[0, :, half * half_wide : (half + 1) * half_wide] = plain(
            normed_ref[0], weight_ref[half]
        )
    pairs = 2 * half_wide // (3 * LANES)
    same_one, same_two = same_rows(seg_ref)
    mask = block_masks(seg_ref, keys_ref, subs)
    first_key = HALO - WINDOW
    for pair in range(pairs):
        mixed = []
        for kind in range(3):
            at = (kind * pairs + pair) * LANES
            conv, sig = gate_of(
                proj_ref[0, :, at : at + LANES], taps_ref[:, at : at + LANES], same_one, same_two
            )
            mixed.append((conv * sig).astype(bf16))
        queries = [by_head(q) for q in cut(mixed[0], subs, HALO, WINDOW)]
        keysets = cut(mixed[1], subs, first_key, 2 * WINDOW)
        valuesets = cut(mixed[2], subs, first_key, 2 * WINDOW)
        weights = parts_of(pair_probs(queries, keysets, mask, score_scale).astype(bf16), subs)
        for sub in range(subs):
            out_ref[0, sub * WINDOW : (sub + 1) * WINDOW, pair * LANES : (pair + 1) * LANES] = (
                join_heads(plain(weights[sub], valuesets[sub])).astype(bf16)
            )


def attend_back_kernel(
    branch_ref, out_weight_ref, proj_ref, taps_ref, seg_ref, keys_ref, out_ref, tap_ref, *, subs, score_scale
):
    @pl.when(pl.program_id(0) == 0)
    def clear():
        tap_ref[...] = jnp.zeros_like(tap_ref)

    grad_attended = contract_last(branch_ref[0], out_weight_ref[...]).astype(bf16)
    pairs = proj_ref.shape[2] // (3 * LANES)
    same_one, same_two = same_rows(seg_ref)
    mask = block_masks(seg_ref, keys_ref, subs)
    first_key = HALO - WINDOW
    for pair in range(pairs):
        values, convs, sigs, mixed = [], [], [], []
        for kind in range(3):
            at = (kind * pairs + pair) * LANES
            value = proj_ref[0, :, at : at + LANES]
            conv, sig = gate_of(value, taps_ref[:, at : at + LANES], same_one, same_two)
            values.append(value)
            convs.append(conv)
            sigs.append(sig)
            mixed.append((conv * sig).astype(bf16))
        queries = [by_head(q) for q in cut(mixed[0], subs, HALO, WINDOW)]
        keysets = cut(mixed[1], subs, first_key, 2 * WINDOW)
        valuesets = cut(mixed[2], subs, first_key, 2 * WINDOW)
        grads = [
            by_head(g)
            for g in cut(grad_attended[:, pair * LANES : (pair + 1) * LANES], subs, 0, WINDOW)
        ]
        probs = pair_probs(queries, keysets, mask, score_scale)
        grad_probs = jnp.concatenate([contract_last(g, v) for g, v in zip(grads, valuesets)], 0)
        inner = jnp.sum(probs * grad_probs, axis=-1, keepdims=True)
        grad_scores = parts_of((probs * (grad_probs - inner)).astype(bf16), subs)
        weights = parts_of(probs.astype(bf16), subs)
        grad_queries = [
            join_heads(plain(g, k)) * score_scale for g, k in zip(grad_scores, keysets)
        ]
        grad_keys = [contract_first(g, q) * score_scale for g, q in zip(grad_scores, queries)]
        grad_values = [contract_first(w, g) for w, g in zip(weights, grads)]

        def overlapped(parts):
            rows = [jnp.zeros((first_key, LANES), f32), parts[0][:WINDOW]]
            for sub in range(1, subs):
                rows.append(parts[sub - 1][WINDOW:] + parts[sub][:WINDOW])
            rows.append(parts[subs - 1][WINDOW:])
            return jnp.concatenate(rows, 0)

        grads_mixed = (
            jnp.concatenate([jnp.zeros((HALO, LANES), f32)] + grad_queries, 0),
            overlapped(grad_keys),
            overlapped(grad_values),
        )
        for kind in range(3):
            at = (kind * pairs + pair) * LANES
            taps = taps_ref[:, at : at + LANES]
            through = grads_mixed[kind] * sigs[kind]
            one = same_one * through
            two = same_two * through
            summed = (
                through * convs[kind] * (1.0 - sigs[kind])
                + taps[0:1] * through
                + taps[1:2] * shifted_up(one, 1)
                + taps[2:3] * shifted_up(two, 2)
            )
            out_ref[0, :, at : at + LANES] = summed.astype(bf16)
            value = values[kind]
            tap_ref[0:1, at : at + LANES] += jnp.sum(through * value, 0, keepdims=True)
            tap_ref[1:2, at : at + LANES] += jnp.sum(
                one * shifted_down(value, 1), 0, keepdims=True
            )
            tap_ref[2:3, at : at + LANES] += jnp.sum(
                two * shifted_down(value, 2), 0, keepdims=True
            )


def attention_specs(rows, columns, subs):
    return [
        pl.BlockSpec((3, columns), lambda b: (0, 0)),
        pl.BlockSpec((1, rows, LANES), lambda b: (b, 0, 0)),
        pl.BlockSpec((1, subs, 2 * WINDOW), lambda b: (b, 0, 0)),
    ]


def attend(where, tokens, gain, taps, seg_rows, seg_keys, pieces, chunk, score_scale):
    blocks, rows, width = tokens.shape
    columns = taps.shape[1]
    subs = seg_keys.shape[1]
    copies = sum(p.shape[0] // chunk for p in pieces)
    return pl.pallas_call(
        functools.partial(
            attend_kernel, n=len(pieces), chunk=chunk, subs=subs, score_scale=score_scale
        ),
        grid=(blocks,),
        out_shape=(
            jax.ShapeDtypeStruct((blocks, rows - HALO, columns // 3), bf16),
            jax.ShapeDtypeStruct((blocks, rows, columns), f32),
            jax.ShapeDtypeStruct((2, width, columns // 2), bf16),
            jax.ShapeDtypeStruct((blocks, rows, width), bf16),
        ),
        in_specs=[
            pl.BlockSpec(memory_space=pltpu.SMEM),
            pl.BlockSpec((1, rows, width), lambda b: (b, 0, 0)),
            pl.BlockSpec((1, width), lambda b: (0, 0)),
        ]
        + attention_specs(rows, columns, subs)
        + [pl.BlockSpec(memory_space=pl.ANY)] * len(pieces),
        out_specs=(
            pl.BlockSpec((1, rows - HALO, columns // 3), lambda b: (b, 0, 0)),
            pl.BlockSpec((1, rows, columns), lambda b: (b, 0, 0)),
            pl.BlockSpec((2, width, columns // 2), lambda b: (0, 0, 0)),
            pl.BlockSpec((1, rows, width), lambda b: (b, 0, 0)),
        ),
        scratch_shapes=[pltpu.SemaphoreType.DMA((copies,))],
        compiler_params=pltpu.CompilerParams(vmem_limit_bytes=60 * MIB),
        cost_estimate=pl.CostEstimate(
            flops=20 * 10**9, bytes_accessed=20 * 10**6, transcendentals=0
        ),
        name="attend",
    )(where, tokens, gain, taps, seg_rows, seg_keys, *pieces)


def attend_back(branch, out_weight, projected, taps, seg_rows, seg_keys, score_scale):
    blocks, rows, columns = projected.shape
    width = branch.shape[2]
    subs = seg_keys.shape[1]
    return pl.pallas_call(
        functools.partial(attend_back_kernel, subs=subs, score_scale=score_scale),
        grid=(blocks,),
        out_shape=(
            jax.ShapeDtypeStruct((blocks, rows, columns), bf16),
            jax.ShapeDtypeStruct((8, columns), f32),
        ),
        in_specs=[
            pl.BlockSpec((1, rows - HALO, width), lambda b: (b, 0, 0)),
            pl.BlockSpec((columns // 3, width), lambda b: (0, 0)),
            pl.BlockSpec((1, rows, columns), lambda b: (b, 0, 0)),
        ]
        + attention_specs(rows, columns, subs),
        out_specs=(
            pl.BlockSpec((1, rows, columns), lambda b: (b, 0, 0)),
            pl.BlockSpec((8, columns), lambda b: (0, 0)),
        ),
        compiler_params=pltpu.CompilerParams(vmem_limit_bytes=60 * MIB),
        cost_estimate=pl.CostEstimate(
            flops=20 * 10**9, bytes_accessed=20 * 10**6, transcendentals=0
        ),
        name="attend_back",
    )(branch, out_weight, projected, taps, seg_rows, seg_keys)


def dense_kernel(where_ref, dense_ref, gate_hbm, hidden_ref, inner_ref, gate_ref, sems, *, chunk):
    for copy in place_pieces([gate_hbm], chunk, where_ref, 0, gate_ref, sems):
        copy.wait()
    rows, hidden_wide = hidden_ref.shape

    @pl.loop(0, rows // TILE)
    def block(index):
        own = pl.ds(pl.multiple_of(index * TILE, TILE), TILE)
        normed = dense_ref[own, :]
        for first in range(0, hidden_wide, TILE):
            unit = slice(first, first + TILE)
            gate = plain(normed, gate_ref[0, :, unit])
            up = plain(normed, gate_ref[1, :, unit])
            sig = jax.nn.sigmoid(gate)
            silu = gate * sig
            hidden_ref[own, unit] = (silu * up).astype(bf16)
            inner_ref[0, own, unit] = up * (sig * (1.0 + gate * (1.0 - sig)))
            inner_ref[1, own, unit] = silu


def fetch_down(down_hbm, down_ref, sem):
    real = down_hbm.shape[0]
    copy = pltpu.make_async_copy(down_hbm, down_ref.at[:real], sem)
    copy.start()
    if real < down_ref.shape[0]:
        down_ref[real:] = jnp.zeros((down_ref.shape[0] - real, down_ref.shape[1]), bf16)
    return copy


def dense_back_kernel(
    where_ref,
    cotangent_ref,
    inner_hbm,
    gate_hbm,
    down_hbm,
    grad_ref,
    joined_ref,
    down_ref,
    inner_ref,
    gate_ref,
    sems,
    *,
    chunk,
):
    rows, width = cotangent_ref.shape
    hidden_wide = joined_ref.shape[2]
    count = gate_hbm.shape[0] // chunk
    down_copy = fetch_down(down_hbm, down_ref, sems.at[count])
    inner_copies = []
    for index in range(rows // TILE):
        own = slice(index * TILE, (index + 1) * TILE)
        copy = pltpu.make_async_copy(
            inner_hbm.at[:, own], inner_ref.at[:, own], sems.at[count + 1 + index]
        )
        copy.start()
        inner_copies.append(copy)
    gate_copies = place_pieces([gate_hbm], chunk, where_ref, 0, gate_ref, sems)
    down_copy.wait()
    for index in range(rows // TILE):
        inner_copies[index].wait()
        own = slice(index * TILE, (index + 1) * TILE)
        cotangent = cotangent_ref[own, :]
        for first in range(0, hidden_wide, TILE):
            unit = slice(first, first + TILE)
            grad = contract_last(cotangent, down_ref[unit])
            joined_ref[0, own, unit] = (grad * inner_ref[0, own, unit]).astype(bf16)
            joined_ref[1, own, unit] = (grad * inner_ref[1, own, unit]).astype(bf16)
    for copy in gate_copies:
        copy.wait()

    @pl.loop(0, rows // TILE)
    def block(index):
        own = pl.ds(pl.multiple_of(index * TILE, TILE), TILE)
        gates = joined_ref[0, own, :]
        ups = joined_ref[1, own, :]
        for first in range(0, width, TILE):
            unit = slice(first, first + TILE)
            grad_ref[own, unit] = (
                contract_last(gates, gate_ref[0, unit]) + contract_last(ups, gate_ref[1, unit])
            ).astype(bf16)


def dense_out_kernel(hidden_ref, down_hbm, out_ref, down_ref, sem):
    fetch_down(down_hbm, down_ref, sem).wait()

    @pl.loop(0, hidden_ref.shape[0] // TILE)
    def block(index):
        own = pl.ds(pl.multiple_of(index * TILE, TILE), TILE)
        out_ref[own, :] = plain(hidden_ref[own, :], down_ref[...]).astype(bf16)


def down_grad_kernel(hidden_ref, cotangent_ref, out_ref):
    out_ref[...] = contract_first(hidden_ref[...], cotangent_ref[...]).astype(bf16)[
        : out_ref.shape[0]
    ]


WHOLE = pl.BlockSpec(memory_space=pltpu.VMEM)
OUTSIDE = pl.BlockSpec(memory_space=pl.ANY)
SCALARS = pl.BlockSpec(memory_space=pltpu.SMEM)


def kernel_params(giga_flops):
    return dict(
        compiler_params=pltpu.CompilerParams(vmem_limit_bytes=60 * MIB),
        cost_estimate=pl.CostEstimate(
            flops=giga_flops * 10**9, bytes_accessed=20 * 10**6, transcendentals=0
        ),
    )


def dense(where, normed, gate, chunk):
    rows, width = normed.shape
    hidden_wide = gate.shape[1]
    return pl.pallas_call(
        functools.partial(dense_kernel, chunk=chunk),
        out_shape=(
            jax.ShapeDtypeStruct((rows, hidden_wide), bf16),
            jax.ShapeDtypeStruct((2, rows, hidden_wide), f32),
        ),
        in_specs=[SCALARS, WHOLE, OUTSIDE],
        out_specs=(WHOLE, WHOLE),
        scratch_shapes=[
            pltpu.VMEM((2, width, hidden_wide), bf16),
            pltpu.SemaphoreType.DMA((gate.shape[0] // chunk,)),
        ],
        name="dense",
        **kernel_params(15),
    )(where, normed, gate)


def dense_back(where, cotangent, inner, gate, chunk, down):
    rows, width = cotangent.shape
    hidden_wide = gate.shape[1]
    copies = 1 + rows // TILE + gate.shape[0] // chunk
    return pl.pallas_call(
        functools.partial(dense_back_kernel, chunk=chunk),
        out_shape=(
            jax.ShapeDtypeStruct((rows, width), bf16),
            jax.ShapeDtypeStruct((2, rows, hidden_wide), bf16),
        ),
        in_specs=[SCALARS, WHOLE, OUTSIDE, OUTSIDE, OUTSIDE],
        out_specs=(WHOLE, WHOLE),
        scratch_shapes=[
            pltpu.VMEM((hidden_wide, width), bf16),
            pltpu.VMEM((2, rows, hidden_wide), f32),
            pltpu.VMEM((2, width, hidden_wide), bf16),
            pltpu.SemaphoreType.DMA((copies,)),
        ],
        name="dense_back",
        **kernel_params(20),
    )(where, cotangent, inner, gate, down)


def dense_out(hidden, down):
    rows, hidden_wide = hidden.shape
    width = down.shape[1]
    return pl.pallas_call(
        dense_out_kernel,
        out_shape=jax.ShapeDtypeStruct((rows, width), bf16),
        in_specs=[WHOLE, OUTSIDE],
        out_specs=WHOLE,
        scratch_shapes=[pltpu.VMEM((hidden_wide, width), bf16), pltpu.SemaphoreType.DMA],
        name="dense_out",
        **kernel_params(8),
    )(hidden, down)


def down_gradient(hidden, cotangent, units):
    rows, hidden_wide = hidden.shape
    width = cotangent.shape[1]
    return pl.pallas_call(
        down_grad_kernel,
        grid=(2,),
        out_shape=jax.ShapeDtypeStruct((units, width), bf16),
        in_specs=[
            pl.BlockSpec((rows, hidden_wide), lambda h: (0, 0)),
            pl.BlockSpec((rows, width // 2), lambda h: (0, h)),
        ],
        out_specs=pl.BlockSpec((units, width // 2), lambda h: (0, h)),
        name="down_grad",
        **kernel_params(8),
    )(hidden, cotangent)


def normed_grad_kernel(grad_ref, weight_ref, out_ref, halo_ref):
    half_wide = weight_ref.shape[2]
    grads = grad_ref[0]
    product = (
        contract_last(grads[:, :half_wide], weight_ref[0])
        + contract_last(grads[:, half_wide:], weight_ref[1])
    ).astype(bf16)
    halo_ref[0] = product[:HALO]
    out_ref[0] = product[HALO:]


def normed_grad(grad_projected, weight):
    blocks, rows, columns = grad_projected.shape
    width = weight.shape[1]
    return pl.pallas_call(
        normed_grad_kernel,
        grid=(blocks,),
        out_shape=(
            jax.ShapeDtypeStruct((blocks, rows - HALO, width), bf16),
            jax.ShapeDtypeStruct((blocks, HALO, width), bf16),
        ),
        in_specs=[
            pl.BlockSpec((1, rows, columns), lambda b: (b, 0, 0)),
            pl.BlockSpec((2, width, columns // 2), lambda b: (0, 0, 0)),
        ],
        out_specs=(
            pl.BlockSpec((1, rows - HALO, width), lambda b: (b, 0, 0)),
            pl.BlockSpec((1, HALO, width), lambda b: (b, 0, 0)),
        ),
        name="normed_grad",
        **kernel_params(15),
    )(grad_projected, weight)


def weight_grad_kernel(left_ref, right_ref, out_ref):
    right = right_ref[...].reshape(right_ref.shape[-2:])
    product = contract_first(left_ref[...], right).astype(bf16)
    planes, unused, rows, columns = out_ref.shape
    out_ref[:, 0] = product[: planes * rows].reshape(planes, rows, columns)


def weight_grad(left, right, planes, rows, name):
    tokens, depth = left.shape
    columns = right.shape[-1] if right.ndim == 3 else right.shape[-1] // 2
    steps = 2 if planes * rows == depth else 1
    if right.ndim == 3:
        right_spec = pl.BlockSpec((1, tokens, columns), lambda h, k: (h, 0, 0))
    else:
        right_spec = pl.BlockSpec((tokens, columns), lambda h, k: (0, h))
    return pl.pallas_call(
        weight_grad_kernel,
        grid=(2, steps),
        out_shape=jax.ShapeDtypeStruct((planes, 2, rows, columns), bf16),
        in_specs=[pl.BlockSpec((tokens, depth // steps), lambda h, k: (0, k)), right_spec],
        out_specs=pl.BlockSpec((planes // steps, 1, rows, columns), lambda h, k: (k, h, 0, 0)),
        compiler_params=pltpu.CompilerParams(vmem_limit_bytes=60 * MIB),
        cost_estimate=pl.CostEstimate(
            flops=20 * 10**9, bytes_accessed=20 * 10**6, transcendentals=0
        ),
        name=name,
    )(left, right)


def fence(*values):
    return lax.optimization_barrier(values)


def layer(
    planes,
    tokens,
    segments,
    cotangent,
    mixer_gain,
    qkv_weight,
    conv_taps,
    out_weight,
    dense_gain,
    gateup_weight,
    down_weight,
):
    count = planes * PLANE
    rows, width = tokens.shape
    ext = HALO + rows
    subs = rows // WINDOW
    quarter = width // 4
    padded = -(-quarter // LANES) * LANES
    half_wide = 3 * padded // 2
    half_width = width // 2
    shard_rows = qkv_weight.shape[0]
    down_rows = down_weight.shape[0]
    square_rows = 4 * shard_rows
    octet_rows = PLANE * shard_rows
    hidden_width = down_rows * count
    hidden_part = hidden_width // 4
    hidden_wide = -(-hidden_part // 256) * 256
    tap_columns = conv_taps.shape[1]
    out_planes = planes // 4
    z = lax.axis_index("z")
    y = lax.axis_index("y")
    x = lax.axis_index("x")
    c = lax.axis_index("core")
    part = 2 * y + x
    score_scale = 1.0 / math.sqrt(HDIM)

    def swap(array, axes):
        return lax.all_to_all(array, axes, 0, 0)

    def flip(array, axis):
        return lax.ppermute(array, axis, [(0, 1), (1, 0)])

    def in_order(own, other, bit):
        return jnp.where(bit == 0, own, other), jnp.where(bit == 0, other, own)

    def absolute(pieces):
        whole = jnp.zeros((planes,) + pieces[0].shape, pieces[0].dtype)
        for step, piece in enumerate(pieces):
            first = ((z + step) % planes,) + (0,) * piece.ndim
            whole = lax.dynamic_update_slice(whole, piece[None], first)
        return whole

    def gather_rows(array, axes):
        return swap(jnp.broadcast_to(array, (4,) + array.shape), axes)

    def rows_at(bits, size):
        return jnp.stack([jnp.asarray(b, jnp.int32) for b in bits]).reshape(-1, size)

    qkv_slices = qkv_weight.reshape(shard_rows, 3, 4, quarter)
    qkv_slices = jnp.pad(qkv_slices, ((0, 0), (0, 0), (0, 0), (0, padded - quarter)))
    qkv_slices = qkv_slices.transpose(2, 0, 1, 3).reshape(4, shard_rows, 2, half_wide)
    qkv_slices = qkv_slices.transpose(0, 2, 1, 3).reshape(PLANE, shard_rows, half_wide)
    owned = jnp.concatenate([mixer_gain, dense_gain, conv_taps.reshape(-1)])
    owned_size = owned.shape[0]
    owned = jnp.pad(owned.reshape(1, -1), ((0, 1), (0, half_wide - owned_size)))
    owned = jnp.broadcast_to(owned, (PLANE, 2, half_wide))
    qkv_slices, gateup_weight, down_weight, out_weight = fence(
        jnp.concatenate([qkv_slices, owned], 1), gateup_weight, down_weight, out_weight
    )

    lines = []
    for d in range(count):
        lines.append(2 * planes * (d % PLANE // 2) + 2 * (d // PLANE) + d % 2)
    out_piece = lax.ppermute(out_weight, ALL, [(lines[d], d) for d in range(count)])
    before = lax.ppermute(tokens[rows - HALO :], ALL, [(d, d + 1) for d in range(count - 1)])

    qkv_piece = swap(qkv_slices, OCTET)
    gateup_slices = gateup_weight.reshape(shard_rows, 2, planes, 4, hidden_part // planes)
    gateup_slices = gateup_slices.transpose(3, 1, 0, 2, 4)
    gateup_slices = gateup_slices.reshape(PLANE, shard_rows, hidden_part)
    gateup_slices = jnp.pad(gateup_slices, ((0, 0), (0, 0), (0, hidden_wide - hidden_part)))
    qkv_piece, gateup_slices, tokens_now, before = fence(
        qkv_piece, gateup_slices, tokens, before
    )
    out_all = lax.all_gather(out_piece, LINE)
    small = [qkv_piece[:, shard_rows, :owned_size]]
    qkv_piece, small[0] = fence(qkv_piece[:, :shard_rows].reshape(octet_rows, half_wide), small[0])

    qkv_pieces, qkv_others = [qkv_piece], []
    onward = [(i, (i - 1) % planes) for i in range(planes)]
    for step in range(1, planes):
        qkv_next = lax.ppermute(qkv_pieces[-1], "z", onward)
        if step == 1:
            gateup_piece = swap(gateup_slices, OCTET).reshape(octet_rows, hidden_wide)
            for by in range(1, planes):
                shift = [(i, (i - by) % planes) for i in range(planes)]
                small.append(lax.ppermute(small[0], "z", shift))
            qkv_next, gateup_piece, tokens_now, small = fence(
                qkv_next, gateup_piece, tokens_now, small
            )
            token_group = gather_rows(jnp.concatenate([before, tokens_now]), SQUARE)
        elif step < planes - 1:
            (qkv_next,) = fence(qkv_next)
        else:
            small = absolute(small).astype(f32)
            gain_one = small[:, :, :shard_rows].reshape(1, width)
            gain_two = small[:, :, shard_rows : 2 * shard_rows].reshape(width)
            taps = small[:, :, 2 * shard_rows :].reshape(count, 3, tap_columns).transpose(1, 0, 2)
            taps = taps.reshape(3, 3, 4, quarter)
            taps = lax.dynamic_index_in_dim(taps, part, 2, keepdims=False)
            taps = jnp.pad(taps, ((0, 0), (0, 0), (0, padded - quarter)))
            taps = taps.reshape(3, 3 * padded)
            cotangent_now = jnp.broadcast_to(cotangent, (4,) + cotangent.shape)
            out = fence(qkv_next, cotangent_now, token_group, gateup_piece, gain_one, gain_two, taps)
            qkv_next, cotangent_now, token_group, gateup_piece, gain_one, gain_two, taps = out
        qkv_others.append(flip(qkv_pieces[-1], "core"))
        qkv_pieces.append(qkv_next)
    qkv_pieces, qkv_others, down_piece, cotangent_now = fence(
        qkv_pieces, qkv_others, down_weight, cotangent_now
    )
    gateup_all = lax.all_gather(gateup_piece, LINE)
    down_all = lax.all_gather(down_piece, LINE).reshape(hidden_part, width)
    qkv_others.append(flip(qkv_pieces[-1], "core"))
    (qkv_others,) = fence(qkv_others)
    out_full = jnp.pad(out_all.reshape(quarter, width), ((0, padded - quarter), (0, 0)))

    padded_segments = jnp.concatenate([jnp.full((HALO,), -1, jnp.int32), segments])
    seg_rows = jnp.stack(
        [
            lax.dynamic_slice_in_dim(padded_segments, (PLANE * z + 2 * b + c) * rows, ext)
            for b in range(4)
        ]
    )
    seg_keys = jnp.stack(
        [
            seg_rows[:, HALO - WINDOW + s * WINDOW : HALO + WINDOW + s * WINDOW]
            for s in range(subs)
        ],
        1,
    )
    seg_rows = jnp.broadcast_to(seg_rows[:, :, None], (4, ext, LANES))

    cotangent_group = swap(cotangent_now, SQUARE).reshape(4 * rows, width)
    where_qkv = []
    for own in range(2):
        for step in range(planes):
            where_qkv += [c ^ own, (z + step) % planes * octet_rows]
    attended, projected, qkv_full, normed_group = attend(
        rows_at(where_qkv, 2),
        token_group,
        gain_one,
        taps,
        seg_rows,
        seg_keys,
        qkv_pieces + qkv_others,
        octet_rows,
        score_scale,
    )
    attended = attended.reshape(4 * rows, padded)
    attended, normed_group, cotangent_group = fence(attended, normed_group, cotangent_group)
    mixer_out = plain(attended, out_full).astype(bf16).reshape(4, rows, width)

    mixer_sum = swap(mixer_out, SQUARE)
    own_tokens = tokens.astype(f32)
    residual = own_tokens + jnp.sum(mixer_sum.astype(f32), 0)
    normed_dense = rms_scale(residual, gain_two).astype(bf16)
    dense_group = gather_rows(normed_dense, SQUARE).reshape(4 * rows, width)

    gateup_chunk = octet_rows
    where_gateup = [k for i in range(planes) for h in range(2) for k in (h, i * gateup_chunk)]
    gateup_all = gateup_all.reshape(-1, hidden_wide)
    where_gateup = rows_at(where_gateup, 2)
    hidden, inner = dense(where_gateup, dense_group, gateup_all, gateup_chunk)
    hidden, inner, cotangent_group = fence(hidden, inner, cotangent_group)
    down_grad = down_gradient(hidden, cotangent_group, hidden_part)
    inner, cotangent_group, down_grad, hidden = fence(inner, cotangent_group, down_grad, hidden)
    down_mine = lax.psum_scatter(
        down_grad.reshape(2 * planes, down_rows, width), LINE, scatter_dimension=0
    )
    grad_dense, grad_inner = fence(
        *dense_back(where_gateup, cotangent_group, inner, gateup_all, gateup_chunk, down_all)
    )

    def scatter_line(array):
        return lax.psum_scatter(
            array.reshape((2 * planes,) + array.shape[2:]), LINE, scatter_dimension=0
        )

    grad_dense = swap(grad_dense.reshape(4, rows, width), SQUARE)
    gateup_grad = weight_grad(dense_group, grad_inner, planes, octet_rows, "gateup_grad")
    grad_dense, gateup_grad, hidden, down_all = fence(grad_dense, gateup_grad, hidden, down_all)
    gateup_mine = scatter_line(gateup_grad)

    unused, rms_back = jax.vjp(rms_scale, residual, gain_two)
    grad_residual, dense_gain_sum = rms_back(jnp.sum(grad_dense.astype(f32), 0))
    grad_residual = grad_residual + cotangent.astype(f32)
    grad_branch = gather_rows(grad_residual.astype(bf16), SQUARE)
    dense_rows = dense_out(hidden, down_all).reshape(4, rows, width)
    grad_branch, out_full, dense_rows, down_mine = fence(
        grad_branch, out_full, dense_rows, down_mine
    )
    dense_sum = swap(dense_rows, SQUARE)

    grad_projected, grad_taps = attend_back(
        grad_branch, out_full, projected, taps, seg_rows, seg_keys, score_scale
    )
    grad_normed, grad_halo = normed_grad(grad_projected, qkv_full)
    grad_projected, grad_normed, grad_halo, dense_sum = fence(
        grad_projected, grad_normed, grad_halo, dense_sum
    )

    halo_sum = swap(grad_halo, SQUARE)
    grad_projected = grad_projected.reshape(4 * ext, 3 * padded)
    normed_rows = normed_group.reshape(4 * ext, width)
    qkv_grad = weight_grad(normed_rows, grad_projected, planes, octet_rows, "qkv_grad")
    grad_branch = grad_branch.reshape(4 * rows, width)
    out = fence(qkv_grad, grad_normed, halo_sum, attended, grad_branch, gateup_mine)
    qkv_grad, grad_normed, halo_sum, attended, grad_branch, gateup_mine = out
    qkv_part = scatter_line(qkv_grad)

    normed_sum = swap(grad_normed, SQUARE)
    late = jnp.sum(halo_sum.astype(f32), 0).astype(bf16)
    late = lax.ppermute(late, ALL, [(d, d - 1) for d in range(1, count)])
    out_grad = contract_first(attended, grad_branch)[:quarter].astype(bf16)
    layer_out = (residual + jnp.sum(dense_sum.astype(f32), 0)).astype(bf16)
    normed_sum, late, gateup_mine, layer_out, out_grad = fence(
        normed_sum, late, gateup_mine, layer_out, out_grad
    )

    gateup_mine = swap(gateup_mine.reshape(PLANE, shard_rows, hidden_wide), OCTET)
    grad_normed = jnp.sum(normed_sum.astype(f32), 0)
    grad_normed = grad_normed + jnp.pad(late.astype(f32), ((rows - HALO, 0), (0, 0)))
    unused, mixer_back = jax.vjp(rms_scale, own_tokens, gain_one.reshape(width))
    grad_rows, mixer_gain_sum = mixer_back(grad_normed)
    input_grad = grad_residual + grad_rows

    grad_taps = grad_taps[:3].reshape(3, 3, 1, padded)[..., :quarter]
    grad_taps = lax.dynamic_update_slice(
        jnp.zeros((3, 3, 4, quarter), f32), grad_taps, (0, 0, part, 0)
    )
    grad_taps = grad_taps.reshape(3, count, tap_columns).transpose(1, 0, 2)
    sums = jnp.concatenate(
        [
            mixer_gain_sum.reshape(count, shard_rows),
            dense_gain_sum.reshape(count, shard_rows),
            grad_taps.reshape(count, 3 * tap_columns),
        ],
        1,
    )
    sums = sums.reshape(planes, PLANE, owned_size).transpose(1, 0, 2).astype(bf16)
    gateup_mine, qkv_part, input_grad, out_grad = fence(
        gateup_mine, qkv_part, input_grad, out_grad
    )
    out_mine = lax.psum_scatter(
        out_grad.reshape(2 * planes, shard_rows, width), LINE, scatter_dimension=0
    )

    qkv_mine = swap(qkv_part.reshape(PLANE, shard_rows, half_wide), OCTET)
    gateup_mine = gateup_mine[:, :, :hidden_part]
    gateup_mine = gateup_mine.reshape(4, 2, shard_rows, planes, hidden_part // planes)
    gateup_mine = gateup_mine.transpose(2, 1, 3, 0, 4).reshape(shard_rows, 2 * hidden_width)
    gateup_mine = gateup_mine.astype(f32)
    qkv_mine, sums, gateup_mine = fence(qkv_mine, sums, gateup_mine)
    sums = jnp.sum(swap(sums, OCTET).astype(f32), 0).astype(bf16)
    sums = jnp.sum(swap(sums, "z").astype(f32), 0)
    qkv_mine = qkv_mine.reshape(4, 2, shard_rows, half_wide).transpose(2, 0, 1, 3)
    qkv_mine = qkv_mine.reshape(shard_rows, 4, 3, padded)[..., :quarter].transpose(0, 2, 1, 3)
    qkv_mine = qkv_mine.reshape(shard_rows, 3 * width).astype(f32)
    out_mine = lax.ppermute(out_mine, ALL, [(d, lines[d]) for d in range(count)])
    return (
        layer_out,
        input_grad,
        sums[:shard_rows],
        qkv_mine,
        sums[2 * shard_rows :].reshape(3, tap_columns),
        out_mine.astype(f32),
        sums[shard_rows : 2 * shard_rows],
        gateup_mine,
        down_mine.astype(f32),
    )


def solution(mesh):
    planes = mesh.devices.size // PLANE
    split = Mesh(mesh.devices.reshape(planes, 2, 2, 2), ALL)
    over_rows = P(ALL, None)
    over_columns = P(None, ALL)
    return jax.shard_map(
        functools.partial(layer, planes),
        mesh=split,
        in_specs=(
            over_rows,
            P(),
            over_rows,
            P(ALL),
            over_rows,
            over_columns,
            over_rows,
            P(ALL),
            over_rows,
            over_rows,
        ),
        out_specs=(
            over_rows,
            over_rows,
            P(ALL),
            over_rows,
            over_columns,
            over_rows,
            P(ALL),
            over_rows,
            over_rows,
        ),
        check_vma=False,
    )
```

```python
import functools
import math

import jax
import jax.numpy as jnp
from jax import lax
from jax.experimental import pallas as pl
from jax.experimental.pallas import tpu as pltpu
from jax.sharding import Mesh, PartitionSpec as P

HDIM = 64
WINDOW = 64
HALO = 80
LANES = 128
PLANE = 8

eps_norm = 1e-05
masked_score = -1e30
bf16 = jnp.bfloat16
f32 = jnp.float32
MIB = 1024 * 1024
TILE = 256
ALL = ("z", "y", "x", "core")
SQUARE = ("y", "x")
OCTET = ("y", "x", "core")
LINE = ("z", "core")


def rms_scale(values, gains):
    inverse = lax.rsqrt(jnp.mean(values * values, axis=-1, keepdims=True) + eps_norm)
    return values * inverse * gains


def contract_last(left_side, right_side):
    return lax.dot_general(
        left_side, right_side, (((1,), (1,)), ((), ())), preferred_element_type=f32
    )


def contract_first(left_side, right_side):
    return lax.dot_general(
        left_side, right_side, (((0,), (0,)), ((), ())), preferred_element_type=f32
    )


def plain(left_side, right_side):
    return jnp.dot(left_side, right_side, preferred_element_type=f32)


def shifted_down(values, by):
    return pltpu.roll(values, by, 0)


def shifted_up(values, by):
    return pltpu.roll(values, values.shape[0] - by, 0)


def gate_of(values, taps, same_one, same_two):
    conv = (
        taps[0:1] * values
        + taps[1:2] * (same_one * shifted_down(values, 1))
        + taps[2:3] * (same_two * shifted_down(values, 2))
    )
    return conv, jax.nn.sigmoid(values)


def by_head(values):
    lane = lax.broadcasted_iota(jnp.int32, values.shape, 1)
    zero = jnp.zeros_like(values)
    return jnp.concatenate(
        [jnp.where(lane < HDIM, values, zero), jnp.where(lane < HDIM, zero, values)], 0
    )


def join_heads(values):
    half = values.shape[0] // 2
    lane = lax.broadcasted_iota(jnp.int32, (half, values.shape[1]), 1)
    return jnp.where(lane < HDIM, values[:half], values[half:])


def block_masks(seg_ref, keys_ref, subs):
    span = 2 * WINDOW
    row = lax.broadcasted_iota(jnp.int32, (WINDOW, span), 0)
    col = lax.broadcasted_iota(jnp.int32, (WINDOW, span), 1)
    near = (col > row) & (col <= row + WINDOW)
    masks = []
    for sub in range(subs):
        first = HALO + sub * WINDOW
        same = seg_ref[0, first : first + WINDOW] == keys_ref[0, sub : sub + 1]
        masks.append(near & same)
    return jnp.concatenate([mask for mask in masks for unused in range(2)], 0)


def same_rows(seg_ref):
    seg = seg_ref[0]
    same_one = (seg == shifted_down(seg, 1)).astype(f32)
    same_two = (seg == shifted_down(seg, 2)).astype(f32)
    return same_one, same_two


def pair_probs(queries, keysets, mask, score_scale):
    scores = jnp.concatenate([contract_last(q, k) for q, k in zip(queries, keysets)], 0)
    scores = jnp.where(mask, scores * score_scale, masked_score)
    exponent = jnp.exp(scores - jnp.max(scores, axis=-1, keepdims=True))
    return exponent * (1.0 / jnp.sum(exponent, axis=-1, keepdims=True))


def cut(values, subs, first, size):
    return [values[first + s * WINDOW : first + s * WINDOW + size] for s in range(subs)]


def parts_of(values, subs):
    return jnp.split(values, subs, 0)


def place_pieces(refs, chunk, where_ref, row, target, sems):
    copies = []
    for ref in refs:
        for first in range(0, ref.shape[0] // chunk * chunk, chunk):
            spot = pl.multiple_of(where_ref[row + len(copies), 1], 16)
            copy = pltpu.make_async_copy(
                ref.at[first : first + chunk],
                target.at[where_ref[row + len(copies), 0], pl.ds(spot, chunk)],
                sems.at[row + len(copies)],
            )
            copy.start()
            copies.append(copy)
    return copies


def attend_kernel(
    where_ref,
    tokens_ref,
    gain_ref,
    taps_ref,
    seg_ref,
    keys_ref,
    *rest,
    n,
    chunk,
    subs,
    score_scale,
):
    piece_refs, (out_ref, proj_ref, weight_ref, normed_ref, sems) = rest[:n], rest[n:]

    @pl.when(pl.program_id(0) == 0)
    def fetch():
        for copy in place_pieces(piece_refs, chunk, where_ref, 0, weight_ref, sems):
            copy.wait()

    normed_ref[0] = rms_scale(tokens_ref[0].astype(f32), gain_ref[...]).astype(bf16)
    half_wide = weight_ref.shape[2]
    for half in range(2):
        proj_ref[0, :, half * half_wide : (half + 1) * half_wide] = plain(
            normed_ref[0], weight_ref[half]
        )
    pairs = 2 * half_wide // (3 * LANES)
    same_one, same_two = same_rows(seg_ref)
    mask = block_masks(seg_ref, keys_ref, subs)
    first_key = HALO - WINDOW
    for pair in range(pairs):
        mixed = []
        for kind in range(3):
            at = (kind * pairs + pair) * LANES
            conv, sig = gate_of(
                proj_ref[0, :, at : at + LANES], taps_ref[:, at : at + LANES], same_one, same_two
            )
            mixed.append((conv * sig).astype(bf16))
        queries = [by_head(q) for q in cut(mixed[0], subs, HALO, WINDOW)]
        keysets = cut(mixed[1], subs, first_key, 2 * WINDOW)
        valuesets = cut(mixed[2], subs, first_key, 2 * WINDOW)
        weights = parts_of(pair_probs(queries, keysets, mask, score_scale).astype(bf16), subs)
        for sub in range(subs):
            out_ref[0, sub * WINDOW : (sub + 1) * WINDOW, pair * LANES : (pair + 1) * LANES] = (
                join_heads(plain(weights[sub], valuesets[sub])).astype(bf16)
            )


def attend_back_kernel(
    branch_ref, out_weight_ref, proj_ref, taps_ref, seg_ref, keys_ref, out_ref, tap_ref, *, subs, score_scale
):
    @pl.when(pl.program_id(0) == 0)
    def clear():
        tap_ref[...] = jnp.zeros_like(tap_ref)

    grad_attended = contract_last(branch_ref[0], out_weight_ref[...]).astype(bf16)
    pairs = proj_ref.shape[2] // (3 * LANES)
    same_one, same_two = same_rows(seg_ref)
    mask = block_masks(seg_ref, keys_ref, subs)
    first_key = HALO - WINDOW
    for pair in range(pairs):
        values, convs, sigs, mixed = [], [], [], []
        for kind in range(3):
            at = (kind * pairs + pair) * LANES
            value = proj_ref[0, :, at : at + LANES]
            conv, sig = gate_of(value, taps_ref[:, at : at + LANES], same_one, same_two)
            values.append(value)
            convs.append(conv)
            sigs.append(sig)
            mixed.append((conv * sig).astype(bf16))
        queries = [by_head(q) for q in cut(mixed[0], subs, HALO, WINDOW)]
        keysets = cut(mixed[1], subs, first_key, 2 * WINDOW)
        valuesets = cut(mixed[2], subs, first_key, 2 * WINDOW)
        grads = [
            by_head(g)
            for g in cut(grad_attended[:, pair * LANES : (pair + 1) * LANES], subs, 0, WINDOW)
        ]
        probs = pair_probs(queries, keysets, mask, score_scale)
        grad_probs = jnp.concatenate([contract_last(g, v) for g, v in zip(grads, valuesets)], 0)
        inner = jnp.sum(probs * grad_probs, axis=-1, keepdims=True)
        grad_scores = parts_of((probs * (grad_probs - inner)).astype(bf16), subs)
        weights = parts_of(probs.astype(bf16), subs)
        grad_queries = [
            join_heads(plain(g, k)) * score_scale for g, k in zip(grad_scores, keysets)
        ]
        grad_keys = [contract_first(g, q) * score_scale for g, q in zip(grad_scores, queries)]
        grad_values = [contract_first(w, g) for w, g in zip(weights, grads)]

        def overlapped(parts):
            rows = [jnp.zeros((first_key, LANES), f32), parts[0][:WINDOW]]
            for sub in range(1, subs):
                rows.append(parts[sub - 1][WINDOW:] + parts[sub][:WINDOW])
            rows.append(parts[subs - 1][WINDOW:])
            return jnp.concatenate(rows, 0)

        grads_mixed = (
            jnp.concatenate([jnp.zeros((HALO, LANES), f32)] + grad_queries, 0),
            overlapped(grad_keys),
            overlapped(grad_values),
        )
        for kind in range(3):
            at = (kind * pairs + pair) * LANES
            taps = taps_ref[:, at : at + LANES]
            through = grads_mixed[kind] * sigs[kind]
            one = same_one * through
            two = same_two * through
            summed = (
                through * convs[kind] * (1.0 - sigs[kind])
                + taps[0:1] * through
                + taps[1:2] * shifted_up(one, 1)
                + taps[2:3] * shifted_up(two, 2)
            )
            out_ref[0, :, at : at + LANES] = summed.astype(bf16)
            value = values[kind]
            tap_ref[0:1, at : at + LANES] += jnp.sum(through * value, 0, keepdims=True)
            tap_ref[1:2, at : at + LANES] += jnp.sum(
                one * shifted_down(value, 1), 0, keepdims=True
            )
            tap_ref[2:3, at : at + LANES] += jnp.sum(
                two * shifted_down(value, 2), 0, keepdims=True
            )


def attention_specs(rows, columns, subs):
    return [
        pl.BlockSpec((3, columns), lambda b: (0, 0)),
        pl.BlockSpec((1, rows, LANES), lambda b: (b, 0, 0)),
        pl.BlockSpec((1, subs, 2 * WINDOW), lambda b: (b, 0, 0)),
    ]


def attend(where, tokens, gain, taps, seg_rows, seg_keys, pieces, chunk, score_scale):
    blocks, rows, width = tokens.shape
    columns = taps.shape[1]
    subs = seg_keys.shape[1]
    copies = sum(p.shape[0] // chunk for p in pieces)
    return pl.pallas_call(
        functools.partial(
            attend_kernel, n=len(pieces), chunk=chunk, subs=subs, score_scale=score_scale
        ),
        grid=(blocks,),
        out_shape=(
            jax.ShapeDtypeStruct((blocks, rows - HALO, columns // 3), bf16),
            jax.ShapeDtypeStruct((blocks, rows, columns), f32),
            jax.ShapeDtypeStruct((2, width, columns // 2), bf16),
            jax.ShapeDtypeStruct((blocks, rows, width), bf16),
        ),
        in_specs=[
            pl.BlockSpec(memory_space=pltpu.SMEM),
            pl.BlockSpec((1, rows, width), lambda b: (b, 0, 0)),
            pl.BlockSpec((1, width), lambda b: (0, 0)),
        ]
        + attention_specs(rows, columns, subs)
        + [pl.BlockSpec(memory_space=pl.ANY)] * len(pieces),
        out_specs=(
            pl.BlockSpec((1, rows - HALO, columns // 3), lambda b: (b, 0, 0)),
            pl.BlockSpec((1, rows, columns), lambda b: (b, 0, 0)),
            pl.BlockSpec((2, width, columns // 2), lambda b: (0, 0, 0)),
            pl.BlockSpec((1, rows, width), lambda b: (b, 0, 0)),
        ),
        scratch_shapes=[pltpu.SemaphoreType.DMA((copies,))],
        compiler_params=pltpu.CompilerParams(vmem_limit_bytes=60 * MIB),
        cost_estimate=pl.CostEstimate(
            flops=20 * 10**9, bytes_accessed=20 * 10**6, transcendentals=0
        ),
        name="attend",
    )(where, tokens, gain, taps, seg_rows, seg_keys, *pieces)


def attend_back(branch, out_weight, projected, taps, seg_rows, seg_keys, score_scale):
    blocks, rows, columns = projected.shape
    width = branch.shape[2]
    subs = seg_keys.shape[1]
    return pl.pallas_call(
        functools.partial(attend_back_kernel, subs=subs, score_scale=score_scale),
        grid=(blocks,),
        out_shape=(
            jax.ShapeDtypeStruct((blocks, rows, columns), bf16),
            jax.ShapeDtypeStruct((8, columns), f32),
        ),
        in_specs=[
            pl.BlockSpec((1, rows - HALO, width), lambda b: (b, 0, 0)),
            pl.BlockSpec((columns // 3, width), lambda b: (0, 0)),
            pl.BlockSpec((1, rows, columns), lambda b: (b, 0, 0)),
        ]
        + attention_specs(rows, columns, subs),
        out_specs=(
            pl.BlockSpec((1, rows, columns), lambda b: (b, 0, 0)),
            pl.BlockSpec((8, columns), lambda b: (0, 0)),
        ),
        compiler_params=pltpu.CompilerParams(vmem_limit_bytes=60 * MIB),
        cost_estimate=pl.CostEstimate(
            flops=20 * 10**9, bytes_accessed=20 * 10**6, transcendentals=0
        ),
        name="attend_back",
    )(branch, out_weight, projected, taps, seg_rows, seg_keys)


def dense_kernel(where_ref, dense_ref, gate_hbm, hidden_ref, inner_ref, gate_ref, sems, *, chunk):
    for copy in place_pieces([gate_hbm], chunk, where_ref, 0, gate_ref, sems):
        copy.wait()
    rows, hidden_wide = hidden_ref.shape

    @pl.loop(0, rows // TILE)
    def block(index):
        own = pl.ds(pl.multiple_of(index * TILE, TILE), TILE)
        normed = dense_ref[own, :]
        for first in range(0, hidden_wide, TILE):
            unit = slice(first, first + TILE)
            gate = plain(normed, gate_ref[0, :, unit])
            up = plain(normed, gate_ref[1, :, unit])
            sig = jax.nn.sigmoid(gate)
            silu = gate * sig
            hidden_ref[own, unit] = (silu * up).astype(bf16)
            inner_ref[0, own, unit] = up * (sig * (1.0 + gate * (1.0 - sig)))
            inner_ref[1, own, unit] = silu


def fetch_down(down_hbm, down_ref, sem):
    real = down_hbm.shape[0]
    copy = pltpu.make_async_copy(down_hbm, down_ref.at[:real], sem)
    copy.start()
    if real < down_ref.shape[0]:
        down_ref[real:] = jnp.zeros((down_ref.shape[0] - real, down_ref.shape[1]), bf16)
    return copy


def dense_back_kernel(
    where_ref,
    cotangent_ref,
    inner_hbm,
    gate_hbm,
    down_hbm,
    grad_ref,
    joined_ref,
    down_ref,
    inner_ref,
    gate_ref,
    sems,
    *,
    chunk,
):
    rows, width = cotangent_ref.shape
    hidden_wide = joined_ref.shape[2]
    count = gate_hbm.shape[0] // chunk
    down_copy = fetch_down(down_hbm, down_ref, sems.at[count])
    inner_copies = []
    for index in range(rows // TILE):
        own = slice(index * TILE, (index + 1) * TILE)
        copy = pltpu.make_async_copy(
            inner_hbm.at[:, own], inner_ref.at[:, own], sems.at[count + 1 + index]
        )
        copy.start()
        inner_copies.append(copy)
    gate_copies = place_pieces([gate_hbm], chunk, where_ref, 0, gate_ref, sems)
    down_copy.wait()
    for index in range(rows // TILE):
        inner_copies[index].wait()
        own = slice(index * TILE, (index + 1) * TILE)
        cotangent = cotangent_ref[own, :]
        for first in range(0, hidden_wide, TILE):
            unit = slice(first, first + TILE)
            grad = contract_last(cotangent, down_ref[unit])
            joined_ref[0, own, unit] = (grad * inner_ref[0, own, unit]).astype(bf16)
            joined_ref[1, own, unit] = (grad * inner_ref[1, own, unit]).astype(bf16)
    for copy in gate_copies:
        copy.wait()

    @pl.loop(0, rows // TILE)
    def block(index):
        own = pl.ds(pl.multiple_of(index * TILE, TILE), TILE)
        gates = joined_ref[0, own, :]
        ups = joined_ref[1, own, :]
        for first in range(0, width, TILE):
            unit = slice(first, first + TILE)
            grad_ref[own, unit] = (
                contract_last(gates, gate_ref[0, unit]) + contract_last(ups, gate_ref[1, unit])
            ).astype(bf16)


def dense_out_kernel(hidden_ref, down_hbm, out_ref, down_ref, sem):
    fetch_down(down_hbm, down_ref, sem).wait()

    @pl.loop(0, hidden_ref.shape[0] // TILE)
    def block(index):
        own = pl.ds(pl.multiple_of(index * TILE, TILE), TILE)
        out_ref[own, :] = plain(hidden_ref[own, :], down_ref[...]).astype(bf16)


def down_grad_kernel(hidden_ref, cotangent_ref, out_ref):
    out_ref[...] = contract_first(hidden_ref[...], cotangent_ref[...]).astype(bf16)[
        : out_ref.shape[0]
    ]


WHOLE = pl.BlockSpec(memory_space=pltpu.VMEM)
OUTSIDE = pl.BlockSpec(memory_space=pl.ANY)
SCALARS = pl.BlockSpec(memory_space=pltpu.SMEM)


def kernel_params(giga_flops):
    return dict(
        compiler_params=pltpu.CompilerParams(vmem_limit_bytes=60 * MIB),
        cost_estimate=pl.CostEstimate(
            flops=giga_flops * 10**9, bytes_accessed=20 * 10**6, transcendentals=0
        ),
    )


def dense(where, normed, gate, chunk):
    rows, width = normed.shape
    hidden_wide = gate.shape[1]
    return pl.pallas_call(
        functools.partial(dense_kernel, chunk=chunk),
        out_shape=(
            jax.ShapeDtypeStruct((rows, hidden_wide), bf16),
            jax.ShapeDtypeStruct((2, rows, hidden_wide), f32),
        ),
        in_specs=[SCALARS, WHOLE, OUTSIDE],
        out_specs=(WHOLE, WHOLE),
        scratch_shapes=[
            pltpu.VMEM((2, width, hidden_wide), bf16),
            pltpu.SemaphoreType.DMA((gate.shape[0] // chunk,)),
        ],
        name="dense",
        **kernel_params(15),
    )(where, normed, gate)


def dense_back(where, cotangent, inner, gate, chunk, down):
    rows, width = cotangent.shape
    hidden_wide = gate.shape[1]
    copies = 1 + rows // TILE + gate.shape[0] // chunk
    return pl.pallas_call(
        functools.partial(dense_back_kernel, chunk=chunk),
        out_shape=(
            jax.ShapeDtypeStruct((rows, width), bf16),
            jax.ShapeDtypeStruct((2, rows, hidden_wide), bf16),
        ),
        in_specs=[SCALARS, WHOLE, OUTSIDE, OUTSIDE, OUTSIDE],
        out_specs=(WHOLE, WHOLE),
        scratch_shapes=[
            pltpu.VMEM((hidden_wide, width), bf16),
            pltpu.VMEM((2, rows, hidden_wide), f32),
            pltpu.VMEM((2, width, hidden_wide), bf16),
            pltpu.SemaphoreType.DMA((copies,)),
        ],
        name="dense_back",
        **kernel_params(20),
    )(where, cotangent, inner, gate, down)


def dense_out(hidden, down):
    rows, hidden_wide = hidden.shape
    width = down.shape[1]
    return pl.pallas_call(
        dense_out_kernel,
        out_shape=jax.ShapeDtypeStruct((rows, width), bf16),
        in_specs=[WHOLE, OUTSIDE],
        out_specs=WHOLE,
        scratch_shapes=[pltpu.VMEM((hidden_wide, width), bf16), pltpu.SemaphoreType.DMA],
        name="dense_out",
        **kernel_params(8),
    )(hidden, down)


def down_gradient(hidden, cotangent, units):
    rows, hidden_wide = hidden.shape
    width = cotangent.shape[1]
    return pl.pallas_call(
        down_grad_kernel,
        grid=(2,),
        out_shape=jax.ShapeDtypeStruct((units, width), bf16),
        in_specs=[
            pl.BlockSpec((rows, hidden_wide), lambda h: (0, 0)),
            pl.BlockSpec((rows, width // 2), lambda h: (0, h)),
        ],
        out_specs=pl.BlockSpec((units, width // 2), lambda h: (0, h)),
        name="down_grad",
        **kernel_params(8),
    )(hidden, cotangent)


def normed_grad_kernel(grad_ref, weight_ref, out_ref, halo_ref):
    half_wide = weight_ref.shape[2]
    grads = grad_ref[0]
    product = (
        contract_last(grads[:, :half_wide], weight_ref[0])
        + contract_last(grads[:, half_wide:], weight_ref[1])
    ).astype(bf16)
    halo_ref[0] = product[:HALO]
    out_ref[0] = product[HALO:]


def normed_grad(grad_projected, weight):
    blocks, rows, columns = grad_projected.shape
    width = weight.shape[1]
    return pl.pallas_call(
        normed_grad_kernel,
        grid=(blocks,),
        out_shape=(
            jax.ShapeDtypeStruct((blocks, rows - HALO, width), bf16),
            jax.ShapeDtypeStruct((blocks, HALO, width), bf16),
        ),
        in_specs=[
            pl.BlockSpec((1, rows, columns), lambda b: (b, 0, 0)),
            pl.BlockSpec((2, width, columns // 2), lambda b: (0, 0, 0)),
        ],
        out_specs=(
            pl.BlockSpec((1, rows - HALO, width), lambda b: (b, 0, 0)),
            pl.BlockSpec((1, HALO, width), lambda b: (b, 0, 0)),
        ),
        name="normed_grad",
        **kernel_params(15),
    )(grad_projected, weight)


def weight_grad_kernel(left_ref, right_ref, out_ref):
    right = right_ref[...].reshape(right_ref.shape[-2:])
    product = contract_first(left_ref[...], right).astype(bf16)
    planes, unused, rows, columns = out_ref.shape
    out_ref[:, 0] = product[: planes * rows].reshape(planes, rows, columns)


def weight_grad(left, right, planes, rows, name):
    tokens, depth = left.shape
    columns = right.shape[-1] if right.ndim == 3 else right.shape[-1] // 2
    steps = 2 if planes * rows == depth else 1
    if right.ndim == 3:
        right_spec = pl.BlockSpec((1, tokens, columns), lambda h, k: (h, 0, 0))
    else:
        right_spec = pl.BlockSpec((tokens, columns), lambda h, k: (0, h))
    return pl.pallas_call(
        weight_grad_kernel,
        grid=(2, steps),
        out_shape=jax.ShapeDtypeStruct((planes, 2, rows, columns), bf16),
        in_specs=[pl.BlockSpec((tokens, depth // steps), lambda h, k: (0, k)), right_spec],
        out_specs=pl.BlockSpec((planes // steps, 1, rows, columns), lambda h, k: (k, h, 0, 0)),
        compiler_params=pltpu.CompilerParams(vmem_limit_bytes=60 * MIB),
        cost_estimate=pl.CostEstimate(
            flops=20 * 10**9, bytes_accessed=20 * 10**6, transcendentals=0
        ),
        name=name,
    )(left, right)


def fence(*values):
    return lax.optimization_barrier(values)


def layer(
    planes,
    tokens,
    segments,
    cotangent,
    mixer_gain,
    qkv_weight,
    conv_taps,
    out_weight,
    dense_gain,
    gateup_weight,
    down_weight,
):
    count = planes * PLANE
    rows, width = tokens.shape
    ext = HALO + rows
    subs = rows // WINDOW
    quarter = width // 4
    padded = -(-quarter // LANES) * LANES
    half_wide = 3 * padded // 2
    half_width = width // 2
    shard_rows = qkv_weight.shape[0]
    down_rows = down_weight.shape[0]
    square_rows = 4 * shard_rows
    octet_rows = PLANE * shard_rows
    hidden_width = down_rows * count
    hidden_part = hidden_width // 4
    hidden_wide = -(-hidden_part // 256) * 256
    tap_columns = conv_taps.shape[1]
    out_planes = planes // 4
    z = lax.axis_index("z")
    y = lax.axis_index("y")
    x = lax.axis_index("x")
    c = lax.axis_index("core")
    part = 2 * y + x
    score_scale = 1.0 / math.sqrt(HDIM)

    def swap(array, axes):
        return lax.all_to_all(array, axes, 0, 0)

    def flip(array, axis):
        return lax.ppermute(array, axis, [(0, 1), (1, 0)])

    def in_order(own, other, bit):
        return jnp.where(bit == 0, own, other), jnp.where(bit == 0, other, own)

    def absolute(pieces):
        whole = jnp.zeros((planes,) + pieces[0].shape, pieces[0].dtype)
        for step, piece in enumerate(pieces):
            first = ((z + step) % planes,) + (0,) * piece.ndim
            whole = lax.dynamic_update_slice(whole, piece[None], first)
        return whole

    def gather_rows(array, axes):
        return swap(jnp.broadcast_to(array, (4,) + array.shape), axes)

    def rows_at(bits, size):
        return jnp.stack([jnp.asarray(b, jnp.int32) for b in bits]).reshape(-1, size)

    qkv_slices = qkv_weight.reshape(shard_rows, 3, 4, quarter)
    qkv_slices = jnp.pad(qkv_slices, ((0, 0), (0, 0), (0, 0), (0, padded - quarter)))
    qkv_slices = qkv_slices.transpose(2, 0, 1, 3).reshape(4, shard_rows, 2, half_wide)
    qkv_slices = qkv_slices.transpose(0, 2, 1, 3).reshape(PLANE, shard_rows, half_wide)
    owned = jnp.concatenate([mixer_gain, dense_gain, conv_taps.reshape(-1)])
    owned_size = owned.shape[0]
    owned = jnp.pad(owned.reshape(1, -1), ((0, 1), (0, half_wide - owned_size)))
    owned = jnp.broadcast_to(owned, (PLANE, 2, half_wide))
    qkv_slices, gateup_weight, down_weight, out_weight = fence(
        jnp.concatenate([qkv_slices, owned], 1), gateup_weight, down_weight, out_weight
    )

    lines = []
    for d in range(count):
        lines.append(2 * planes * (d % PLANE // 2) + 2 * (d // PLANE) + d % 2)
    out_piece = lax.ppermute(out_weight, ALL, [(lines[d], d) for d in range(count)])
    before = lax.ppermute(tokens[rows - HALO :], ALL, [(d, d + 1) for d in range(count - 1)])

    qkv_piece = swap(qkv_slices, OCTET)
    gateup_slices = gateup_weight.reshape(shard_rows, 2, planes, 4, hidden_part // planes)
    gateup_slices = gateup_slices.transpose(3, 1, 0, 2, 4)
    gateup_slices = gateup_slices.reshape(PLANE, shard_rows, hidden_part)
    gateup_slices = jnp.pad(gateup_slices, ((0, 0), (0, 0), (0, hidden_wide - hidden_part)))
    qkv_piece, gateup_slices, tokens_now, before = fence(
        qkv_piece, gateup_slices, tokens, before
    )
    out_all = lax.all_gather(out_piece, LINE)
    small = [qkv_piece[:, shard_rows, :owned_size]]
    qkv_piece, small[0] = fence(qkv_piece[:, :shard_rows].reshape(octet_rows, half_wide), small[0])

    qkv_pieces, qkv_others = [qkv_piece], []
    onward = [(i, (i - 1) % planes) for i in range(planes)]
    for step in range(1, planes):
        qkv_next = lax.ppermute(qkv_pieces[-1], "z", onward)
        if step == 1:
            gateup_piece = swap(gateup_slices, OCTET).reshape(octet_rows, hidden_wide)
            for by in range(1, planes):
                shift = [(i, (i - by) % planes) for i in range(planes)]
                small.append(lax.ppermute(small[0], "z", shift))
            qkv_next, gateup_piece, tokens_now, small = fence(
                qkv_next, gateup_piece, tokens_now, small
            )
            token_group = gather_rows(jnp.concatenate([before, tokens_now]), SQUARE)
        elif step < planes - 1:
            (qkv_next,) = fence(qkv_next)
        else:
            small = absolute(small).astype(f32)
            gain_one = small[:, :, :shard_rows].reshape(1, width)
            gain_two = small[:, :, shard_rows : 2 * shard_rows].reshape(width)
            taps = small[:, :, 2 * shard_rows :].reshape(count, 3, tap_columns).transpose(1, 0, 2)
            taps = taps.reshape(3, 3, 4, quarter)
            taps = lax.dynamic_index_in_dim(taps, part, 2, keepdims=False)
            taps = jnp.pad(taps, ((0, 0), (0, 0), (0, padded - quarter)))
            taps = taps.reshape(3, 3 * padded)
            cotangent_now = jnp.broadcast_to(cotangent, (4,) + cotangent.shape)
            out = fence(qkv_next, cotangent_now, token_group, gateup_piece, gain_one, gain_two, taps)
            qkv_next, cotangent_now, token_group, gateup_piece, gain_one, gain_two, taps = out
        qkv_others.append(flip(qkv_pieces[-1], "core"))
        qkv_pieces.append(qkv_next)
    qkv_pieces, qkv_others, down_piece, cotangent_now = fence(
        qkv_pieces, qkv_others, down_weight, cotangent_now
    )
    gateup_all = lax.all_gather(gateup_piece, LINE)
    down_all = lax.all_gather(down_piece, LINE).reshape(hidden_part, width)
    qkv_others.append(flip(qkv_pieces[-1], "core"))
    (qkv_others,) = fence(qkv_others)
    out_full = jnp.pad(out_all.reshape(quarter, width), ((0, padded - quarter), (0, 0)))

    padded_segments = jnp.concatenate([jnp.full((HALO,), -1, jnp.int32), segments])
    seg_rows = jnp.stack(
        [
            lax.dynamic_slice_in_dim(padded_segments, (PLANE * z + 2 * b + c) * rows, ext)
            for b in range(4)
        ]
    )
    seg_keys = jnp.stack(
        [
            seg_rows[:, HALO - WINDOW + s * WINDOW : HALO + WINDOW + s * WINDOW]
            for s in range(subs)
        ],
        1,
    )
    seg_rows = jnp.broadcast_to(seg_rows[:, :, None], (4, ext, LANES))

    cotangent_group = swap(cotangent_now, SQUARE).reshape(4 * rows, width)
    where_qkv = []
    for own in range(2):
        for step in range(planes):
            where_qkv += [c ^ own, (z + step) % planes * octet_rows]
    attended, projected, qkv_full, normed_group = attend(
        rows_at(where_qkv, 2),
        token_group,
        gain_one,
        taps,
        seg_rows,
        seg_keys,
        qkv_pieces + qkv_others,
        octet_rows,
        score_scale,
    )
    attended = attended.reshape(4 * rows, padded)
    attended, normed_group, cotangent_group = fence(attended, normed_group, cotangent_group)
    mixer_out = plain(attended, out_full).astype(bf16).reshape(4, rows, width)

    mixer_sum = swap(mixer_out, SQUARE)
    own_tokens = tokens.astype(f32)
    residual = own_tokens + jnp.sum(mixer_sum.astype(f32), 0)
    normed_dense = rms_scale(residual, gain_two).astype(bf16)
    dense_group = gather_rows(normed_dense, SQUARE).reshape(4 * rows, width)

    gateup_chunk = octet_rows
    where_gateup = [k for i in range(planes) for h in range(2) for k in (h, i * gateup_chunk)]
    gateup_all = gateup_all.reshape(-1, hidden_wide)
    where_gateup = rows_at(where_gateup, 2)
    hidden, inner = dense(where_gateup, dense_group, gateup_all, gateup_chunk)
    hidden, inner, cotangent_group = fence(hidden, inner, cotangent_group)
    down_grad = down_gradient(hidden, cotangent_group, hidden_part)
    inner, cotangent_group, down_grad, hidden = fence(inner, cotangent_group, down_grad, hidden)
    down_mine = lax.psum_scatter(
        down_grad.reshape(2 * planes, down_rows, width), LINE, scatter_dimension=0
    )
    grad_dense, grad_inner = fence(
        *dense_back(where_gateup, cotangent_group, inner, gateup_all, gateup_chunk, down_all)
    )

    def scatter_line(array):
        return lax.psum_scatter(
            array.reshape((2 * planes,) + array.shape[2:]), LINE, scatter_dimension=0
        )

    grad_dense = swap(grad_dense.reshape(4, rows, width), SQUARE)
    gateup_grad = weight_grad(dense_group, grad_inner, planes, octet_rows, "gateup_grad")
    grad_dense, gateup_grad, hidden, down_all = fence(grad_dense, gateup_grad, hidden, down_all)
    gateup_mine = scatter_line(gateup_grad)

    unused, rms_back = jax.vjp(rms_scale, residual, gain_two)
    grad_residual, dense_gain_sum = rms_back(jnp.sum(grad_dense.astype(f32), 0))
    grad_residual = grad_residual + cotangent.astype(f32)
    grad_branch = gather_rows(grad_residual.astype(bf16), SQUARE)
    dense_rows = dense_out(hidden, down_all).reshape(4, rows, width)
    grad_branch, out_full, dense_rows, down_mine = fence(
        grad_branch, out_full, dense_rows, down_mine
    )
    dense_sum = swap(dense_rows, SQUARE)

    grad_projected, grad_taps = attend_back(
        grad_branch, out_full, projected, taps, seg_rows, seg_keys, score_scale
    )
    grad_normed, grad_halo = normed_grad(grad_projected, qkv_full)
    grad_projected, grad_normed, grad_halo, dense_sum = fence(
        grad_projected, grad_normed, grad_halo, dense_sum
    )

    halo_sum = swap(grad_halo, SQUARE)
    grad_projected = grad_projected.reshape(4 * ext, 3 * padded)
    normed_rows = normed_group.reshape(4 * ext, width)
    qkv_grad = weight_grad(normed_rows, grad_projected, planes, octet_rows, "qkv_grad")
    grad_branch = grad_branch.reshape(4 * rows, width)
    out = fence(qkv_grad, grad_normed, halo_sum, attended, grad_branch, gateup_mine)
    qkv_grad, grad_normed, halo_sum, attended, grad_branch, gateup_mine = out
    qkv_part = scatter_line(qkv_grad)

    normed_sum = swap(grad_normed, SQUARE)
    late = jnp.sum(halo_sum.astype(f32), 0).astype(bf16)
    late = lax.ppermute(late, ALL, [(d, d - 1) for d in range(1, count)])
    out_grad = contract_first(attended, grad_branch)[:quarter].astype(bf16)
    layer_out = (residual + jnp.sum(dense_sum.astype(f32), 0)).astype(bf16)
    normed_sum, late, gateup_mine, layer_out, out_grad = fence(
        normed_sum, late, gateup_mine, layer_out, out_grad
    )

    gateup_mine = swap(gateup_mine.reshape(PLANE, shard_rows, hidden_wide), OCTET)
    grad_normed = jnp.sum(normed_sum.astype(f32), 0)
    grad_normed = grad_normed + jnp.pad(late.astype(f32), ((rows - HALO, 0), (0, 0)))
    unused, mixer_back = jax.vjp(rms_scale, own_tokens, gain_one.reshape(width))
    grad_rows, mixer_gain_sum = mixer_back(grad_normed)
    input_grad = grad_residual + grad_rows

    grad_taps = grad_taps[:3].reshape(3, 3, 1, padded)[..., :quarter]
    grad_taps = lax.dynamic_update_slice(
        jnp.zeros((3, 3, 4, quarter), f32), grad_taps, (0, 0, part, 0)
    )
    grad_taps = grad_taps.reshape(3, count, tap_columns).transpose(1, 0, 2)
    sums = jnp.concatenate(
        [
            mixer_gain_sum.reshape(count, shard_rows),
            dense_gain_sum.reshape(count, shard_rows),
            grad_taps.reshape(count, 3 * tap_columns),
        ],
        1,
    )
    sums = sums.reshape(planes, PLANE, owned_size).transpose(1, 0, 2).astype(bf16)
    gateup_mine, sums, input_grad = fence(gateup_mine, sums, input_grad)

    sums, qkv_part, out_grad = fence(swap(sums, OCTET), qkv_part, out_grad)
    out_mine = lax.psum_scatter(
        out_grad.reshape(2 * planes, shard_rows, width), LINE, scatter_dimension=0
    )
    qkv_mine = swap(qkv_part.reshape(PLANE, shard_rows, half_wide), OCTET)
    sums = jnp.sum(sums.astype(f32), 0)
    parts = []
    for by in range(1, planes):
        sent = lax.dynamic_index_in_dim(sums, (z + by) % planes, 0, keepdims=False).astype(bf16)
        parts.append(lax.ppermute(sent, "z", [(i, (i + by) % planes) for i in range(planes)]))
    sums = lax.dynamic_index_in_dim(sums, z, 0, keepdims=False)
    for arrived in parts:
        sums = sums + arrived.astype(f32)
    gateup_mine = gateup_mine[:, :, :hidden_part]
    gateup_mine = gateup_mine.reshape(4, 2, shard_rows, planes, hidden_part // planes)
    gateup_mine = gateup_mine.transpose(2, 1, 3, 0, 4).reshape(shard_rows, 2 * hidden_width)
    gateup_mine = gateup_mine.astype(f32)
    qkv_mine, sums, gateup_mine = fence(qkv_mine, sums, gateup_mine)
    qkv_mine = qkv_mine.reshape(4, 2, shard_rows, half_wide).transpose(2, 0, 1, 3)
    qkv_mine = qkv_mine.reshape(shard_rows, 4, 3, padded)[..., :quarter].transpose(0, 2, 1, 3)
    qkv_mine = qkv_mine.reshape(shard_rows, 3 * width).astype(f32)
    out_mine = lax.ppermute(out_mine, ALL, [(d, lines[d]) for d in range(count)])
    return (
        layer_out,
        input_grad,
        sums[:shard_rows],
        qkv_mine,
        sums[2 * shard_rows :].reshape(3, tap_columns),
        out_mine.astype(f32),
        sums[shard_rows : 2 * shard_rows],
        gateup_mine,
        down_mine.astype(f32),
    )


def solution(mesh):
    planes = mesh.devices.size // PLANE
    split = Mesh(mesh.devices.reshape(planes, 2, 2, 2), ALL)
    over_rows = P(ALL, None)
    over_columns = P(None, ALL)
    return jax.shard_map(
        functools.partial(layer, planes),
        mesh=split,
        in_specs=(
            over_rows,
            P(),
            over_rows,
            P(ALL),
            over_rows,
            over_columns,
            over_rows,
            P(ALL),
            over_rows,
            over_rows,
        ),
        out_specs=(
            over_rows,
            over_rows,
            P(ALL),
            over_rows,
            over_columns,
            over_rows,
            P(ALL),
            over_rows,
            over_rows,
        ),
        check_vma=False,
    )
```

```python
import functools
import math

import jax
import jax.numpy as jnp
from jax import lax
from jax.experimental import pallas as pl
from jax.experimental.pallas import tpu as pltpu
from jax.sharding import Mesh, PartitionSpec as P

HDIM = 64
WINDOW = 64
HALO = 80
LANES = 128
PLANE = 8

eps_norm = 1e-05
masked_score = -1e30
bf16 = jnp.bfloat16
f32 = jnp.float32
MIB = 1024 * 1024
TILE = 256
ALL = ("z", "y", "x", "core")
SQUARE = ("y", "x")
OCTET = ("y", "x", "core")
LINE = ("z", "core")


def rms_scale(values, gains):
    inverse = lax.rsqrt(jnp.mean(values * values, axis=-1, keepdims=True) + eps_norm)
    return values * inverse * gains


def contract_last(left_side, right_side):
    return lax.dot_general(
        left_side, right_side, (((1,), (1,)), ((), ())), preferred_element_type=f32
    )


def contract_first(left_side, right_side):
    return lax.dot_general(
        left_side, right_side, (((0,), (0,)), ((), ())), preferred_element_type=f32
    )


def plain(left_side, right_side):
    return jnp.dot(left_side, right_side, preferred_element_type=f32)


def shifted_down(values, by):
    return pltpu.roll(values, by, 0)


def shifted_up(values, by):
    return pltpu.roll(values, values.shape[0] - by, 0)


def gate_of(values, taps, same_one, same_two):
    conv = (
        taps[0:1] * values
        + taps[1:2] * (same_one * shifted_down(values, 1))
        + taps[2:3] * (same_two * shifted_down(values, 2))
    )
    return conv, jax.nn.sigmoid(values)


def by_head(values):
    lane = lax.broadcasted_iota(jnp.int32, values.shape, 1)
    zero = jnp.zeros_like(values)
    return jnp.concatenate(
        [jnp.where(lane < HDIM, values, zero), jnp.where(lane < HDIM, zero, values)], 0
    )


def join_heads(values):
    half = values.shape[0] // 2
    lane = lax.broadcasted_iota(jnp.int32, (half, values.shape[1]), 1)
    return jnp.where(lane < HDIM, values[:half], values[half:])


def block_masks(seg_ref, keys_ref, subs):
    span = 2 * WINDOW
    row = lax.broadcasted_iota(jnp.int32, (WINDOW, span), 0)
    col = lax.broadcasted_iota(jnp.int32, (WINDOW, span), 1)
    near = (col > row) & (col <= row + WINDOW)
    masks = []
    for sub in range(subs):
        first = HALO + sub * WINDOW
        same = seg_ref[0, first : first + WINDOW] == keys_ref[0, sub : sub + 1]
        masks.append(near & same)
    return jnp.concatenate([mask for mask in masks for unused in range(2)], 0)


def same_rows(seg_ref):
    seg = seg_ref[0]
    same_one = (seg == shifted_down(seg, 1)).astype(f32)
    same_two = (seg == shifted_down(seg, 2)).astype(f32)
    return same_one, same_two


def pair_probs(queries, keysets, mask, score_scale):
    scores = jnp.concatenate([contract_last(q, k) for q, k in zip(queries, keysets)], 0)
    scores = jnp.where(mask, scores * score_scale, masked_score)
    exponent = jnp.exp(scores - jnp.max(scores, axis=-1, keepdims=True))
    return exponent * (1.0 / jnp.sum(exponent, axis=-1, keepdims=True))


def cut(values, subs, first, size):
    return [values[first + s * WINDOW : first + s * WINDOW + size] for s in range(subs)]


def parts_of(values, subs):
    return jnp.split(values, subs, 0)


def place_pieces(refs, chunk, where_ref, row, target, sems):
    copies = []
    for ref in refs:
        for first in range(0, ref.shape[0] // chunk * chunk, chunk):
            spot = pl.multiple_of(where_ref[row + len(copies), 1], 16)
            copy = pltpu.make_async_copy(
                ref.at[first : first + chunk],
                target.at[where_ref[row + len(copies), 0], pl.ds(spot, chunk)],
                sems.at[row + len(copies)],
            )
            copy.start()
            copies.append(copy)
    return copies


def attend_kernel(
    where_ref,
    tokens_ref,
    gain_ref,
    taps_ref,
    seg_ref,
    keys_ref,
    *rest,
    n,
    chunk,
    subs,
    score_scale,
):
    piece_refs, (out_ref, proj_ref, weight_ref, normed_ref, sems) = rest[:n], rest[n:]

    @pl.when(pl.program_id(0) == 0)
    def fetch():
        for copy in place_pieces(piece_refs, chunk, where_ref, 0, weight_ref, sems):
            copy.wait()

    normed_ref[0] = rms_scale(tokens_ref[0].astype(f32), gain_ref[...]).astype(bf16)
    half_wide = weight_ref.shape[2]
    for half in range(2):
        proj_ref[0, :, half * half_wide : (half + 1) * half_wide] = plain(
            normed_ref[0], weight_ref[half]
        )
    pairs = 2 * half_wide // (3 * LANES)
    same_one, same_two = same_rows(seg_ref)
    mask = block_masks(seg_ref, keys_ref, subs)
    first_key = HALO - WINDOW
    for pair in range(pairs):
        mixed = []
        for kind in range(3):
            at = (kind * pairs + pair) * LANES
            conv, sig = gate_of(
                proj_ref[0, :, at : at + LANES], taps_ref[:, at : at + LANES], same_one, same_two
            )
            mixed.append((conv * sig).astype(bf16))
        queries = [by_head(q) for q in cut(mixed[0], subs, HALO, WINDOW)]
        keysets = cut(mixed[1], subs, first_key, 2 * WINDOW)
        valuesets = cut(mixed[2], subs, first_key, 2 * WINDOW)
        weights = parts_of(pair_probs(queries, keysets, mask, score_scale).astype(bf16), subs)
        for sub in range(subs):
            out_ref[0, sub * WINDOW : (sub + 1) * WINDOW, pair * LANES : (pair + 1) * LANES] = (
                join_heads(plain(weights[sub], valuesets[sub])).astype(bf16)
            )


def attend_back_kernel(
    branch_ref, out_weight_ref, proj_ref, taps_ref, seg_ref, keys_ref, out_ref, tap_ref, *, subs, score_scale
):
    @pl.when(pl.program_id(0) == 0)
    def clear():
        tap_ref[...] = jnp.zeros_like(tap_ref)

    grad_attended = contract_last(branch_ref[0], out_weight_ref[...]).astype(bf16)
    pairs = proj_ref.shape[2] // (3 * LANES)
    same_one, same_two = same_rows(seg_ref)
    mask = block_masks(seg_ref, keys_ref, subs)
    first_key = HALO - WINDOW
    for pair in range(pairs):
        values, convs, sigs, mixed = [], [], [], []
        for kind in range(3):
            at = (kind * pairs + pair) * LANES
            value = proj_ref[0, :, at : at + LANES]
            conv, sig = gate_of(value, taps_ref[:, at : at + LANES], same_one, same_two)
            values.append(value)
            convs.append(conv)
            sigs.append(sig)
            mixed.append((conv * sig).astype(bf16))
        queries = [by_head(q) for q in cut(mixed[0], subs, HALO, WINDOW)]
        keysets = cut(mixed[1], subs, first_key, 2 * WINDOW)
        valuesets = cut(mixed[2], subs, first_key, 2 * WINDOW)
        grads = [
            by_head(g)
            for g in cut(grad_attended[:, pair * LANES : (pair + 1) * LANES], subs, 0, WINDOW)
        ]
        probs = pair_probs(queries, keysets, mask, score_scale)
        grad_probs = jnp.concatenate([contract_last(g, v) for g, v in zip(grads, valuesets)], 0)
        inner = jnp.sum(probs * grad_probs, axis=-1, keepdims=True)
        grad_scores = parts_of((probs * (grad_probs - inner)).astype(bf16), subs)
        weights = parts_of(probs.astype(bf16), subs)
        grad_queries = [
            join_heads(plain(g, k)) * score_scale for g, k in zip(grad_scores, keysets)
        ]
        grad_keys = [contract_first(g, q) * score_scale for g, q in zip(grad_scores, queries)]
        grad_values = [contract_first(w, g) for w, g in zip(weights, grads)]

        def overlapped(parts):
            rows = [jnp.zeros((first_key, LANES), f32), parts[0][:WINDOW]]
            for sub in range(1, subs):
                rows.append(parts[sub - 1][WINDOW:] + parts[sub][:WINDOW])
            rows.append(parts[subs - 1][WINDOW:])
            return jnp.concatenate(rows, 0)

        grads_mixed = (
            jnp.concatenate([jnp.zeros((HALO, LANES), f32)] + grad_queries, 0),
            overlapped(grad_keys),
            overlapped(grad_values),
        )
        for kind in range(3):
            at = (kind * pairs + pair) * LANES
            taps = taps_ref[:, at : at + LANES]
            through = grads_mixed[kind] * sigs[kind]
            one = same_one * through
            two = same_two * through
            summed = (
                through * convs[kind] * (1.0 - sigs[kind])
                + taps[0:1] * through
                + taps[1:2] * shifted_up(one, 1)
                + taps[2:3] * shifted_up(two, 2)
            )
            out_ref[0, :, at : at + LANES] = summed.astype(bf16)
            value = values[kind]
            tap_ref[0:1, at : at + LANES] += jnp.sum(through * value, 0, keepdims=True)
            tap_ref[1:2, at : at + LANES] += jnp.sum(
                one * shifted_down(value, 1), 0, keepdims=True
            )
            tap_ref[2:3, at : at + LANES] += jnp.sum(
                two * shifted_down(value, 2), 0, keepdims=True
            )


def attention_specs(rows, columns, subs):
    return [
        pl.BlockSpec((3, columns), lambda b: (0, 0)),
        pl.BlockSpec((1, rows, LANES), lambda b: (b, 0, 0)),
        pl.BlockSpec((1, subs, 2 * WINDOW), lambda b: (b, 0, 0)),
    ]


def attend(where, tokens, gain, taps, seg_rows, seg_keys, pieces, chunk, score_scale):
    blocks, rows, width = tokens.shape
    columns = taps.shape[1]
    subs = seg_keys.shape[1]
    copies = sum(p.shape[0] // chunk for p in pieces)
    return pl.pallas_call(
        functools.partial(
            attend_kernel, n=len(pieces), chunk=chunk, subs=subs, score_scale=score_scale
        ),
        grid=(blocks,),
        out_shape=(
            jax.ShapeDtypeStruct((blocks, rows - HALO, columns // 3), bf16),
            jax.ShapeDtypeStruct((blocks, rows, columns), f32),
            jax.ShapeDtypeStruct((2, width, columns // 2), bf16),
            jax.ShapeDtypeStruct((blocks, rows, width), bf16),
        ),
        in_specs=[
            pl.BlockSpec(memory_space=pltpu.SMEM),
            pl.BlockSpec((1, rows, width), lambda b: (b, 0, 0)),
            pl.BlockSpec((1, width), lambda b: (0, 0)),
        ]
        + attention_specs(rows, columns, subs)
        + [pl.BlockSpec(memory_space=pl.ANY)] * len(pieces),
        out_specs=(
            pl.BlockSpec((1, rows - HALO, columns // 3), lambda b: (b, 0, 0)),
            pl.BlockSpec((1, rows, columns), lambda b: (b, 0, 0)),
            pl.BlockSpec((2, width, columns // 2), lambda b: (0, 0, 0)),
            pl.BlockSpec((1, rows, width), lambda b: (b, 0, 0)),
        ),
        scratch_shapes=[pltpu.SemaphoreType.DMA((copies,))],
        compiler_params=pltpu.CompilerParams(vmem_limit_bytes=60 * MIB),
        cost_estimate=pl.CostEstimate(
            flops=20 * 10**9, bytes_accessed=20 * 10**6, transcendentals=0
        ),
        name="attend",
    )(where, tokens, gain, taps, seg_rows, seg_keys, *pieces)


def attend_back(branch, out_weight, projected, taps, seg_rows, seg_keys, score_scale):
    blocks, rows, columns = projected.shape
    width = branch.shape[2]
    subs = seg_keys.shape[1]
    return pl.pallas_call(
        functools.partial(attend_back_kernel, subs=subs, score_scale=score_scale),
        grid=(blocks,),
        out_shape=(
            jax.ShapeDtypeStruct((blocks, rows, columns), bf16),
            jax.ShapeDtypeStruct((8, columns), f32),
        ),
        in_specs=[
            pl.BlockSpec((1, rows - HALO, width), lambda b: (b, 0, 0)),
            pl.BlockSpec((columns // 3, width), lambda b: (0, 0)),
            pl.BlockSpec((1, rows, columns), lambda b: (b, 0, 0)),
        ]
        + attention_specs(rows, columns, subs),
        out_specs=(
            pl.BlockSpec((1, rows, columns), lambda b: (b, 0, 0)),
            pl.BlockSpec((8, columns), lambda b: (0, 0)),
        ),
        compiler_params=pltpu.CompilerParams(vmem_limit_bytes=60 * MIB),
        cost_estimate=pl.CostEstimate(
            flops=20 * 10**9, bytes_accessed=20 * 10**6, transcendentals=0
        ),
        name="attend_back",
    )(branch, out_weight, projected, taps, seg_rows, seg_keys)


def dense_kernel(where_ref, dense_ref, gate_hbm, hidden_ref, inner_ref, gate_ref, sems, *, chunk):
    rows, hidden_wide = hidden_ref.shape
    count = gate_hbm.shape[0] // chunk
    ready = []
    for part, columns in enumerate((slice(0, TILE), slice(TILE, hidden_wide))):
        copies = []
        for index in range(count):
            spot = pl.multiple_of(where_ref[index, 1], 16)
            copy = pltpu.make_async_copy(
                gate_hbm.at[index * chunk : (index + 1) * chunk, columns],
                gate_ref.at[where_ref[index, 0], pl.ds(spot, chunk), columns],
                sems.at[part * count + index],
            )
            copy.start()
            copies.append(copy)
        ready.append(copies)

    def units(begin, end):
        @pl.loop(0, rows // TILE)
        def block(index):
            own = pl.ds(pl.multiple_of(index * TILE, TILE), TILE)
            normed = dense_ref[own, :]
            for first in range(begin, end, TILE):
                unit = slice(first, first + TILE)
                gate = plain(normed, gate_ref[0, :, unit])
                up = plain(normed, gate_ref[1, :, unit])
                sig = jax.nn.sigmoid(gate)
                silu = gate * sig
                hidden_ref[own, unit] = (silu * up).astype(bf16)
                inner_ref[0, own, unit] = up * (sig * (1.0 + gate * (1.0 - sig)))
                inner_ref[1, own, unit] = silu

    for copy in ready[0]:
        copy.wait()
    units(0, TILE)
    for copy in ready[1]:
        copy.wait()
    units(TILE, hidden_wide)


def fetch_down(down_hbm, down_ref, sem):
    real = down_hbm.shape[0]
    copy = pltpu.make_async_copy(down_hbm, down_ref.at[:real], sem)
    copy.start()
    if real < down_ref.shape[0]:
        down_ref[real:] = jnp.zeros((down_ref.shape[0] - real, down_ref.shape[1]), bf16)
    return copy


def dense_back_kernel(
    where_ref,
    cotangent_ref,
    inner_hbm,
    gate_hbm,
    down_hbm,
    grad_ref,
    joined_ref,
    down_ref,
    inner_ref,
    gate_ref,
    sems,
    *,
    chunk,
):
    rows, width = cotangent_ref.shape
    hidden_wide = joined_ref.shape[2]
    count = gate_hbm.shape[0] // chunk
    down_copy = fetch_down(down_hbm, down_ref, sems.at[count])
    inner_copies = []
    for index in range(rows // TILE):
        own = slice(index * TILE, (index + 1) * TILE)
        copy = pltpu.make_async_copy(
            inner_hbm.at[:, own], inner_ref.at[:, own], sems.at[count + 1 + index]
        )
        copy.start()
        inner_copies.append(copy)
    gate_copies = place_pieces([gate_hbm], chunk, where_ref, 0, gate_ref, sems)
    down_copy.wait()
    for index in range(rows // TILE):
        inner_copies[index].wait()
        own = slice(index * TILE, (index + 1) * TILE)
        cotangent = cotangent_ref[own, :]
        for first in range(0, hidden_wide, TILE):
            unit = slice(first, first + TILE)
            grad = contract_last(cotangent, down_ref[unit])
            joined_ref[0, own, unit] = (grad * inner_ref[0, own, unit]).astype(bf16)
            joined_ref[1, own, unit] = (grad * inner_ref[1, own, unit]).astype(bf16)
    for copy in gate_copies:
        copy.wait()

    @pl.loop(0, rows // TILE)
    def block(index):
        own = pl.ds(pl.multiple_of(index * TILE, TILE), TILE)
        gates = joined_ref[0, own, :]
        ups = joined_ref[1, own, :]
        for first in range(0, width, TILE):
            unit = slice(first, first + TILE)
            grad_ref[own, unit] = (
                contract_last(gates, gate_ref[0, unit]) + contract_last(ups, gate_ref[1, unit])
            ).astype(bf16)


def dense_out_kernel(hidden_ref, down_hbm, out_ref, down_ref, sem):
    fetch_down(down_hbm, down_ref, sem).wait()

    @pl.loop(0, hidden_ref.shape[0] // TILE)
    def block(index):
        own = pl.ds(pl.multiple_of(index * TILE, TILE), TILE)
        out_ref[own, :] = plain(hidden_ref[own, :], down_ref[...]).astype(bf16)


def down_grad_kernel(hidden_ref, cotangent_ref, out_ref):
    out_ref[...] = contract_first(hidden_ref[...], cotangent_ref[...]).astype(bf16)[
        : out_ref.shape[0]
    ]


WHOLE = pl.BlockSpec(memory_space=pltpu.VMEM)
OUTSIDE = pl.BlockSpec(memory_space=pl.ANY)
SCALARS = pl.BlockSpec(memory_space=pltpu.SMEM)


def kernel_params(giga_flops):
    return dict(
        compiler_params=pltpu.CompilerParams(vmem_limit_bytes=60 * MIB),
        cost_estimate=pl.CostEstimate(
            flops=giga_flops * 10**9, bytes_accessed=20 * 10**6, transcendentals=0
        ),
    )


def dense(where, normed, gate, chunk):
    rows, width = normed.shape
    hidden_wide = gate.shape[1]
    return pl.pallas_call(
        functools.partial(dense_kernel, chunk=chunk),
        out_shape=(
            jax.ShapeDtypeStruct((rows, hidden_wide), bf16),
            jax.ShapeDtypeStruct((2, rows, hidden_wide), f32),
        ),
        in_specs=[SCALARS, WHOLE, OUTSIDE],
        out_specs=(WHOLE, WHOLE),
        scratch_shapes=[
            pltpu.VMEM((2, width, hidden_wide), bf16),
            pltpu.SemaphoreType.DMA((2 * (gate.shape[0] // chunk),)),
        ],
        name="dense",
        **kernel_params(15),
    )(where, normed, gate)


def dense_back(where, cotangent, inner, gate, chunk, down):
    rows, width = cotangent.shape
    hidden_wide = gate.shape[1]
    copies = 1 + rows // TILE + gate.shape[0] // chunk
    return pl.pallas_call(
        functools.partial(dense_back_kernel, chunk=chunk),
        out_shape=(
            jax.ShapeDtypeStruct((rows, width), bf16),
            jax.ShapeDtypeStruct((2, rows, hidden_wide), bf16),
        ),
        in_specs=[SCALARS, WHOLE, OUTSIDE, OUTSIDE, OUTSIDE],
        out_specs=(WHOLE, WHOLE),
        scratch_shapes=[
            pltpu.VMEM((hidden_wide, width), bf16),
            pltpu.VMEM((2, rows, hidden_wide), f32),
            pltpu.VMEM((2, width, hidden_wide), bf16),
            pltpu.SemaphoreType.DMA((copies,)),
        ],
        name="dense_back",
        **kernel_params(20),
    )(where, cotangent, inner, gate, down)


def dense_out(hidden, down):
    rows, hidden_wide = hidden.shape
    width = down.shape[1]
    return pl.pallas_call(
        dense_out_kernel,
        out_shape=jax.ShapeDtypeStruct((rows, width), bf16),
        in_specs=[WHOLE, OUTSIDE],
        out_specs=WHOLE,
        scratch_shapes=[pltpu.VMEM((hidden_wide, width), bf16), pltpu.SemaphoreType.DMA],
        name="dense_out",
        **kernel_params(8),
    )(hidden, down)


def down_gradient(hidden, cotangent, units):
    rows, hidden_wide = hidden.shape
    width = cotangent.shape[1]
    return pl.pallas_call(
        down_grad_kernel,
        grid=(2,),
        out_shape=jax.ShapeDtypeStruct((units, width), bf16),
        in_specs=[
            pl.BlockSpec((rows, hidden_wide), lambda h: (0, 0)),
            pl.BlockSpec((rows, width // 2), lambda h: (0, h)),
        ],
        out_specs=pl.BlockSpec((units, width // 2), lambda h: (0, h)),
        name="down_grad",
        **kernel_params(8),
    )(hidden, cotangent)


def normed_grad_kernel(grad_ref, weight_ref, out_ref, halo_ref):
    half_wide = weight_ref.shape[2]
    grads = grad_ref[0]
    product = (
        contract_last(grads[:, :half_wide], weight_ref[0])
        + contract_last(grads[:, half_wide:], weight_ref[1])
    ).astype(bf16)
    halo_ref[0] = product[:HALO]
    out_ref[0] = product[HALO:]


def normed_grad(grad_projected, weight):
    blocks, rows, columns = grad_projected.shape
    width = weight.shape[1]
    return pl.pallas_call(
        normed_grad_kernel,
        grid=(blocks,),
        out_shape=(
            jax.ShapeDtypeStruct((blocks, rows - HALO, width), bf16),
            jax.ShapeDtypeStruct((blocks, HALO, width), bf16),
        ),
        in_specs=[
            pl.BlockSpec((1, rows, columns), lambda b: (b, 0, 0)),
            pl.BlockSpec((2, width, columns // 2), lambda b: (0, 0, 0)),
        ],
        out_specs=(
            pl.BlockSpec((1, rows - HALO, width), lambda b: (b, 0, 0)),
            pl.BlockSpec((1, HALO, width), lambda b: (b, 0, 0)),
        ),
        name="normed_grad",
        **kernel_params(15),
    )(grad_projected, weight)


def weight_grad_kernel(left_ref, right_ref, out_ref):
    right = right_ref[...].reshape(right_ref.shape[-2:])
    product = contract_first(left_ref[...], right).astype(bf16)
    planes, unused, rows, columns = out_ref.shape
    out_ref[:, 0] = product[: planes * rows].reshape(planes, rows, columns)


def weight_grad(left, right, planes, rows, name):
    tokens, depth = left.shape
    columns = right.shape[-1] if right.ndim == 3 else right.shape[-1] // 2
    steps = 2 if planes * rows == depth else 1
    if right.ndim == 3:
        right_spec = pl.BlockSpec((1, tokens, columns), lambda h, k: (h, 0, 0))
    else:
        right_spec = pl.BlockSpec((tokens, columns), lambda h, k: (0, h))
    return pl.pallas_call(
        weight_grad_kernel,
        grid=(2, steps),
        out_shape=jax.ShapeDtypeStruct((planes, 2, rows, columns), bf16),
        in_specs=[pl.BlockSpec((tokens, depth // steps), lambda h, k: (0, k)), right_spec],
        out_specs=pl.BlockSpec((planes // steps, 1, rows, columns), lambda h, k: (k, h, 0, 0)),
        compiler_params=pltpu.CompilerParams(vmem_limit_bytes=60 * MIB),
        cost_estimate=pl.CostEstimate(
            flops=20 * 10**9, bytes_accessed=20 * 10**6, transcendentals=0
        ),
        name=name,
    )(left, right)


def fence(*values):
    return lax.optimization_barrier(values)


def layer(
    planes,
    tokens,
    segments,
    cotangent,
    mixer_gain,
    qkv_weight,
    conv_taps,
    out_weight,
    dense_gain,
    gateup_weight,
    down_weight,
):
    count = planes * PLANE
    rows, width = tokens.shape
    ext = HALO + rows
    subs = rows // WINDOW
    quarter = width // 4
    padded = -(-quarter // LANES) * LANES
    half_wide = 3 * padded // 2
    half_width = width // 2
    shard_rows = qkv_weight.shape[0]
    down_rows = down_weight.shape[0]
    square_rows = 4 * shard_rows
    octet_rows = PLANE * shard_rows
    hidden_width = down_rows * count
    hidden_part = hidden_width // 4
    hidden_wide = -(-hidden_part // 256) * 256
    tap_columns = conv_taps.shape[1]
    out_planes = planes // 4
    z = lax.axis_index("z")
    y = lax.axis_index("y")
    x = lax.axis_index("x")
    c = lax.axis_index("core")
    part = 2 * y + x
    score_scale = 1.0 / math.sqrt(HDIM)

    def swap(array, axes):
        return lax.all_to_all(array, axes, 0, 0)

    def flip(array, axis):
        return lax.ppermute(array, axis, [(0, 1), (1, 0)])

    def in_order(own, other, bit):
        return jnp.where(bit == 0, own, other), jnp.where(bit == 0, other, own)

    def absolute(pieces):
        whole = jnp.zeros((planes,) + pieces[0].shape, pieces[0].dtype)
        for step, piece in enumerate(pieces):
            first = ((z + step) % planes,) + (0,) * piece.ndim
            whole = lax.dynamic_update_slice(whole, piece[None], first)
        return whole

    def gather_rows(array, axes):
        return swap(jnp.broadcast_to(array, (4,) + array.shape), axes)

    def rows_at(bits, size):
        return jnp.stack([jnp.asarray(b, jnp.int32) for b in bits]).reshape(-1, size)

    qkv_slices = qkv_weight.reshape(shard_rows, 3, 4, quarter)
    qkv_slices = jnp.pad(qkv_slices, ((0, 0), (0, 0), (0, 0), (0, padded - quarter)))
    qkv_slices = qkv_slices.transpose(2, 0, 1, 3).reshape(4, shard_rows, 2, half_wide)
    qkv_slices = qkv_slices.transpose(0, 2, 1, 3).reshape(PLANE, shard_rows, half_wide)
    owned = jnp.concatenate([mixer_gain, dense_gain, conv_taps.reshape(-1)])
    owned_size = owned.shape[0]
    owned = jnp.pad(owned.reshape(1, -1), ((0, 1), (0, half_wide - owned_size)))
    owned = jnp.broadcast_to(owned, (PLANE, 2, half_wide))
    qkv_slices, gateup_weight, down_weight, out_weight = fence(
        jnp.concatenate([qkv_slices, owned], 1), gateup_weight, down_weight, out_weight
    )

    lines = []
    for d in range(count):
        lines.append(2 * planes * (d % PLANE // 2) + 2 * (d // PLANE) + d % 2)
    out_piece = lax.ppermute(out_weight, ALL, [(lines[d], d) for d in range(count)])
    before = lax.ppermute(tokens[rows - HALO :], ALL, [(d, d + 1) for d in range(count - 1)])

    qkv_piece = swap(qkv_slices, OCTET)
    gateup_slices = gateup_weight.reshape(shard_rows, 2, planes, 4, hidden_part // planes)
    gateup_slices = gateup_slices.transpose(3, 1, 0, 2, 4)
    gateup_slices = gateup_slices.reshape(PLANE, shard_rows, hidden_part)
    gateup_slices = jnp.pad(gateup_slices, ((0, 0), (0, 0), (0, hidden_wide - hidden_part)))
    qkv_piece, gateup_slices, tokens_now, before = fence(
        qkv_piece, gateup_slices, tokens, before
    )
    out_all = lax.all_gather(out_piece, LINE)
    small = [qkv_piece[:, shard_rows, :owned_size]]
    qkv_piece, small[0] = fence(qkv_piece[:, :shard_rows].reshape(octet_rows, half_wide), small[0])

    qkv_pieces, qkv_others = [qkv_piece], []
    onward = [(i, (i - 1) % planes) for i in range(planes)]
    for step in range(1, planes):
        qkv_next = lax.ppermute(qkv_pieces[-1], "z", onward)
        if step == 1:
            gateup_piece = swap(gateup_slices, OCTET).reshape(octet_rows, hidden_wide)
            for by in range(1, planes):
                shift = [(i, (i - by) % planes) for i in range(planes)]
                small.append(lax.ppermute(small[0], "z", shift))
            qkv_next, gateup_piece, tokens_now, small = fence(
                qkv_next, gateup_piece, tokens_now, small
            )
            token_group = gather_rows(jnp.concatenate([before, tokens_now]), SQUARE)
        elif step < planes - 1:
            (qkv_next,) = fence(qkv_next)
        else:
            small = absolute(small).astype(f32)
            gain_one = small[:, :, :shard_rows].reshape(1, width)
            gain_two = small[:, :, shard_rows : 2 * shard_rows].reshape(width)
            taps = small[:, :, 2 * shard_rows :].reshape(count, 3, tap_columns).transpose(1, 0, 2)
            taps = taps.reshape(3, 3, 4, quarter)
            taps = lax.dynamic_index_in_dim(taps, part, 2, keepdims=False)
            taps = jnp.pad(taps, ((0, 0), (0, 0), (0, padded - quarter)))
            taps = taps.reshape(3, 3 * padded)
            cotangent_now = jnp.broadcast_to(cotangent, (4,) + cotangent.shape)
            out = fence(qkv_next, cotangent_now, token_group, gateup_piece, gain_one, gain_two, taps)
            qkv_next, cotangent_now, token_group, gateup_piece, gain_one, gain_two, taps = out
        qkv_others.append(flip(qkv_pieces[-1], "core"))
        qkv_pieces.append(qkv_next)
    qkv_pieces, qkv_others, down_piece, cotangent_now = fence(
        qkv_pieces, qkv_others, down_weight, cotangent_now
    )
    gateup_all = lax.all_gather(gateup_piece, LINE)
    down_all = lax.all_gather(down_piece, LINE).reshape(hidden_part, width)
    qkv_others.append(flip(qkv_pieces[-1], "core"))
    (qkv_others,) = fence(qkv_others)
    out_full = jnp.pad(out_all.reshape(quarter, width), ((0, padded - quarter), (0, 0)))

    padded_segments = jnp.concatenate([jnp.full((HALO,), -1, jnp.int32), segments])
    seg_rows = jnp.stack(
        [
            lax.dynamic_slice_in_dim(padded_segments, (PLANE * z + 2 * b + c) * rows, ext)
            for b in range(4)
        ]
    )
    seg_keys = jnp.stack(
        [
            seg_rows[:, HALO - WINDOW + s * WINDOW : HALO + WINDOW + s * WINDOW]
            for s in range(subs)
        ],
        1,
    )
    seg_rows = jnp.broadcast_to(seg_rows[:, :, None], (4, ext, LANES))

    cotangent_group = swap(cotangent_now, SQUARE).reshape(4 * rows, width)
    where_qkv = []
    for own in range(2):
        for step in range(planes):
            where_qkv += [c ^ own, (z + step) % planes * octet_rows]
    attended, projected, qkv_full, normed_group = attend(
        rows_at(where_qkv, 2),
        token_group,
        gain_one,
        taps,
        seg_rows,
        seg_keys,
        qkv_pieces + qkv_others,
        octet_rows,
        score_scale,
    )
    attended = attended.reshape(4 * rows, padded)
    attended, normed_group, cotangent_group = fence(attended, normed_group, cotangent_group)
    mixer_out = plain(attended, out_full).astype(bf16).reshape(4, rows, width)

    mixer_sum = swap(mixer_out, SQUARE)
    own_tokens = tokens.astype(f32)
    residual = own_tokens + jnp.sum(mixer_sum.astype(f32), 0)
    normed_dense = rms_scale(residual, gain_two).astype(bf16)
    dense_group = gather_rows(normed_dense, SQUARE).reshape(4 * rows, width)

    gateup_chunk = octet_rows
    where_gateup = [k for i in range(planes) for h in range(2) for k in (h, i * gateup_chunk)]
    gateup_all = gateup_all.reshape(-1, hidden_wide)
    where_gateup = rows_at(where_gateup, 2)
    hidden, inner = dense(where_gateup, dense_group, gateup_all, gateup_chunk)
    hidden, inner, cotangent_group = fence(hidden, inner, cotangent_group)
    down_grad = down_gradient(hidden, cotangent_group, hidden_part)
    inner, cotangent_group, down_grad, hidden = fence(inner, cotangent_group, down_grad, hidden)
    down_mine = lax.psum_scatter(
        down_grad.reshape(2 * planes, down_rows, width), LINE, scatter_dimension=0
    )
    grad_dense, grad_inner = fence(
        *dense_back(where_gateup, cotangent_group, inner, gateup_all, gateup_chunk, down_all)
    )

    def scatter_line(array):
        return lax.psum_scatter(
            array.reshape((2 * planes,) + array.shape[2:]), LINE, scatter_dimension=0
        )

    grad_dense = swap(grad_dense.reshape(4, rows, width), SQUARE)
    gateup_grad = weight_grad(dense_group, grad_inner, planes, octet_rows, "gateup_grad")
    grad_dense, gateup_grad, hidden, down_all = fence(grad_dense, gateup_grad, hidden, down_all)
    gateup_mine = scatter_line(gateup_grad)

    unused, rms_back = jax.vjp(rms_scale, residual, gain_two)
    grad_residual, dense_gain_sum = rms_back(jnp.sum(grad_dense.astype(f32), 0))
    grad_residual = grad_residual + cotangent.astype(f32)
    grad_branch = gather_rows(grad_residual.astype(bf16), SQUARE)
    dense_rows = dense_out(hidden, down_all).reshape(4, rows, width)
    grad_branch, out_full, dense_rows, down_mine = fence(
        grad_branch, out_full, dense_rows, down_mine
    )
    dense_sum = swap(dense_rows, SQUARE)

    grad_projected, grad_taps = attend_back(
        grad_branch, out_full, projected, taps, seg_rows, seg_keys, score_scale
    )
    grad_normed, grad_halo = normed_grad(grad_projected, qkv_full)
    grad_projected, grad_normed, grad_halo, dense_sum = fence(
        grad_projected, grad_normed, grad_halo, dense_sum
    )

    halo_sum = swap(grad_halo, SQUARE)
    grad_projected = grad_projected.reshape(4 * ext, 3 * padded)
    normed_rows = normed_group.reshape(4 * ext, width)
    qkv_grad = weight_grad(normed_rows, grad_projected, planes, octet_rows, "qkv_grad")
    grad_branch = grad_branch.reshape(4 * rows, width)
    out = fence(qkv_grad, grad_normed, halo_sum, attended, grad_branch, gateup_mine)
    qkv_grad, grad_normed, halo_sum, attended, grad_branch, gateup_mine = out
    qkv_part = scatter_line(qkv_grad)

    normed_sum = swap(grad_normed, SQUARE)
    late = jnp.sum(halo_sum.astype(f32), 0).astype(bf16)
    late = lax.ppermute(late, ALL, [(d, d - 1) for d in range(1, count)])
    out_grad = contract_first(attended, grad_branch)[:quarter].astype(bf16)
    layer_out = (residual + jnp.sum(dense_sum.astype(f32), 0)).astype(bf16)
    normed_sum, late, gateup_mine, layer_out, out_grad = fence(
        normed_sum, late, gateup_mine, layer_out, out_grad
    )

    gateup_mine = swap(gateup_mine.reshape(PLANE, shard_rows, hidden_wide), OCTET)
    grad_normed = jnp.sum(normed_sum.astype(f32), 0)
    grad_normed = grad_normed + jnp.pad(late.astype(f32), ((rows - HALO, 0), (0, 0)))
    unused, mixer_back = jax.vjp(rms_scale, own_tokens, gain_one.reshape(width))
    grad_rows, mixer_gain_sum = mixer_back(grad_normed)
    input_grad = grad_residual + grad_rows

    grad_taps = grad_taps[:3].reshape(3, 3, 1, padded)[..., :quarter]
    grad_taps = lax.dynamic_update_slice(
        jnp.zeros((3, 3, 4, quarter), f32), grad_taps, (0, 0, part, 0)
    )
    grad_taps = grad_taps.reshape(3, count, tap_columns).transpose(1, 0, 2)
    sums = jnp.concatenate(
        [
            mixer_gain_sum.reshape(count, shard_rows),
            dense_gain_sum.reshape(count, shard_rows),
            grad_taps.reshape(count, 3 * tap_columns),
        ],
        1,
    )
    sums = sums.reshape(planes, PLANE, owned_size).transpose(1, 0, 2).astype(bf16)
    gateup_mine, sums, input_grad = fence(gateup_mine, sums, input_grad)

    sums, qkv_part, out_grad = fence(swap(sums, OCTET), qkv_part, out_grad)
    out_mine = lax.psum_scatter(
        out_grad.reshape(2 * planes, shard_rows, width), LINE, scatter_dimension=0
    )
    qkv_mine = swap(qkv_part.reshape(PLANE, shard_rows, half_wide), OCTET)
    sums = jnp.sum(sums.astype(f32), 0)
    parts = []
    for by in range(1, planes):
        sent = lax.dynamic_index_in_dim(sums, (z + by) % planes, 0, keepdims=False).astype(bf16)
        parts.append(lax.ppermute(sent, "z", [(i, (i + by) % planes) for i in range(planes)]))
    sums = lax.dynamic_index_in_dim(sums, z, 0, keepdims=False)
    for arrived in parts:
        sums = sums + arrived.astype(f32)
    gateup_mine = gateup_mine[:, :, :hidden_part]
    gateup_mine = gateup_mine.reshape(4, 2, shard_rows, planes, hidden_part // planes)
    gateup_mine = gateup_mine.transpose(2, 1, 3, 0, 4).reshape(shard_rows, 2 * hidden_width)
    gateup_mine = gateup_mine.astype(f32)
    qkv_mine, sums, gateup_mine = fence(qkv_mine, sums, gateup_mine)
    qkv_mine = qkv_mine.reshape(4, 2, shard_rows, half_wide).transpose(2, 0, 1, 3)
    qkv_mine = qkv_mine.reshape(shard_rows, 4, 3, padded)[..., :quarter].transpose(0, 2, 1, 3)
    qkv_mine = qkv_mine.reshape(shard_rows, 3 * width).astype(f32)
    out_mine = lax.ppermute(out_mine, ALL, [(d, lines[d]) for d in range(count)])
    return (
        layer_out,
        input_grad,
        sums[:shard_rows],
        qkv_mine,
        sums[2 * shard_rows :].reshape(3, tap_columns),
        out_mine.astype(f32),
        sums[shard_rows : 2 * shard_rows],
        gateup_mine,
        down_mine.astype(f32),
    )


def solution(mesh):
    planes = mesh.devices.size // PLANE
    split = Mesh(mesh.devices.reshape(planes, 2, 2, 2), ALL)
    over_rows = P(ALL, None)
    over_columns = P(None, ALL)
    return jax.shard_map(
        functools.partial(layer, planes),
        mesh=split,
        in_specs=(
            over_rows,
            P(),
            over_rows,
            P(ALL),
            over_rows,
            over_columns,
            over_rows,
            P(ALL),
            over_rows,
            over_rows,
        ),
        out_specs=(
            over_rows,
            over_rows,
            P(ALL),
            over_rows,
            over_columns,
            over_rows,
            P(ALL),
            over_rows,
            over_rows,
        ),
        check_vma=False,
    )
```

```python
import functools
import math

import jax
import jax.numpy as jnp
from jax import lax
from jax.experimental import pallas as pl
from jax.experimental.pallas import tpu as pltpu
from jax.sharding import Mesh, PartitionSpec as P

HDIM = 64
WINDOW = 64
HALO = 80
LANES = 128
PLANE = 8

eps_norm = 1e-05
masked_score = -1e30
bf16 = jnp.bfloat16
f32 = jnp.float32
MIB = 1024 * 1024
TILE = 256
ALL = ("z", "y", "x", "core")
SQUARE = ("y", "x")
OCTET = ("y", "x", "core")
LINE = ("z", "core")


def rms_scale(values, gains):
    inverse = lax.rsqrt(jnp.mean(values * values, axis=-1, keepdims=True) + eps_norm)
    return values * inverse * gains


def contract_last(left_side, right_side):
    return lax.dot_general(
        left_side, right_side, (((1,), (1,)), ((), ())), preferred_element_type=f32
    )


def contract_first(left_side, right_side):
    return lax.dot_general(
        left_side, right_side, (((0,), (0,)), ((), ())), preferred_element_type=f32
    )


def plain(left_side, right_side):
    return jnp.dot(left_side, right_side, preferred_element_type=f32)


def shifted_down(values, by):
    return pltpu.roll(values, by, 0)


def shifted_up(values, by):
    return pltpu.roll(values, values.shape[0] - by, 0)


def gate_of(values, taps, same_one, same_two):
    conv = (
        taps[0:1] * values
        + taps[1:2] * (same_one * shifted_down(values, 1))
        + taps[2:3] * (same_two * shifted_down(values, 2))
    )
    return conv, jax.nn.sigmoid(values)


def by_head(values):
    lane = lax.broadcasted_iota(jnp.int32, values.shape, 1)
    zero = jnp.zeros_like(values)
    return jnp.concatenate(
        [jnp.where(lane < HDIM, values, zero), jnp.where(lane < HDIM, zero, values)], 0
    )


def join_heads(values):
    half = values.shape[0] // 2
    lane = lax.broadcasted_iota(jnp.int32, (half, values.shape[1]), 1)
    return jnp.where(lane < HDIM, values[:half], values[half:])


def block_masks(seg_ref, keys_ref, subs):
    span = 2 * WINDOW
    row = lax.broadcasted_iota(jnp.int32, (WINDOW, span), 0)
    col = lax.broadcasted_iota(jnp.int32, (WINDOW, span), 1)
    near = (col > row) & (col <= row + WINDOW)
    masks = []
    for sub in range(subs):
        first = HALO + sub * WINDOW
        same = seg_ref[0, first : first + WINDOW] == keys_ref[0, sub : sub + 1]
        masks.append(near & same)
    return jnp.concatenate([mask for mask in masks for unused in range(2)], 0)


def same_rows(seg_ref):
    seg = seg_ref[0]
    same_one = (seg == shifted_down(seg, 1)).astype(f32)
    same_two = (seg == shifted_down(seg, 2)).astype(f32)
    return same_one, same_two


def pair_probs(queries, keysets, mask, score_scale):
    scores = jnp.concatenate([contract_last(q, k) for q, k in zip(queries, keysets)], 0)
    scores = jnp.where(mask, scores * score_scale, masked_score)
    exponent = jnp.exp(scores - jnp.max(scores, axis=-1, keepdims=True))
    return exponent * (1.0 / jnp.sum(exponent, axis=-1, keepdims=True))


def cut(values, subs, first, size):
    return [values[first + s * WINDOW : first + s * WINDOW + size] for s in range(subs)]


def parts_of(values, subs):
    return jnp.split(values, subs, 0)


def place_pieces(refs, chunk, where_ref, row, target, sems):
    copies = []
    for ref in refs:
        for first in range(0, ref.shape[0] // chunk * chunk, chunk):
            spot = pl.multiple_of(where_ref[row + len(copies), 1], 16)
            copy = pltpu.make_async_copy(
                ref.at[first : first + chunk],
                target.at[where_ref[row + len(copies), 0], pl.ds(spot, chunk)],
                sems.at[row + len(copies)],
            )
            copy.start()
            copies.append(copy)
    return copies


def attend_kernel(
    where_ref,
    tokens_ref,
    gain_ref,
    taps_ref,
    seg_ref,
    keys_ref,
    *rest,
    n,
    chunk,
    subs,
    score_scale,
):
    piece_refs, (out_ref, proj_ref, weight_ref, normed_ref, sems) = rest[:n], rest[n:]

    @pl.when(pl.program_id(0) == 0)
    def fetch():
        for copy in place_pieces(piece_refs, chunk, where_ref, 0, weight_ref, sems):
            copy.wait()

    normed_ref[0] = rms_scale(tokens_ref[0].astype(f32), gain_ref[...]).astype(bf16)
    half_wide = weight_ref.shape[2]
    for half in range(2):
        proj_ref[0, :, half * half_wide : (half + 1) * half_wide] = plain(
            normed_ref[0], weight_ref[half]
        )
    pairs = 2 * half_wide // (3 * LANES)
    same_one, same_two = same_rows(seg_ref)
    mask = block_masks(seg_ref, keys_ref, subs)
    first_key = HALO - WINDOW
    for pair in range(pairs):
        mixed = []
        for kind in range(3):
            at = (kind * pairs + pair) * LANES
            conv, sig = gate_of(
                proj_ref[0, :, at : at + LANES], taps_ref[:, at : at + LANES], same_one, same_two
            )
            mixed.append((conv * sig).astype(bf16))
        queries = [by_head(q) for q in cut(mixed[0], subs, HALO, WINDOW)]
        keysets = cut(mixed[1], subs, first_key, 2 * WINDOW)
        valuesets = cut(mixed[2], subs, first_key, 2 * WINDOW)
        weights = parts_of(pair_probs(queries, keysets, mask, score_scale).astype(bf16), subs)
        for sub in range(subs):
            out_ref[0, sub * WINDOW : (sub + 1) * WINDOW, pair * LANES : (pair + 1) * LANES] = (
                join_heads(plain(weights[sub], valuesets[sub])).astype(bf16)
            )


def attend_back_kernel(
    branch_ref, out_weight_ref, proj_ref, taps_ref, seg_ref, keys_ref, out_ref, tap_ref, *, subs, score_scale
):
    @pl.when(pl.program_id(0) == 0)
    def clear():
        tap_ref[...] = jnp.zeros_like(tap_ref)

    grad_attended = contract_last(branch_ref[0], out_weight_ref[...]).astype(bf16)
    pairs = proj_ref.shape[2] // (3 * LANES)
    same_one, same_two = same_rows(seg_ref)
    mask = block_masks(seg_ref, keys_ref, subs)
    first_key = HALO - WINDOW
    for pair in range(pairs):
        values, convs, sigs, mixed = [], [], [], []
        for kind in range(3):
            at = (kind * pairs + pair) * LANES
            value = proj_ref[0, :, at : at + LANES]
            conv, sig = gate_of(value, taps_ref[:, at : at + LANES], same_one, same_two)
            values.append(value)
            convs.append(conv)
            sigs.append(sig)
            mixed.append((conv * sig).astype(bf16))
        queries = [by_head(q) for q in cut(mixed[0], subs, HALO, WINDOW)]
        keysets = cut(mixed[1], subs, first_key, 2 * WINDOW)
        valuesets = cut(mixed[2], subs, first_key, 2 * WINDOW)
        grads = [
            by_head(g)
            for g in cut(grad_attended[:, pair * LANES : (pair + 1) * LANES], subs, 0, WINDOW)
        ]
        probs = pair_probs(queries, keysets, mask, score_scale)
        grad_probs = jnp.concatenate([contract_last(g, v) for g, v in zip(grads, valuesets)], 0)
        inner = jnp.sum(probs * grad_probs, axis=-1, keepdims=True)
        grad_scores = parts_of((probs * (grad_probs - inner)).astype(bf16), subs)
        weights = parts_of(probs.astype(bf16), subs)
        grad_queries = [
            join_heads(plain(g, k)) * score_scale for g, k in zip(grad_scores, keysets)
        ]
        grad_keys = [contract_first(g, q) * score_scale for g, q in zip(grad_scores, queries)]
        grad_values = [contract_first(w, g) for w, g in zip(weights, grads)]

        def overlapped(parts):
            rows = [jnp.zeros((first_key, LANES), f32), parts[0][:WINDOW]]
            for sub in range(1, subs):
                rows.append(parts[sub - 1][WINDOW:] + parts[sub][:WINDOW])
            rows.append(parts[subs - 1][WINDOW:])
            return jnp.concatenate(rows, 0)

        grads_mixed = (
            jnp.concatenate([jnp.zeros((HALO, LANES), f32)] + grad_queries, 0),
            overlapped(grad_keys),
            overlapped(grad_values),
        )
        for kind in range(3):
            at = (kind * pairs + pair) * LANES
            taps = taps_ref[:, at : at + LANES]
            through = grads_mixed[kind] * sigs[kind]
            one = same_one * through
            two = same_two * through
            summed = (
                through * convs[kind] * (1.0 - sigs[kind])
                + taps[0:1] * through
                + taps[1:2] * shifted_up(one, 1)
                + taps[2:3] * shifted_up(two, 2)
            )
            out_ref[0, :, at : at + LANES] = summed.astype(bf16)
            value = values[kind]
            tap_ref[0:1, at : at + LANES] += jnp.sum(through * value, 0, keepdims=True)
            tap_ref[1:2, at : at + LANES] += jnp.sum(
                one * shifted_down(value, 1), 0, keepdims=True
            )
            tap_ref[2:3, at : at + LANES] += jnp.sum(
                two * shifted_down(value, 2), 0, keepdims=True
            )


def attention_specs(rows, columns, subs):
    return [
        pl.BlockSpec((3, columns), lambda b: (0, 0)),
        pl.BlockSpec((1, rows, LANES), lambda b: (b, 0, 0)),
        pl.BlockSpec((1, subs, 2 * WINDOW), lambda b: (b, 0, 0)),
    ]


def attend(where, tokens, gain, taps, seg_rows, seg_keys, pieces, chunk, score_scale):
    blocks, rows, width = tokens.shape
    columns = taps.shape[1]
    subs = seg_keys.shape[1]
    copies = sum(p.shape[0] // chunk for p in pieces)
    return pl.pallas_call(
        functools.partial(
            attend_kernel, n=len(pieces), chunk=chunk, subs=subs, score_scale=score_scale
        ),
        grid=(blocks,),
        out_shape=(
            jax.ShapeDtypeStruct((blocks, rows - HALO, columns // 3), bf16),
            jax.ShapeDtypeStruct((blocks, rows, columns), f32),
            jax.ShapeDtypeStruct((2, width, columns // 2), bf16),
            jax.ShapeDtypeStruct((blocks, rows, width), bf16),
        ),
        in_specs=[
            pl.BlockSpec(memory_space=pltpu.SMEM),
            pl.BlockSpec((1, rows, width), lambda b: (b, 0, 0)),
            pl.BlockSpec((1, width), lambda b: (0, 0)),
        ]
        + attention_specs(rows, columns, subs)
        + [pl.BlockSpec(memory_space=pl.ANY)] * len(pieces),
        out_specs=(
            pl.BlockSpec((1, rows - HALO, columns // 3), lambda b: (b, 0, 0)),
            pl.BlockSpec((1, rows, columns), lambda b: (b, 0, 0)),
            pl.BlockSpec((2, width, columns // 2), lambda b: (0, 0, 0)),
            pl.BlockSpec((1, rows, width), lambda b: (b, 0, 0)),
        ),
        scratch_shapes=[pltpu.SemaphoreType.DMA((copies,))],
        compiler_params=pltpu.CompilerParams(vmem_limit_bytes=60 * MIB),
        cost_estimate=pl.CostEstimate(
            flops=20 * 10**9, bytes_accessed=20 * 10**6, transcendentals=0
        ),
        name="attend",
    )(where, tokens, gain, taps, seg_rows, seg_keys, *pieces)


def attend_back(branch, out_weight, projected, taps, seg_rows, seg_keys, score_scale):
    blocks, rows, columns = projected.shape
    width = branch.shape[2]
    subs = seg_keys.shape[1]
    return pl.pallas_call(
        functools.partial(attend_back_kernel, subs=subs, score_scale=score_scale),
        grid=(blocks,),
        out_shape=(
            jax.ShapeDtypeStruct((blocks, rows, columns), bf16),
            jax.ShapeDtypeStruct((8, columns), f32),
        ),
        in_specs=[
            pl.BlockSpec((1, rows - HALO, width), lambda b: (b, 0, 0)),
            pl.BlockSpec((columns // 3, width), lambda b: (0, 0)),
            pl.BlockSpec((1, rows, columns), lambda b: (b, 0, 0)),
        ]
        + attention_specs(rows, columns, subs),
        out_specs=(
            pl.BlockSpec((1, rows, columns), lambda b: (b, 0, 0)),
            pl.BlockSpec((8, columns), lambda b: (0, 0)),
        ),
        compiler_params=pltpu.CompilerParams(vmem_limit_bytes=60 * MIB),
        cost_estimate=pl.CostEstimate(
            flops=20 * 10**9, bytes_accessed=20 * 10**6, transcendentals=0
        ),
        name="attend_back",
    )(branch, out_weight, projected, taps, seg_rows, seg_keys)


def dense_kernel(where_ref, dense_ref, gate_hbm, hidden_ref, inner_ref, gate_ref, sems, *, chunk):
    rows, hidden_wide = hidden_ref.shape
    count = gate_hbm.shape[0] // chunk
    ready = []
    for part, columns in enumerate((slice(0, TILE), slice(TILE, hidden_wide))):
        copies = []
        for index in range(count):
            spot = pl.multiple_of(where_ref[index, 1], 16)
            copy = pltpu.make_async_copy(
                gate_hbm.at[index * chunk : (index + 1) * chunk, columns],
                gate_ref.at[where_ref[index, 0], pl.ds(spot, chunk), columns],
                sems.at[part * count + index],
            )
            copy.start()
            copies.append(copy)
        ready.append(copies)

    def units(begin, end):
        @pl.loop(0, rows // TILE)
        def block(index):
            own = pl.ds(pl.multiple_of(index * TILE, TILE), TILE)
            normed = dense_ref[own, :]
            for first in range(begin, end, TILE):
                unit = slice(first, first + TILE)
                gate = plain(normed, gate_ref[0, :, unit])
                up = plain(normed, gate_ref[1, :, unit])
                sig = jax.nn.sigmoid(gate)
                silu = gate * sig
                hidden_ref[own, unit] = (silu * up).astype(bf16)
                inner_ref[0, own, unit] = up * (sig * (1.0 + gate * (1.0 - sig)))
                inner_ref[1, own, unit] = silu

    for copy in ready[0]:
        copy.wait()
    units(0, TILE)
    for copy in ready[1]:
        copy.wait()
    units(TILE, hidden_wide)


def fetch_down(down_hbm, down_ref, sem):
    real = down_hbm.shape[0]
    copy = pltpu.make_async_copy(down_hbm, down_ref.at[:real], sem)
    copy.start()
    if real < down_ref.shape[0]:
        down_ref[real:] = jnp.zeros((down_ref.shape[0] - real, down_ref.shape[1]), bf16)
    return copy


def dense_back_kernel(
    where_ref,
    cotangent_ref,
    inner_hbm,
    gate_hbm,
    down_hbm,
    grad_ref,
    joined_ref,
    down_ref,
    inner_ref,
    gate_ref,
    sems,
    *,
    chunk,
):
    rows, width = cotangent_ref.shape
    hidden_wide = joined_ref.shape[2]
    count = gate_hbm.shape[0] // chunk
    down_copy = fetch_down(down_hbm, down_ref, sems.at[count])
    inner_copies = []
    for index in range(rows // TILE):
        own = slice(index * TILE, (index + 1) * TILE)
        copy = pltpu.make_async_copy(
            inner_hbm.at[:, own], inner_ref.at[:, own], sems.at[count + 1 + index]
        )
        copy.start()
        inner_copies.append(copy)
    gate_copies = place_pieces([gate_hbm], chunk, where_ref, 0, gate_ref, sems)
    down_copy.wait()
    for index in range(rows // TILE):
        inner_copies[index].wait()
        own = slice(index * TILE, (index + 1) * TILE)
        cotangent = cotangent_ref[own, :]
        for first in range(0, hidden_wide, TILE):
            unit = slice(first, first + TILE)
            grad = contract_last(cotangent, down_ref[unit])
            joined_ref[0, own, unit] = (grad * inner_ref[0, own, unit]).astype(bf16)
            joined_ref[1, own, unit] = (grad * inner_ref[1, own, unit]).astype(bf16)
    for copy in gate_copies:
        copy.wait()

    @pl.loop(0, rows // TILE)
    def block(index):
        own = pl.ds(pl.multiple_of(index * TILE, TILE), TILE)
        gates = joined_ref[0, own, :]
        ups = joined_ref[1, own, :]
        for first in range(0, width, TILE):
            unit = slice(first, first + TILE)
            grad_ref[own, unit] = (
                contract_last(gates, gate_ref[0, unit]) + contract_last(ups, gate_ref[1, unit])
            ).astype(bf16)


def dense_out_kernel(hidden_ref, down_hbm, out_ref, down_ref, sem):
    fetch_down(down_hbm, down_ref, sem).wait()

    @pl.loop(0, hidden_ref.shape[0] // TILE)
    def block(index):
        own = pl.ds(pl.multiple_of(index * TILE, TILE), TILE)
        out_ref[own, :] = plain(hidden_ref[own, :], down_ref[...]).astype(bf16)


def down_grad_kernel(hidden_ref, cotangent_ref, out_ref):
    out_ref[...] = contract_first(hidden_ref[...], cotangent_ref[...]).astype(bf16)[
        : out_ref.shape[0]
    ]


WHOLE = pl.BlockSpec(memory_space=pltpu.VMEM)
OUTSIDE = pl.BlockSpec(memory_space=pl.ANY)
SCALARS = pl.BlockSpec(memory_space=pltpu.SMEM)


def kernel_params(giga_flops):
    return dict(
        compiler_params=pltpu.CompilerParams(vmem_limit_bytes=60 * MIB),
        cost_estimate=pl.CostEstimate(
            flops=giga_flops * 10**9, bytes_accessed=20 * 10**6, transcendentals=0
        ),
    )


def dense(where, normed, gate, chunk):
    rows, width = normed.shape
    hidden_wide = gate.shape[1]
    return pl.pallas_call(
        functools.partial(dense_kernel, chunk=chunk),
        out_shape=(
            jax.ShapeDtypeStruct((rows, hidden_wide), bf16),
            jax.ShapeDtypeStruct((2, rows, hidden_wide), f32),
        ),
        in_specs=[SCALARS, WHOLE, OUTSIDE],
        out_specs=(WHOLE, WHOLE),
        scratch_shapes=[
            pltpu.VMEM((2, width, hidden_wide), bf16),
            pltpu.SemaphoreType.DMA((2 * (gate.shape[0] // chunk),)),
        ],
        name="dense",
        **kernel_params(15),
    )(where, normed, gate)


def dense_back(where, cotangent, inner, gate, chunk, down):
    rows, width = cotangent.shape
    hidden_wide = gate.shape[1]
    copies = 1 + rows // TILE + gate.shape[0] // chunk
    return pl.pallas_call(
        functools.partial(dense_back_kernel, chunk=chunk),
        out_shape=(
            jax.ShapeDtypeStruct((rows, width), bf16),
            jax.ShapeDtypeStruct((2, rows, hidden_wide), bf16),
        ),
        in_specs=[SCALARS, WHOLE, OUTSIDE, OUTSIDE, OUTSIDE],
        out_specs=(WHOLE, WHOLE),
        scratch_shapes=[
            pltpu.VMEM((hidden_wide, width), bf16),
            pltpu.VMEM((2, rows, hidden_wide), f32),
            pltpu.VMEM((2, width, hidden_wide), bf16),
            pltpu.SemaphoreType.DMA((copies,)),
        ],
        name="dense_back",
        **kernel_params(20),
    )(where, cotangent, inner, gate, down)


def dense_out(hidden, down):
    rows, hidden_wide = hidden.shape
    width = down.shape[1]
    return pl.pallas_call(
        dense_out_kernel,
        out_shape=jax.ShapeDtypeStruct((rows, width), bf16),
        in_specs=[WHOLE, OUTSIDE],
        out_specs=WHOLE,
        scratch_shapes=[pltpu.VMEM((hidden_wide, width), bf16), pltpu.SemaphoreType.DMA],
        name="dense_out",
        **kernel_params(8),
    )(hidden, down)


def down_gradient(hidden, cotangent, units):
    rows, hidden_wide = hidden.shape
    width = cotangent.shape[1]
    return pl.pallas_call(
        down_grad_kernel,
        grid=(2,),
        out_shape=jax.ShapeDtypeStruct((units, width), bf16),
        in_specs=[
            pl.BlockSpec((rows, hidden_wide), lambda h: (0, 0)),
            pl.BlockSpec((rows, width // 2), lambda h: (0, h)),
        ],
        out_specs=pl.BlockSpec((units, width // 2), lambda h: (0, h)),
        name="down_grad",
        **kernel_params(8),
    )(hidden, cotangent)


def normed_grad_kernel(grad_ref, weight_ref, out_ref, halo_ref):
    half_wide = weight_ref.shape[2]
    grads = grad_ref[0]
    product = (
        contract_last(grads[:, :half_wide], weight_ref[0])
        + contract_last(grads[:, half_wide:], weight_ref[1])
    ).astype(bf16)
    halo_ref[0] = product[:HALO]
    out_ref[0] = product[HALO:]


def normed_grad(grad_projected, weight):
    blocks, rows, columns = grad_projected.shape
    width = weight.shape[1]
    return pl.pallas_call(
        normed_grad_kernel,
        grid=(blocks,),
        out_shape=(
            jax.ShapeDtypeStruct((blocks, rows - HALO, width), bf16),
            jax.ShapeDtypeStruct((blocks, HALO, width), bf16),
        ),
        in_specs=[
            pl.BlockSpec((1, rows, columns), lambda b: (b, 0, 0)),
            pl.BlockSpec((2, width, columns // 2), lambda b: (0, 0, 0)),
        ],
        out_specs=(
            pl.BlockSpec((1, rows - HALO, width), lambda b: (b, 0, 0)),
            pl.BlockSpec((1, HALO, width), lambda b: (b, 0, 0)),
        ),
        name="normed_grad",
        **kernel_params(15),
    )(grad_projected, weight)


def weight_grad_kernel(left_ref, right_ref, out_ref):
    right = right_ref[...].reshape(right_ref.shape[-2:])
    product = contract_first(left_ref[...], right).astype(bf16)
    planes, unused, rows, columns = out_ref.shape
    out_ref[:, 0] = product[: planes * rows].reshape(planes, rows, columns)


def weight_grad(left, right, planes, rows, name):
    tokens, depth = left.shape
    columns = right.shape[-1] if right.ndim == 3 else right.shape[-1] // 2
    steps = 2 if planes * rows == depth else 1
    if right.ndim == 3:
        right_spec = pl.BlockSpec((1, tokens, columns), lambda h, k: (h, 0, 0))
    else:
        right_spec = pl.BlockSpec((tokens, columns), lambda h, k: (0, h))
    return pl.pallas_call(
        weight_grad_kernel,
        grid=(2, steps),
        out_shape=jax.ShapeDtypeStruct((planes, 2, rows, columns), bf16),
        in_specs=[pl.BlockSpec((tokens, depth // steps), lambda h, k: (0, k)), right_spec],
        out_specs=pl.BlockSpec((planes // steps, 1, rows, columns), lambda h, k: (k, h, 0, 0)),
        compiler_params=pltpu.CompilerParams(vmem_limit_bytes=60 * MIB),
        cost_estimate=pl.CostEstimate(
            flops=20 * 10**9, bytes_accessed=20 * 10**6, transcendentals=0
        ),
        name=name,
    )(left, right)


def fence(*values):
    return lax.optimization_barrier(values)


def layer(
    planes,
    tokens,
    segments,
    cotangent,
    mixer_gain,
    qkv_weight,
    conv_taps,
    out_weight,
    dense_gain,
    gateup_weight,
    down_weight,
):
    count = planes * PLANE
    rows, width = tokens.shape
    ext = HALO + rows
    subs = rows // WINDOW
    quarter = width // 4
    padded = -(-quarter // LANES) * LANES
    half_wide = 3 * padded // 2
    half_width = width // 2
    shard_rows = qkv_weight.shape[0]
    down_rows = down_weight.shape[0]
    square_rows = 4 * shard_rows
    octet_rows = PLANE * shard_rows
    hidden_width = down_rows * count
    hidden_part = hidden_width // 4
    hidden_wide = -(-hidden_part // 256) * 256
    tap_columns = conv_taps.shape[1]
    out_planes = planes // 4
    z = lax.axis_index("z")
    y = lax.axis_index("y")
    x = lax.axis_index("x")
    c = lax.axis_index("core")
    part = 2 * y + x
    score_scale = 1.0 / math.sqrt(HDIM)

    def swap(array, axes):
        return lax.all_to_all(array, axes, 0, 0)

    def flip(array, axis):
        return lax.ppermute(array, axis, [(0, 1), (1, 0)])

    def in_order(own, other, bit):
        return jnp.where(bit == 0, own, other), jnp.where(bit == 0, other, own)

    def absolute(pieces):
        whole = jnp.zeros((planes,) + pieces[0].shape, pieces[0].dtype)
        for step, piece in enumerate(pieces):
            first = ((z + step) % planes,) + (0,) * piece.ndim
            whole = lax.dynamic_update_slice(whole, piece[None], first)
        return whole

    def gather_rows(array, axes):
        return swap(jnp.broadcast_to(array, (4,) + array.shape), axes)

    def rows_at(bits, size):
        return jnp.stack([jnp.asarray(b, jnp.int32) for b in bits]).reshape(-1, size)

    qkv_slices = qkv_weight.reshape(shard_rows, 3, 4, quarter)
    qkv_slices = jnp.pad(qkv_slices, ((0, 0), (0, 0), (0, 0), (0, padded - quarter)))
    qkv_slices = qkv_slices.transpose(2, 0, 1, 3).reshape(4, shard_rows, 2, half_wide)
    qkv_slices = qkv_slices.transpose(0, 2, 1, 3).reshape(PLANE, shard_rows, half_wide)
    owned = jnp.concatenate([mixer_gain, dense_gain, conv_taps.reshape(-1)])
    owned_size = owned.shape[0]
    owned = jnp.pad(owned.reshape(1, -1), ((0, 1), (0, half_wide - owned_size)))
    owned = jnp.broadcast_to(owned, (PLANE, 2, half_wide))
    qkv_slices, gateup_weight, down_weight, out_weight = fence(
        jnp.concatenate([qkv_slices, owned], 1), gateup_weight, down_weight, out_weight
    )

    lines = []
    for d in range(count):
        lines.append(2 * planes * (d % PLANE // 2) + 2 * (d // PLANE) + d % 2)
    out_piece = lax.ppermute(out_weight, ALL, [(lines[d], d) for d in range(count)])
    before = lax.ppermute(tokens[rows - HALO :], ALL, [(d, d + 1) for d in range(count - 1)])

    qkv_piece = swap(qkv_slices, OCTET)
    gateup_slices = gateup_weight.reshape(shard_rows, 2, planes, 4, hidden_part // planes)
    gateup_slices = gateup_slices.transpose(3, 1, 0, 2, 4)
    gateup_slices = gateup_slices.reshape(PLANE, shard_rows, hidden_part)
    gateup_slices = jnp.pad(gateup_slices, ((0, 0), (0, 0), (0, hidden_wide - hidden_part)))
    qkv_piece, gateup_slices, tokens_now, before = fence(
        qkv_piece, gateup_slices, tokens, before
    )
    out_all = lax.all_gather(out_piece, LINE)
    small = [qkv_piece[:, shard_rows, :owned_size]]
    qkv_piece, small[0] = fence(qkv_piece[:, :shard_rows].reshape(octet_rows, half_wide), small[0])

    qkv_pieces, qkv_others = [qkv_piece], []
    onward = [(i, (i - 1) % planes) for i in range(planes)]
    for step in range(1, planes):
        qkv_next = lax.ppermute(qkv_pieces[-1], "z", onward)
        if step == 1:
            gateup_piece = swap(gateup_slices, OCTET).reshape(octet_rows, hidden_wide)
            for by in range(1, planes):
                shift = [(i, (i - by) % planes) for i in range(planes)]
                small.append(lax.ppermute(small[0], "z", shift))
            qkv_next, gateup_piece, tokens_now, small = fence(
                qkv_next, gateup_piece, tokens_now, small
            )
            token_group = gather_rows(jnp.concatenate([before, tokens_now]), SQUARE)
        elif step < planes - 1:
            cotangent_now = jnp.broadcast_to(cotangent, (4,) + cotangent.shape)
            qkv_next, cotangent_now = fence(qkv_next, cotangent_now)
        else:
            small = absolute(small).astype(f32)
            gain_one = small[:, :, :shard_rows].reshape(1, width)
            gain_two = small[:, :, shard_rows : 2 * shard_rows].reshape(width)
            taps = small[:, :, 2 * shard_rows :].reshape(count, 3, tap_columns).transpose(1, 0, 2)
            taps = taps.reshape(3, 3, 4, quarter)
            taps = lax.dynamic_index_in_dim(taps, part, 2, keepdims=False)
            taps = jnp.pad(taps, ((0, 0), (0, 0), (0, padded - quarter)))
            taps = taps.reshape(3, 3 * padded)
            out = fence(qkv_next, cotangent_now, token_group, gateup_piece, gain_one, gain_two, taps)
            qkv_next, cotangent_now, token_group, gateup_piece, gain_one, gain_two, taps = out
        qkv_others.append(flip(qkv_pieces[-1], "core"))
        qkv_pieces.append(qkv_next)
    qkv_pieces, qkv_others, down_piece, cotangent_now = fence(
        qkv_pieces, qkv_others, down_weight, cotangent_now
    )
    gateup_all = lax.all_gather(gateup_piece, LINE)
    down_all = lax.all_gather(down_piece, LINE).reshape(hidden_part, width)
    qkv_others.append(flip(qkv_pieces[-1], "core"))
    (qkv_others,) = fence(qkv_others)
    out_full = jnp.pad(out_all.reshape(quarter, width), ((0, padded - quarter), (0, 0)))

    padded_segments = jnp.concatenate([jnp.full((HALO,), -1, jnp.int32), segments])
    seg_rows = jnp.stack(
        [
            lax.dynamic_slice_in_dim(padded_segments, (PLANE * z + 2 * b + c) * rows, ext)
            for b in range(4)
        ]
    )
    seg_keys = jnp.stack(
        [
            seg_rows[:, HALO - WINDOW + s * WINDOW : HALO + WINDOW + s * WINDOW]
            for s in range(subs)
        ],
        1,
    )
    seg_rows = jnp.broadcast_to(seg_rows[:, :, None], (4, ext, LANES))

    cotangent_group = swap(cotangent_now, SQUARE).reshape(4 * rows, width)
    where_qkv = []
    for own in range(2):
        for step in range(planes):
            where_qkv += [c ^ own, (z + step) % planes * octet_rows]
    attended, projected, qkv_full, normed_group = attend(
        rows_at(where_qkv, 2),
        token_group,
        gain_one,
        taps,
        seg_rows,
        seg_keys,
        qkv_pieces + qkv_others,
        octet_rows,
        score_scale,
    )
    attended = attended.reshape(4 * rows, padded)
    attended, normed_group, cotangent_group = fence(attended, normed_group, cotangent_group)
    mixer_out = plain(attended, out_full).astype(bf16).reshape(4, rows, width)

    mixer_sum = swap(mixer_out, SQUARE)
    own_tokens = tokens.astype(f32)
    residual = own_tokens + jnp.sum(mixer_sum.astype(f32), 0)
    normed_dense = rms_scale(residual, gain_two).astype(bf16)
    dense_group = gather_rows(normed_dense, SQUARE).reshape(4 * rows, width)

    gateup_chunk = octet_rows
    where_gateup = [k for i in range(planes) for h in range(2) for k in (h, i * gateup_chunk)]
    gateup_all = gateup_all.reshape(-1, hidden_wide)
    where_gateup = rows_at(where_gateup, 2)
    hidden, inner = dense(where_gateup, dense_group, gateup_all, gateup_chunk)
    hidden, inner, cotangent_group = fence(hidden, inner, cotangent_group)
    down_grad = down_gradient(hidden, cotangent_group, hidden_part)
    inner, cotangent_group, down_grad, hidden = fence(inner, cotangent_group, down_grad, hidden)
    down_mine = lax.psum_scatter(
        down_grad.reshape(2 * planes, down_rows, width), LINE, scatter_dimension=0
    )
    grad_dense, grad_inner = fence(
        *dense_back(where_gateup, cotangent_group, inner, gateup_all, gateup_chunk, down_all)
    )

    def scatter_line(array):
        return lax.psum_scatter(
            array.reshape((2 * planes,) + array.shape[2:]), LINE, scatter_dimension=0
        )

    grad_dense = swap(grad_dense.reshape(4, rows, width), SQUARE)
    gateup_grad = weight_grad(dense_group, grad_inner, planes, octet_rows, "gateup_grad")
    grad_dense, gateup_grad, hidden, down_all = fence(grad_dense, gateup_grad, hidden, down_all)
    gateup_mine = scatter_line(gateup_grad)

    unused, rms_back = jax.vjp(rms_scale, residual, gain_two)
    grad_residual, dense_gain_sum = rms_back(jnp.sum(grad_dense.astype(f32), 0))
    grad_residual = grad_residual + cotangent.astype(f32)
    grad_branch = gather_rows(grad_residual.astype(bf16), SQUARE)
    dense_rows = dense_out(hidden, down_all).reshape(4, rows, width)
    grad_branch, out_full, dense_rows, down_mine = fence(
        grad_branch, out_full, dense_rows, down_mine
    )
    dense_sum = swap(dense_rows, SQUARE)

    grad_projected, grad_taps = attend_back(
        grad_branch, out_full, projected, taps, seg_rows, seg_keys, score_scale
    )
    grad_normed, grad_halo = normed_grad(grad_projected, qkv_full)
    grad_projected, grad_normed, grad_halo, dense_sum = fence(
        grad_projected, grad_normed, grad_halo, dense_sum
    )

    halo_sum = swap(grad_halo, SQUARE)
    grad_projected = grad_projected.reshape(4 * ext, 3 * padded)
    normed_rows = normed_group.reshape(4 * ext, width)
    qkv_grad = weight_grad(normed_rows, grad_projected, planes, octet_rows, "qkv_grad")
    grad_branch = grad_branch.reshape(4 * rows, width)
    out = fence(qkv_grad, grad_normed, halo_sum, attended, grad_branch, gateup_mine)
    qkv_grad, grad_normed, halo_sum, attended, grad_branch, gateup_mine = out
    qkv_part = scatter_line(qkv_grad)

    normed_sum = swap(grad_normed, SQUARE)
    late = jnp.sum(halo_sum.astype(f32), 0).astype(bf16)
    late = lax.ppermute(late, ALL, [(d, d - 1) for d in range(1, count)])
    out_grad = contract_first(attended, grad_branch)[:quarter].astype(bf16)
    layer_out = (residual + jnp.sum(dense_sum.astype(f32), 0)).astype(bf16)
    normed_sum, late, gateup_mine, layer_out, out_grad = fence(
        normed_sum, late, gateup_mine, layer_out, out_grad
    )

    gateup_mine = swap(gateup_mine.reshape(PLANE, shard_rows, hidden_wide), OCTET)
    grad_normed = jnp.sum(normed_sum.astype(f32), 0)
    grad_normed = grad_normed + jnp.pad(late.astype(f32), ((rows - HALO, 0), (0, 0)))
    unused, mixer_back = jax.vjp(rms_scale, own_tokens, gain_one.reshape(width))
    grad_rows, mixer_gain_sum = mixer_back(grad_normed)
    input_grad = grad_residual + grad_rows

    grad_taps = grad_taps[:3].reshape(3, 3, 1, padded)[..., :quarter]
    grad_taps = lax.dynamic_update_slice(
        jnp.zeros((3, 3, 4, quarter), f32), grad_taps, (0, 0, part, 0)
    )
    grad_taps = grad_taps.reshape(3, count, tap_columns).transpose(1, 0, 2)
    sums = jnp.concatenate(
        [
            mixer_gain_sum.reshape(count, shard_rows),
            dense_gain_sum.reshape(count, shard_rows),
            grad_taps.reshape(count, 3 * tap_columns),
        ],
        1,
    )
    sums = sums.reshape(planes, PLANE, owned_size).transpose(1, 0, 2).astype(bf16)
    gateup_mine, sums, input_grad = fence(gateup_mine, sums, input_grad)

    sums, qkv_part, out_grad = fence(swap(sums, OCTET), qkv_part, out_grad)
    out_mine = lax.psum_scatter(
        out_grad.reshape(2 * planes, shard_rows, width), LINE, scatter_dimension=0
    )
    qkv_mine = swap(qkv_part.reshape(PLANE, shard_rows, half_wide), OCTET)
    sums = jnp.sum(sums.astype(f32), 0)
    parts = []
    for by in range(1, planes):
        sent = lax.dynamic_index_in_dim(sums, (z + by) % planes, 0, keepdims=False).astype(bf16)
        parts.append(lax.ppermute(sent, "z", [(i, (i + by) % planes) for i in range(planes)]))
    sums = lax.dynamic_index_in_dim(sums, z, 0, keepdims=False)
    for arrived in parts:
        sums = sums + arrived.astype(f32)
    gateup_mine = gateup_mine[:, :, :hidden_part]
    gateup_mine = gateup_mine.reshape(4, 2, shard_rows, planes, hidden_part // planes)
    gateup_mine = gateup_mine.transpose(2, 1, 3, 0, 4).reshape(shard_rows, 2 * hidden_width)
    gateup_mine = gateup_mine.astype(f32)
    qkv_mine, sums, gateup_mine = fence(qkv_mine, sums, gateup_mine)
    qkv_mine = qkv_mine.reshape(4, 2, shard_rows, half_wide).transpose(2, 0, 1, 3)
    qkv_mine = qkv_mine.reshape(shard_rows, 4, 3, padded)[..., :quarter].transpose(0, 2, 1, 3)
    qkv_mine = qkv_mine.reshape(shard_rows, 3 * width).astype(f32)
    out_mine = lax.ppermute(out_mine, ALL, [(d, lines[d]) for d in range(count)])
    return (
        layer_out,
        input_grad,
        sums[:shard_rows],
        qkv_mine,
        sums[2 * shard_rows :].reshape(3, tap_columns),
        out_mine.astype(f32),
        sums[shard_rows : 2 * shard_rows],
        gateup_mine,
        down_mine.astype(f32),
    )


def solution(mesh):
    planes = mesh.devices.size // PLANE
    split = Mesh(mesh.devices.reshape(planes, 2, 2, 2), ALL)
    over_rows = P(ALL, None)
    over_columns = P(None, ALL)
    return jax.shard_map(
        functools.partial(layer, planes),
        mesh=split,
        in_specs=(
            over_rows,
            P(),
            over_rows,
            P(ALL),
            over_rows,
            over_columns,
            over_rows,
            P(ALL),
            over_rows,
            over_rows,
        ),
        out_specs=(
            over_rows,
            over_rows,
            P(ALL),
            over_rows,
            over_columns,
            over_rows,
            P(ALL),
            over_rows,
            over_rows,
        ),
        check_vma=False,
    )
```
